128 devices in a mesh: image: 8 (over x, z_lo), domain: 16 (over y, z_hi, core).
Axes of the slice: x: 4, y: 4, z: 4 (z_hi: 2, z_lo: 2; z = z_hi * 2 + z_lo), core: 2. Of those that a mesh axis runs over, the one named last changes fastest.
Arguments:
- displacement: float32 [8, 3, 1572864], P('image', None, 'domain'), may hold values from -0.5 to 0.5, as said below
- velocity: float32 [8, 3, 1572864], P('image', None, 'domain'), may hold values from -1.2 to 1.2
Outputs:
- displacement_next: float32 [8, 3, 1572864], P('image', None, 'domain')
- velocity_next: float32 [8, 3, 1572864], P('image', None, 'domain')
The draws below stay inside these ranges and needn't reach their ends.
Inputs may be any that keep to these rules, and one draw needn't show every extreme that they name: `displacement`: displacements from the lattice sites.
All inputs are finite; a program needn't handle non-finite values.
Results may differ from the reference program's by a relative error of at most 0.0003.
Values sent between devices are 32-bit elements; how exact they have to be, the bound alone decides.
No kernel may reach another device: no remote copies, remote signals or barrier semaphores. Data moves between devices by JAX's collectives and lax.ppermute only.
A program may use at most 128 MiB of HBM per device.

```python
import math
import jax
import jax.numpy as jnp
from jax import lax

SIDE = 32
FIRE_STEPS = 2
IMAGES = 8
ATOMS = 1572864


def draw_displacement(key, part):
    key = jax.random.fold_in(key, 7)
    scale_key = jax.random.fold_in(key, 1)
    noise_key = jax.random.fold_in(key, 2)
    plane_size = SIDE * SIDE
    atom_ids = jnp.arange(ATOMS)
    plane = atom_ids // plane_size
    site_ids = atom_ids % plane_size
    col_u = site_ids // SIDE
    col_v = site_ids % SIDE
    lateral_y = (col_u + col_v + plane % 2).astype(jnp.float32) * 1.8075
    center = (SIDE - 0.5) * 1.8075
    planes = ATOMS // plane_size
    progress = jnp.arange(IMAGES).astype(jnp.float32) / (IMAGES - 1)
    profile = jnp.tanh((lateral_y - center) / 2.0) * (0.5 + 0.5 * jnp.cos(2.0 * math.pi * plane.astype(jnp.float32) / planes))
    slip = 0.25 * progress[:, None] * profile[None, :]
    image_scale = 0.02 * jnp.exp(math.log(3.0) * jax.random.uniform(scale_key, (IMAGES, 1, 1)))
    noise = jnp.clip(jax.random.normal(noise_key, (IMAGES, 3, ATOMS)), -3.0, 3.0)
    shear = jnp.stack([slip, jnp.zeros_like(slip), jnp.zeros_like(slip)], axis=1)
    return (noise * image_scale + shear).astype(jnp.float32)


def steps_of(stream_key, shape, split, smallest, top_value):
    def one(axis_at, blocks):
        heights = jax.random.uniform(jax.random.fold_in(jax.random.fold_in(stream_key, 6), axis_at), (blocks,), jnp.float32, smallest / len(split), top_value / len(split))
        return jnp.repeat(jnp.exp(heights), shape[axis_at] // blocks).reshape((-1,) + (1,) * (len(shape) - axis_at - 1))

    factor_of = one(*split[0])
    for cut in split[1:]:
        factor_of = factor_of * one(*cut)
    return factor_of


def centred(key, extent, scale, bound, shards=(), held_as=jnp.bfloat16):
    loudness = steps_of(key, extent, shards, -0.22, 0.18) if shards else 1.0
    values = jax.random.normal(key, extent, jnp.float32) * scale * loudness
    return jnp.minimum(jnp.maximum(values, -bound), bound).astype(held_as)


def setup_inputs(seed: int = 0) -> dict:
    key_list = jax.random.split(jax.random.key(seed), 3)
    displacement = draw_displacement(jax.random.fold_in(key_list[2], 71), 0)
    velocity = centred(key_list[1], (IMAGES, 3, ATOMS), 0.2, 1.2, ((0, 8), (2, 16)), jnp.float32)
    return dict(displacement=displacement, velocity=velocity)


lattice_const = 3.615
cutoff_sq = 9.61
nearest_sq = 6.533136
pair_scale = 30.0
pair_depth = 0.3
embed_scale = 1.2
bulk_root = 3.605551275463989
spring_const = 2.0
time_step = 0.1
fire_mixing = 0.1
stabilizer = 1e-06

def neighbour_table(parity):
    moves = [(0, 1, 0), (0, -1, 0), (0, 0, 1), (0, 0, -1)]
    sign = -1 if parity == 0 else 1
    for plane_step in (-1, 1):
        for step_u in (0, 1):
            for step_v in (0, 1):
                moves.append((plane_step, sign * step_u, sign * step_v))
    table = []
    for plane_step, step_u, step_v in moves:
        lift = 0 if plane_step == 0 else 1 if parity == 0 else -1
        table.append((plane_step, step_u, step_v, step_u + step_v + lift, step_u - step_v))
    return table

def lateral_valid(step_u, step_v, kind):
    site_ids = jnp.arange(SIDE * SIDE)
    col_u = site_ids // SIDE + step_u
    col_v = site_ids % SIDE + step_v
    return ((col_u >= 0) & (col_u < SIDE) & (col_v >= 0) & (col_v < SIDE)).astype(kind)

def lateral_shift(field, step_u, step_v):
    return jnp.roll(field, -(step_u * SIDE + step_v), axis=-1)

def slot_pair(own, before, after, entry):
    plane_step, step_u, step_v, lift_y, lift_z = entry
    kind = own.dtype
    source = (before, own, after)[plane_step + 1]
    other = lateral_shift(source, step_u, step_v)
    half_const = 0.5 * lattice_const
    offset = jnp.asarray([plane_step * half_const, lift_y * half_const, lift_z * half_const], kind)[:, None, None]
    separation = other - own + offset
    dist_sq = lax.optimization_barrier(jnp.sum(separation * separation, axis=0))
    valid = lateral_valid(step_u, step_v, kind)
    reach = valid * jnp.maximum(1.0 - dist_sq / cutoff_sq, 0.0)
    return (separation, dist_sq, reach)

def density_terms(own, before, after, parity):
    rho = jnp.zeros(own.shape[1:], own.dtype)
    pair_energy = jnp.zeros((), own.dtype)
    for entry in neighbour_table(parity):
        separation, dist_sq, reach = slot_pair(own, before, after, entry)
        cubic = reach * reach * reach
        ratio = dist_sq / nearest_sq
        rho = rho + pair_scale * cubic * (2.0 - ratio)
        pair_energy = pair_energy + 0.5 * pair_scale * pair_depth * jnp.sum(cubic * (2.5 - 2.0 * ratio))
    return (rho, pair_energy)

def force_terms(own, before, after, parity, own_slope, before_slope, after_slope):
    force = jnp.zeros_like(own)
    for entry in neighbour_table(parity):
        separation, dist_sq, reach = slot_pair(own, before, after, entry)
        square = reach * reach
        cubic = square * reach
        ratio = dist_sq / nearest_sq
        dens_slope = pair_scale * (-3.0 * square / cutoff_sq * (2.0 - ratio) - cubic / nearest_sq)
        pair_slope = pair_scale * pair_depth * (-3.0 * square / cutoff_sq * (2.5 - 2.0 * ratio) - 2.0 * cubic / nearest_sq)
        partner_slope = lateral_shift((before_slope, own_slope, after_slope)[entry[0] + 1], entry[1], entry[2])
        weight = pair_slope + (own_slope + partner_slope) * dens_slope
        force = force + 2.0 * weight[None] * separation
    return force

def take_planes(array, start, count, axis):
    return lax.slice_in_dim(array, start, start + 2 * count - 1, 2, axis)

def plane_densities(layered, count):
    half_count = count // 2
    even_rho, even_pair = density_terms(take_planes(layered, 1, half_count, 1), take_planes(layered, 0, half_count, 1), take_planes(layered, 2, half_count, 1), 0)
    odd_rho, odd_pair = density_terms(take_planes(layered, 2, half_count, 1), take_planes(layered, 1, half_count, 1), take_planes(layered, 3, half_count, 1), 1)
    rho = jnp.stack([even_rho, odd_rho], axis=1).reshape(count, SIDE * SIDE)
    return (rho, even_pair + odd_pair)

def plane_forces(layered, slope_ext, count):
    half_count = count // 2
    even_force = force_terms(take_planes(layered, 1, half_count, 1), take_planes(layered, 0, half_count, 1), take_planes(layered, 2, half_count, 1), 0, take_planes(slope_ext, 1, half_count, 0), take_planes(slope_ext, 0, half_count, 0), take_planes(slope_ext, 2, half_count, 0))
    odd_force = force_terms(take_planes(layered, 2, half_count, 1), take_planes(layered, 1, half_count, 1), take_planes(layered, 3, half_count, 1), 1, take_planes(slope_ext, 2, half_count, 0), take_planes(slope_ext, 1, half_count, 0), take_planes(slope_ext, 3, half_count, 0))
    return jnp.stack([even_force, odd_force], axis=2).reshape(3, count * SIDE * SIDE)

def embedding(rho):
    root = jnp.sqrt(1.0 + rho)
    return (-embed_scale * (root - bulk_root), -0.5 * embed_scale / root)

def image_forces(displaced):
    plane_count = displaced.shape[1] // (SIDE * SIDE)
    planes = displaced.reshape(3, plane_count, SIDE * SIDE)
    layered = jnp.concatenate([planes[:, -1:], planes, planes[:, :1]], axis=1)
    rho, pair_energy = plane_densities(layered, plane_count)
    energy_atoms, slope = embedding(rho)
    slope_ext = jnp.concatenate([slope[-1:], slope, slope[:1]], axis=0)
    forces = plane_forces(layered, slope_ext, plane_count)
    return (forces, jnp.sum(energy_atoms) + pair_energy)

def tangent_weights(e_prev, e_here, e_next):
    rise = e_next - e_here
    fall = e_here - e_prev
    larger = jnp.maximum(jnp.abs(rise), jnp.abs(fall))
    smaller = jnp.minimum(jnp.abs(rise), jnp.abs(fall))
    upward = (e_next > e_here) & (e_here > e_prev)
    downward = (e_next < e_here) & (e_here < e_prev)
    toward = e_next > e_prev
    weight_fwd = jnp.where(upward, 1.0, jnp.where(downward, 0.0, jnp.where(toward, larger, smaller)))
    weight_bwd = jnp.where(upward, 0.0, jnp.where(downward, 1.0, jnp.where(toward, smaller, larger)))
    return (weight_fwd, weight_bwd)

def reference(displacement, velocity):
    images = displacement.shape[0]
    order = jnp.arange(images)
    inner_flag = ((order > 0) & (order < images - 1)).astype(displacement.dtype)[:, None, None]
    for step_index in range(FIRE_STEPS):
        forces, energies = lax.map(image_forces, displacement)
        forward = displacement[2:] - displacement[1:-1]
        backward = displacement[1:-1] - displacement[:-2]
        weight_fwd, weight_bwd = tangent_weights(energies[:-2], energies[1:-1], energies[2:])
        tangent = weight_fwd[:, None, None] * forward + weight_bwd[:, None, None] * backward
        unit = tangent / jnp.sqrt(lax.optimization_barrier(jnp.sum(tangent * tangent, axis=(1, 2))) + stabilizer)[:, None, None]
        inside = forces[1:-1]
        along = lax.optimization_barrier(jnp.sum(inside * unit, axis=(1, 2)))
        spring = spring_const * (jnp.sqrt(lax.optimization_barrier(jnp.sum(forward * forward, axis=(1, 2))) + stabilizer) - jnp.sqrt(lax.optimization_barrier(jnp.sum(backward * backward, axis=(1, 2))) + stabilizer))
        neb_inside = inside + (spring - along)[:, None, None] * unit
        edge = jnp.zeros_like(forces[:1])
        neb = jnp.concatenate([edge, neb_inside, edge], axis=0)
        speed_norm = jnp.sqrt(jnp.sum(inner_flag * velocity * velocity) + stabilizer)
        force_norm = jnp.sqrt(jnp.sum(neb * neb) + stabilizer)
        velocity = ((1.0 - fire_mixing) * velocity + fire_mixing * (speed_norm / force_norm) * neb + time_step * neb) * inner_flag
        displacement = displacement + time_step * velocity
    return (displacement, velocity)
```

```python
import functools
import math

import jax
import jax.numpy as jnp
from jax import lax
from jax.experimental import pallas as pl
from jax.experimental.pallas import tpu as pltpu
from jax.sharding import PartitionSpec as P

SIDE = 32
FIRE_STEPS = 2
QUANTITIES = 8
HALO = 2

lattice_const = 3.615
cutoff_sq = 9.61
nearest_sq = 6.533136
pair_scale = 30.0
pair_depth = 0.3
embed_scale = 1.2
bulk_root = 3.605551275463989
spring_const = 2.0
time_step = 0.1
fire_mixing = 0.1
stabilizer = 1e-06

reach_root = math.sqrt(cutoff_sq)
unit_half = 0.5 * lattice_const / reach_root
kappa = cutoff_sq / nearest_sq
dens_shift = (2.0 - kappa) / kappa
pair_shift = (2.5 - 2.0 * kappa) / (2.0 * kappa)
dens_scale = pair_scale * kappa
pair_energy_scale = pair_scale * pair_depth * 2.0 * kappa
dens_slope_shift = 0.75 * dens_shift
pair_slope_shift = 0.75 * pair_shift
dens_slope_scale = -4.0 * dens_scale / cutoff_sq
pair_slope_scale = -4.0 * pair_energy_scale / cutoff_sq
slope_ratio = dens_slope_scale / pair_slope_scale
force_scale = 2.0 * pair_slope_scale * reach_root


def shift_v(field, step, lanes):
    return pltpu.roll(field, (-step) % 128, 1)


def shift_u(field, step, lanes):
    turned = pltpu.roll(field, (-step * SIDE) % 128, 1)
    carried = pltpu.roll(turned, (-step) % 8, 0)
    edge = lanes >= 128 - SIDE if step > 0 else lanes < SIDE
    return jnp.where(edge, carried, turned)


def partners(field, step, lanes):
    along_u = shift_u(field, step, lanes)
    return (shift_v(field, step, lanes), along_u, shift_v(along_u, step, lanes))


def gather_back(at_v, at_u, at_uv, step, lanes):
    return shift_u(at_u + shift_v(at_uv, -step, lanes), -step, lanes) + shift_v(at_v, -step, lanes)


def limits(step, u, v):
    far = jnp.float32(-1e30)
    in_u = (u + step >= 0) & (u + step < SIDE)
    in_v = (v + step >= 0) & (v + step < SIDE)
    one = jnp.ones_like(u, jnp.float32)
    return (
        jnp.where(in_v, one, far),
        jnp.where(in_u, one, far),
        jnp.where(in_u & in_v, one, far),
    )


def force_kernel(own_ref, low_ref, high_ref, force_ref, energy_ref, pos, seps, slopes, rho, embed):
    f32 = jnp.float32
    planes = own_ref.shape[1]
    lanes = lax.broadcasted_iota(jnp.int32, (8, 128), 1)
    subl = lax.broadcasted_iota(jnp.int32, (8, 128), 0)
    site_u = subl * 4 + lanes // SIDE
    site_v = lanes % SIDE
    inverse = f32(1.0 / reach_root)
    pos[:, 0:HALO] = low_ref[...] * inverse
    pos[:, HALO + planes : HALO + planes + HALO] = high_ref[...] * inverse
    pos[:, planes + 2 * HALO :] = jnp.zeros((3, 2, 8, 128), f32)

    def fill(t, carry):
        for j in range(8):
            for axis in range(3):
                pos[axis, HALO + t * 8 + j] = own_ref[axis, t * 8 + j] * inverse
        return carry

    lax.fori_loop(0, planes // 8, fill, 0)

    def separations(e, step):
        h = f32(unit_half)
        sh = f32(step * unit_half)
        own = [pos[axis, e] for axis in range(3)]
        nxt = [pos[axis, e + 1] for axis in range(3)]
        turned = [partners(nxt[axis], step, lanes) for axis in range(3)]
        own_x = own[0] - h
        y_of = (own[1] + sh, own[1], own[1] - sh)
        z_of = (own[2] - sh, own[2], own[2] + sh)
        cross = [
            (nxt[0] - own_x, nxt[1] - y_of[0], nxt[2] - z_of[1]),
            (turned[0][0] - own_x, turned[1][0] - y_of[1], turned[2][0] - z_of[2]),
            (turned[0][1] - own_x, turned[1][1] - y_of[1], turned[2][1] - z_of[0]),
            (turned[0][2] - own_x, turned[1][2] - y_of[2], turned[2][2] - z_of[1]),
        ]
        near_y = nxt[1] - sh
        near_zv = nxt[2] + sh
        near_zu = nxt[2] - sh
        inside = [
            (turned[0][0] - nxt[0], turned[1][0] - near_y, turned[2][0] - near_zv),
            (turned[0][1] - nxt[0], turned[1][1] - near_y, turned[2][1] - near_zu),
        ]
        return cross + inside

    def density(e, step, bounds, carry):
        rho_part, sum_f, sum_c = carry
        one = jnp.ones((8, 128), f32)
        tops = (one, bounds[0], bounds[1], bounds[2], bounds[0], bounds[1])
        dens, cubes = [], []
        for k, sep in enumerate(separations(e, step)):
            y = sep[0] * sep[0] + sep[1] * sep[1] + sep[2] * sep[2]
            c = jnp.maximum(tops[k] - y, 0.0)
            square = c * c
            cube = square * c
            dens.append(cube * (c + f32(dens_shift)))
            cubes.append(cube)
            for axis in range(3):
                seps[e, k, axis] = sep[axis]
            slopes[e, k, 0] = square * (c + f32(pair_slope_shift))
            slopes[e, k, 1] = square * (c + f32(dens_slope_shift))
        cross = (dens[0] + dens[1]) + (dens[2] + dens[3])
        inside = dens[4] + dens[5]
        rho[e] = rho_part + cross
        back = gather_back(dens[1] + dens[4], dens[2] + dens[5], dens[3], step, lanes)
        weight = jnp.where((e >= 1) & (e <= planes), 1.0, 0.0).astype(f32)
        sum_f = sum_f + weight * (cross + inside)
        sum_c = sum_c + weight * (
            ((cubes[0] + cubes[1]) + (cubes[2] + cubes[3])) + (cubes[4] + cubes[5])
        )
        return (dens[0] + inside + back, sum_f, sum_c)

    down = limits(-1, site_u, site_v)
    up = limits(1, site_u, site_v)
    zero = jnp.zeros((8, 128), f32)

    def density_pair(t, carry):
        carry = density(2 * t, -1, down, carry)
        return density(2 * t + 1, 1, up, carry)

    _, sum_f, sum_c = lax.fori_loop(0, planes // 2 + 2, density_pair, (zero, zero, zero))

    def embedding(e):
        w = 1.0 + f32(dens_scale) * rho[e]
        inv = lax.rsqrt(w)
        embed[e] = f32(-0.5 * embed_scale * slope_ratio) * inv
        return w * inv - f32(bulk_root)

    embedding(0)
    embedding(1)
    embedding(HALO + planes)
    embedding(HALO + planes + 1)

    def embed_some(t, total):
        parts = [embedding(HALO + t * 8 + j) for j in range(8)]
        return total + (
            ((parts[0] + parts[1]) + (parts[2] + parts[3]))
            + ((parts[4] + parts[5]) + (parts[6] + parts[7]))
        )

    roots = lax.fori_loop(0, planes // 8, embed_some, zero)
    energy_ref[...] = f32(-embed_scale) * roots + f32(pair_energy_scale) * (
        sum_f + f32(pair_shift - dens_shift) * sum_c
    )

    def force(e, step, carry):
        own = embed[e]
        nxt = embed[e + 1]
        at_v, at_u, at_uv = partners(nxt, step, lanes)
        partner = (own + nxt, own + at_v, own + at_u, own + at_uv, nxt + at_v, nxt + at_u)
        weight = [slopes[e, k, 0] + partner[k] * slopes[e, k, 1] for k in range(6)]
        out = []
        for axis in range(3):
            g = [weight[k] * seps[e, k, axis] for k in range(6)]
            total = carry[axis] + ((g[0] + g[1]) + (g[2] + g[3]))
            force_ref[axis, jnp.maximum(e - HALO, 0)] = f32(force_scale) * total
            back = gather_back(g[1] + g[4], g[2] + g[5], g[3], step, lanes)
            out.append((g[4] + g[5]) - g[0] - back)
        return tuple(out)

    def force_pair(t, carry):
        carry = force(2 * t, -1, carry)
        return force(2 * t + 1, 1, carry)

    lax.fori_loop(0, planes // 2 + 1, force_pair, (zero, zero, zero))


def image_forces(own, low, high):
    vmem = pl.BlockSpec(memory_space=pltpu.VMEM)
    planes = own.shape[1]
    rows = planes + 2 * HALO
    return pl.pallas_call(
        force_kernel,
        out_shape=(
            jax.ShapeDtypeStruct((3, planes, 8, 128), jnp.float32),
            jax.ShapeDtypeStruct((8, 128), jnp.float32),
        ),
        in_specs=[vmem] * 3,
        out_specs=(vmem, vmem),
        scratch_shapes=[
            pltpu.VMEM((3, rows + 2, 8, 128), jnp.float32),
            pltpu.VMEM((rows, 6, 3, 8, 128), jnp.float32),
            pltpu.VMEM((rows, 6, 2, 8, 128), jnp.float32),
            pltpu.VMEM((rows, 8, 128), jnp.float32),
            pltpu.VMEM((rows, 8, 128), jnp.float32),
        ],
        compiler_params=pltpu.CompilerParams(vmem_limit_bytes=32 * 1024 * 1024),
        cost_estimate=pl.CostEstimate(
            flops=40_000_000, bytes_accessed=30_000_000, transcendentals=0
        ),
        name="slab_forces",
    )(own, low, high)


def total_of(tile):
    return jnp.sum(jnp.sum(tile, axis=0, keepdims=True), axis=1, keepdims=True)


def moment_kernel(count, *refs):
    path, forces, speeds = refs[: count + 2], refs[count + 2 : 2 * count + 2], refs[2 * count + 2 : 3 * count + 2]
    energies, out_ref, acc = refs[3 * count + 2 : 4 * count + 2], refs[4 * count + 2], refs[4 * count + 3]
    step = pl.program_id(0)
    planes = path[0].shape[1]
    zero = jnp.zeros((8, 128), jnp.float32)

    @pl.when(step == 0)
    def _():
        acc[...] = jnp.zeros_like(acc)

    def one(p, carry):
        carry = list(carry)
        for axis in range(3):
            at = [ref[axis, p] for ref in path]
            diff = [at[j + 1] - at[j] for j in range(count + 1)]
            square = [d * d for d in diff]
            for j in range(count):
                force, speed = forces[j][axis, p], speeds[j][axis, p]
                terms = (
                    force * force,
                    force * diff[j + 1],
                    force * diff[j],
                    square[j + 1],
                    square[j],
                    diff[j] * diff[j + 1],
                    speed * speed,
                )
                for k, term in enumerate(terms):
                    carry[7 * j + k] = carry[7 * j + k] + term
        return tuple(carry)

    def some(t, carry):
        for j in range(2):
            carry = one(2 * t + j, carry)
        return carry

    sums = lax.fori_loop(0, planes // 2, some, (zero,) * (7 * count))
    for k in range(7 * count):
        acc[k] += sums[k]

    @pl.when(step == pl.num_programs(0) - 1)
    def _():
        lane = lax.broadcasted_iota(jnp.int32, (1, 128), 1)
        row = jnp.zeros((1, 128), jnp.float32)
        for j in range(count):
            row = row + jnp.where(lane == 8 * j, total_of(energies[j][...]), 0.0)
            for k in range(7):
                row = row + jnp.where(lane == 8 * j + 1 + k, total_of(acc[7 * j + k]), 0.0)
        out_ref[...] = jnp.broadcast_to(row, out_ref.shape)


def moments(path, forces, speeds, energies, copies, chunk):
    count = len(forces)
    planes = path[0].shape[1]
    block = pl.BlockSpec((3, chunk, 8, 128), lambda t: (0, t, 0, 0))
    tile = pl.BlockSpec((8, 128), lambda t: (0, 0))
    return pl.pallas_call(
        functools.partial(moment_kernel, count),
        grid=(planes // chunk,),
        out_shape=jax.ShapeDtypeStruct((copies, 128), jnp.float32),
        in_specs=[block] * (3 * count + 2) + [tile] * count,
        out_specs=pl.BlockSpec((copies, 128), lambda t: (0, 0)),
        scratch_shapes=[pltpu.VMEM((7 * count, 8, 128), jnp.float32)],
        compiler_params=pltpu.CompilerParams(vmem_limit_bytes=32 * 1024 * 1024),
        name="path_moments",
    )(*path, *forces, *speeds, *energies)


def path_terms(summary, images):
    lane = lax.broadcasted_iota(jnp.int32, (8, 128), 1)
    image = lax.broadcasted_iota(jnp.int32, (8, 128), 0)

    def column(k):
        picked = jnp.sum(jnp.where(lane == k, summary, 0.0), axis=1, keepdims=True)
        return jnp.broadcast_to(picked, (8, 128))

    e_here, ff, f_fwd, f_bwd, fwd_sq, bwd_sq, fwd_bwd, speed_sq = [column(k) for k in range(8)]
    e_prev = pltpu.roll(e_here, 1, 0)
    e_next = pltpu.roll(e_here, 7, 0)
    inner = (image > 0) & (image < images - 1)
    rise = e_next - e_here
    fall = e_here - e_prev
    larger = jnp.maximum(jnp.abs(rise), jnp.abs(fall))
    smaller = jnp.minimum(jnp.abs(rise), jnp.abs(fall))
    upward = (e_next > e_here) & (e_here > e_prev)
    downward = (e_next < e_here) & (e_here < e_prev)
    toward = e_next > e_prev
    weight_fwd = jnp.where(
        upward, 1.0, jnp.where(downward, 0.0, jnp.where(toward, larger, smaller))
    )
    weight_bwd = jnp.where(
        upward, 0.0, jnp.where(downward, 1.0, jnp.where(toward, smaller, larger))
    )
    tangent_sq = (
        weight_fwd * weight_fwd * fwd_sq
        + 2.0 * weight_fwd * weight_bwd * fwd_bwd
        + weight_bwd * weight_bwd * bwd_sq
    )
    norm_sq = tangent_sq + stabilizer
    force_tan = weight_fwd * f_fwd + weight_bwd * f_bwd
    spring = spring_const * (jnp.sqrt(fwd_sq + stabilizer) - jnp.sqrt(bwd_sq + stabilizer))
    coefficient = -force_tan / norm_sq + spring / jnp.sqrt(norm_sq)
    neb_sq = ff + 2.0 * coefficient * force_tan + coefficient * coefficient * tangent_sq

    def over_inner(value):
        return jnp.sum(jnp.where(inner, value, 0.0), axis=0, keepdims=True)

    force_norm = jnp.sqrt(over_inner(neb_sq) + stabilizer)
    speed_norm = jnp.sqrt(over_inner(speed_sq) + stabilizer)
    gain = jnp.broadcast_to(fire_mixing * (speed_norm / force_norm) + time_step, (8, 128))
    keep = jnp.where(inner, 1.0 - fire_mixing, 0.0)
    push = jnp.where(inner, gain, 0.0)
    along_fwd = jnp.where(inner, gain * coefficient * weight_fwd, 0.0)
    along_bwd = jnp.where(inner, gain * coefficient * weight_bwd, 0.0)
    return keep, push, along_fwd, along_bwd


def update_kernel(count, images, first_ref, gathered_ref, *refs):
    path, forces, speeds = refs[: count + 2], refs[count + 2 : 2 * count + 2], refs[2 * count + 2 : 3 * count + 2]
    moved, new_speeds = refs[3 * count + 2 : 4 * count + 2], refs[4 * count + 2 : 5 * count + 2]
    terms = refs[5 * count + 2]
    planes = path[0].shape[1]

    @pl.when(pl.program_id(0) == 0)
    def _():
        image = lax.broadcasted_iota(jnp.int32, (8, 128), 0)
        lane = lax.broadcasted_iota(jnp.int32, (8, 128), 1)
        summary = jnp.zeros((8, 128), jnp.float32)
        per_group = gathered_ref.shape[0] // (images // count)
        for g in range(images // count):
            rows = gathered_ref[g * per_group : (g + 1) * per_group, :]
            row = jnp.broadcast_to(jnp.sum(rows, axis=0, keepdims=True), (8, 128))
            for j in range(count):
                own_row = row if j == 0 else pltpu.roll(row, 128 - 8 * j, 1)
                summary = jnp.where(image == g * count + j, own_row, summary)
        values = path_terms(summary, images)
        for j in range(count):
            here = image == first_ref[0] + j
            for k, value in enumerate(values):
                own = jnp.sum(jnp.where(here, value, 0.0), axis=0, keepdims=True)
                terms[j, k] = jnp.broadcast_to(own, (8, 128))

    def one(p):
        for axis in range(3):
            at = [ref[axis, p] for ref in path]
            for j in range(count):
                speed = (
                    terms[j, 0] * speeds[j][axis, p]
                    + terms[j, 1] * forces[j][axis, p]
                    + terms[j, 2] * (at[j + 2] - at[j + 1])
                    + terms[j, 3] * (at[j + 1] - at[j])
                )
                new_speeds[j][axis, p] = speed
                moved[j][axis, p] = at[j + 1] + time_step * speed

    def some(t, carry):
        for j in range(2):
            one(2 * t + j)
        return carry

    lax.fori_loop(0, planes // 2, some, 0)


def update(first, gathered, path, forces, speeds, images, chunk):
    count = len(forces)
    planes = path[0].shape[1]
    block = pl.BlockSpec((3, chunk, 8, 128), lambda t: (0, t, 0, 0))
    out = jax.ShapeDtypeStruct((3, planes, 8, 128), jnp.float32)
    results = pl.pallas_call(
        functools.partial(update_kernel, count, images),
        grid=(planes // chunk,),
        out_shape=(out,) * (2 * count),
        in_specs=[
            pl.BlockSpec(memory_space=pltpu.SMEM),
            pl.BlockSpec(gathered.shape, lambda t: (0, 0)),
        ]
        + [block] * (3 * count + 2),
        out_specs=(block,) * (2 * count),
        scratch_shapes=[pltpu.VMEM((count, 4, 8, 128), jnp.float32)],
        compiler_params=pltpu.CompilerParams(vmem_limit_bytes=32 * 1024 * 1024),
        name="fire_update",
    )(first, gathered, *path, *forces, *speeds)
    return results[:count], results[count:]


def local(displacement, velocity):
    planes = displacement.shape[2] // (SIDE * SIDE)
    own_image = lax.axis_index("image")
    images = lax.axis_size("image")
    slabs = lax.axis_size("domain")
    ahead = [(i, (i + 1) % slabs) for i in range(slabs)]
    behind = [(target, source) for source, target in ahead]
    first = own_image.astype(jnp.int32).reshape(1)
    current = displacement.reshape(3, planes, 8, 128)
    moving = velocity.reshape(3, planes, 8, 128)
    for step_index in range(FIRE_STEPS):
        low = lax.ppermute(current[:, -HALO:], "domain", ahead)
        high = lax.ppermute(current[:, :HALO], "domain", behind)
        before = lax.ppermute(current, "image", [(i, i + 1) for i in range(images - 1)])
        after = lax.ppermute(current, "image", [(i + 1, i) for i in range(images - 1)])
        forces, energy = image_forces(current, low, high)
        path = (before, current, after)
        payload = moments(path, (forces,), (moving,), (energy,), images * slabs, 16)
        gathered = lax.all_to_all(payload, ("image", "domain"), 0, 0, tiled=True)
        (current,), (moving,) = update(first, gathered, path, (forces,), (moving,), images, 16)
    return (current.reshape(displacement.shape), moving.reshape(velocity.shape))


def solution(mesh):
    spec = P("image", None, "domain")
    return jax.shard_map(
        local,
        mesh=mesh,
        in_specs=(spec, spec),
        out_specs=(spec, spec),
        check_vma=False,
    )
```

```python
import functools
import math

import jax
import jax.numpy as jnp
from jax import lax
from jax.experimental import pallas as pl
from jax.experimental.pallas import tpu as pltpu
from jax.sharding import PartitionSpec as P

SIDE = 32
FIRE_STEPS = 2
QUANTITIES = 8
HALO = 2
PLACE_UNROLL = 16
EMBED_UNROLL = 48
FINISH_UNROLL = 16
CHUNKS = 2
MOMENT_CHUNK = 12
UPDATE_CHUNK = 12

lattice_const = 3.615
cutoff_sq = 9.61
nearest_sq = 6.533136
pair_scale = 30.0
pair_depth = 0.3
embed_scale = 1.2
bulk_root = 3.605551275463989
spring_const = 2.0
time_step = 0.1
fire_mixing = 0.1
stabilizer = 1e-06

reach_root = math.sqrt(cutoff_sq)
unit_half = 0.5 * lattice_const / reach_root
kappa = cutoff_sq / nearest_sq
dens_shift = (2.0 - kappa) / kappa
pair_shift = (2.5 - 2.0 * kappa) / (2.0 * kappa)
dens_scale = pair_scale * kappa
pair_energy_scale = pair_scale * pair_depth * 2.0 * kappa
dens_slope_shift = 0.75 * dens_shift
pair_slope_shift = 0.75 * pair_shift
dens_slope_scale = -4.0 * dens_scale / cutoff_sq
pair_slope_scale = -4.0 * pair_energy_scale / cutoff_sq
slope_ratio = dens_slope_scale / pair_slope_scale
force_scale = 2.0 * pair_slope_scale * reach_root


def shift(field, step_u, step_v, lanes):
    reach = step_u * SIDE + step_v
    turned = pltpu.roll(field, (-reach) % 128, 1)
    if step_u == 0:
        return turned
    carried = pltpu.roll(turned, (-step_u) % 8, 0)
    return jnp.where(lanes >= 128 - reach if reach > 0 else lanes < -reach, carried, turned)


def partners(field, step, lanes):
    return (
        shift(field, 0, step, lanes),
        shift(field, step, 0, lanes),
        shift(field, step, step, lanes),
    )


def gather_back(at_v, at_u, at_uv, step, lanes):
    return (
        shift(at_v, 0, -step, lanes)
        + shift(at_u, -step, 0, lanes)
        + shift(at_uv, -step, -step, lanes)
    )


def limits(step, u, v):
    far = jnp.float32(-1e30)
    in_u = (u + step >= 0) & (u + step < SIDE)
    in_v = (v + step >= 0) & (v + step < SIDE)
    one = jnp.ones_like(u, jnp.float32)
    return (
        jnp.where(in_v, one, far),
        jnp.where(in_u, one, far),
        jnp.where(in_u & in_v, one, far),
    )


def side_of(plane):
    return 1 if plane % 2 == 0 else -1


def force_kernel(
    own_ref, low_ref, high_ref, force_ref, energy_ref, pos, turned, seps, slopes, rho, back, embed, force_back
):
    f32 = jnp.float32
    planes = own_ref.shape[1]
    top = planes + 2 * HALO
    lanes = lax.broadcasted_iota(jnp.int32, (8, 128), 1)
    subl = lax.broadcasted_iota(jnp.int32, (8, 128), 0)
    site_u = subl * 4 + lanes // SIDE
    site_v = lanes % SIDE
    inverse = f32(1.0 / reach_root)
    zero = jnp.zeros((8, 128), f32)

    def place(q, side, values):
        for axis in range(3):
            value = values[axis] * inverse
            pos[axis, q] = value
            for k, seen in enumerate(partners(value, side, lanes)):
                turned[axis, k, q] = seen

    for q in range(HALO):
        place(q, side_of(q), [low_ref[axis, q] for axis in range(3)])
        place(planes + HALO + q, side_of(q), [high_ref[axis, q] for axis in range(3)])

    def place_some(t, carry):
        for j in range(PLACE_UNROLL):
            p = t * PLACE_UNROLL + j
            place(p + HALO, side_of(j), [own_ref[axis, p] for axis in range(3)])
        return carry

    lax.fori_loop(0, planes // PLACE_UNROLL, place_some, 0)

    def separations(e, step):
        h = f32(unit_half)
        sh = f32(step * unit_half)
        own = [pos[axis, e] for axis in range(3)]
        nxt = [pos[axis, e + 1] for axis in range(3)]
        seen = [[turned[axis, k, e + 1] for k in range(3)] for axis in range(3)]
        own_x = own[0] - h
        y_of = (own[1] + sh, own[1], own[1] - sh)
        z_of = (own[2] - sh, own[2], own[2] + sh)
        cross = [
            (nxt[0] - own_x, nxt[1] - y_of[0], nxt[2] - z_of[1]),
            (seen[0][0] - own_x, seen[1][0] - y_of[1], seen[2][0] - z_of[2]),
            (seen[0][1] - own_x, seen[1][1] - y_of[1], seen[2][1] - z_of[0]),
            (seen[0][2] - own_x, seen[1][2] - y_of[2], seen[2][2] - z_of[1]),
        ]
        near_y = nxt[1] - sh
        near_zv = nxt[2] + sh
        near_zu = nxt[2] - sh
        inside = [
            (seen[0][0] - nxt[0], seen[1][0] - near_y, seen[2][0] - near_zv),
            (seen[0][1] - nxt[0], seen[1][1] - near_y, seen[2][1] - near_zu),
        ]
        return cross + inside

    def density(e, step, bounds, carry):
        rho_part, sum_f, sum_c = carry
        one = jnp.ones((8, 128), f32)
        tops = (one, bounds[0], bounds[1], bounds[2], bounds[0], bounds[1])
        dens, cubes = [], []
        for k, sep in enumerate(separations(e, step)):
            y = sep[0] * sep[0] + sep[1] * sep[1] + sep[2] * sep[2]
            c = jnp.maximum(tops[k] - y, 0.0)
            square = c * c
            cube = square * c
            dens.append(cube * (c + f32(dens_shift)))
            cubes.append(cube)
            for axis in range(3):
                seps[e, k, axis] = sep[axis]
            slopes[e, k, 0] = square * (c + f32(pair_slope_shift))
            slopes[e, k, 1] = square * (c + f32(dens_slope_shift))
        cross = (dens[0] + dens[1]) + (dens[2] + dens[3])
        inside = dens[4] + dens[5]
        rho[e] = rho_part + cross
        back[0, e + 1] = dens[1] + dens[4]
        back[1, e + 1] = dens[2] + dens[5]
        back[2, e + 1] = dens[3]
        weight = jnp.where((e >= 1) & (e <= planes), 1.0, 0.0).astype(f32)
        sum_f = sum_f + weight * (cross + inside)
        sum_c = sum_c + weight * (
            ((cubes[0] + cubes[1]) + (cubes[2] + cubes[3])) + (cubes[4] + cubes[5])
        )
        return (dens[0] + inside, sum_f, sum_c)

    down = limits(-1, site_u, site_v)
    up = limits(1, site_u, site_v)

    def density_pair(t, carry):
        carry = density(2 * t, -1, down, carry)
        return density(2 * t + 1, 1, up, carry)

    carry = lax.fori_loop(0, planes // 2 + 1, density_pair, (zero, zero, zero))
    _, sum_f, sum_c = density(planes + 2, -1, down, carry)

    def embedding(q, side):
        total = rho[q] + gather_back(back[0, q], back[1, q], back[2, q], side, lanes)
        w = 1.0 + f32(dens_scale) * total
        inv = lax.rsqrt(w)
        embed[0, q] = f32(-0.5 * embed_scale * slope_ratio) * inv
        return w * inv - f32(bulk_root)

    embedding(1, side_of(1))
    embedding(planes + HALO, side_of(0))

    def embed_some(t, total):
        for j in range(EMBED_UNROLL):
            total = total + embedding(HALO + t * EMBED_UNROLL + j, side_of(j))
        return total

    roots = lax.fori_loop(0, planes // EMBED_UNROLL, embed_some, zero)
    energy_ref[...] = f32(-embed_scale) * roots + f32(pair_energy_scale) * (
        sum_f + f32(pair_shift - dens_shift) * sum_c
    )

    def see(q, side):
        for k, seen in enumerate(partners(embed[0, q], side, lanes)):
            embed[1 + k, q] = seen

    see(planes + HALO, side_of(0))

    def see_some(t, carry):
        for j in range(EMBED_UNROLL):
            see(HALO + t * EMBED_UNROLL + j, side_of(j))
        return carry

    lax.fori_loop(0, planes // EMBED_UNROLL, see_some, 0)

    def force(e, keep, carry):
        own = embed[0, e]
        nxt = embed[0, e + 1]
        at_v, at_u, at_uv = [embed[1 + k, e + 1] for k in range(3)]
        partner = (own + nxt, own + at_v, own + at_u, own + at_uv, nxt + at_v, nxt + at_u)
        weight = [slopes[e, k, 0] + partner[k] * slopes[e, k, 1] for k in range(6)]
        out = []
        for axis in range(3):
            g = [weight[k] * seps[e, k, axis] for k in range(6)]
            if keep:
                force_ref[axis, e - HALO] = carry[axis] + ((g[0] + g[1]) + (g[2] + g[3]))
            force_back[axis, 0, e + 1] = g[1] + g[4]
            force_back[axis, 1, e + 1] = g[2] + g[5]
            force_back[axis, 2, e + 1] = g[3]
            out.append((g[4] + g[5]) - g[0])
        return tuple(out)

    def force_pair(t, carry):
        carry = force(HALO + 2 * t, True, carry)
        return force(HALO + 2 * t + 1, True, carry)

    lax.fori_loop(0, planes // 2, force_pair, force(1, False, (zero, zero, zero)))

    def finish(t, carry):
        for j in range(FINISH_UNROLL):
            p = t * FINISH_UNROLL + j
            for axis in range(3):
                parts = [force_back[axis, k, p + HALO] for k in range(3)]
                force_ref[axis, p] = f32(force_scale) * (
                    force_ref[axis, p] - gather_back(*parts, side_of(j), lanes)
                )
        return carry

    lax.fori_loop(0, planes // FINISH_UNROLL, finish, 0)


def image_forces(own, low, high):
    vmem = pl.BlockSpec(memory_space=pltpu.VMEM)
    planes = own.shape[1]
    rows = planes + 2 * HALO
    return pl.pallas_call(
        force_kernel,
        out_shape=(
            jax.ShapeDtypeStruct((3, planes, 8, 128), jnp.float32),
            jax.ShapeDtypeStruct((8, 128), jnp.float32),
        ),
        in_specs=[vmem] * 3,
        out_specs=(vmem, vmem),
        scratch_shapes=[
            pltpu.VMEM((3, rows, 8, 128), jnp.float32),
            pltpu.VMEM((3, 3, rows, 8, 128), jnp.float32),
            pltpu.VMEM((rows, 6, 3, 8, 128), jnp.float32),
            pltpu.VMEM((rows, 6, 2, 8, 128), jnp.float32),
            pltpu.VMEM((rows, 8, 128), jnp.float32),
            pltpu.VMEM((3, rows, 8, 128), jnp.float32),
            pltpu.VMEM((4, rows, 8, 128), jnp.float32),
            pltpu.VMEM((3, 3, rows, 8, 128), jnp.float32),
        ],
        compiler_params=pltpu.CompilerParams(vmem_limit_bytes=40 * 1024 * 1024),
        cost_estimate=pl.CostEstimate(
            flops=40_000_000, bytes_accessed=30_000_000, transcendentals=0
        ),
        name="slab_forces",
    )(own, low, high)


def total_of(tile):
    return jnp.sum(jnp.sum(tile, axis=0, keepdims=True), axis=1, keepdims=True)


def moment_kernel(side_ref, *refs):
    path, forces, speeds, energies = refs[:4], refs[4:6], refs[6:8], refs[8:10]
    out_ref, acc = refs[10], refs[11]
    step = pl.program_id(0)
    planes = path[0].shape[1]
    zero = jnp.zeros((8, 128), jnp.float32)

    @pl.when(step == 0)
    def _():
        acc[...] = jnp.zeros_like(acc)

    def one(p, carry):
        carry = list(carry)
        for axis in range(3):
            at = [ref[axis, p] for ref in path]
            diff = [at[j + 1] - at[j] for j in range(3)]
            square = [d * d for d in diff]
            for j in range(2):
                force, speed = forces[j][axis, p], speeds[j][axis, p]
                terms = (
                    force * force,
                    force * diff[j + 1],
                    force * diff[j],
                    square[j + 1],
                    square[j],
                    diff[j] * diff[j + 1],
                    speed * speed,
                )
                for k, term in enumerate(terms):
                    carry[7 * j + k] = carry[7 * j + k] + term
        return tuple(carry)

    def some(t, carry):
        for j in range(2):
            carry = one(2 * t + j, carry)
        return carry

    sums = lax.fori_loop(0, planes // 2, some, (zero,) * 14)
    for k in range(14):
        acc[k] += sums[k]

    @pl.when(step == pl.num_programs(0) - 1)
    def _():
        lane = lax.broadcasted_iota(jnp.int32, (1, 128), 1)
        odd = side_ref[0] == 1
        sign = jnp.where(odd, -1.0, 1.0).astype(jnp.float32)
        row = jnp.zeros((1, 128), jnp.float32)
        for j in range(2):
            ahead = [total_of(acc[7 * j + k]) for k in range(7)]
            values = (
                total_of(energies[j][...]),
                ahead[0],
                sign * jnp.where(odd, ahead[2], ahead[1]),
                sign * jnp.where(odd, ahead[1], ahead[2]),
                jnp.where(odd, ahead[4], ahead[3]),
                jnp.where(odd, ahead[3], ahead[4]),
                ahead[5],
                ahead[6],
            )
            for k, value in enumerate(values):
                row = row + jnp.where(lane == 8 * j + k, value, 0.0)
        out_ref[...] = jnp.broadcast_to(row, out_ref.shape)


def moments(side, path, forces, speeds, energies, copies, chunk):
    planes = path[0].shape[1]
    block = pl.BlockSpec((3, chunk, 8, 128), lambda t: (0, t, 0, 0))
    tile = pl.BlockSpec((8, 128), lambda t: (0, 0))
    return pl.pallas_call(
        moment_kernel,
        grid=(planes // chunk,),
        out_shape=jax.ShapeDtypeStruct((copies, 128), jnp.float32),
        in_specs=[pl.BlockSpec(memory_space=pltpu.SMEM)] + [block] * 8 + [tile] * 2,
        out_specs=pl.BlockSpec((copies, 128), lambda t: (0, 0)),
        scratch_shapes=[pltpu.VMEM((14, 8, 128), jnp.float32)],
        compiler_params=pltpu.CompilerParams(vmem_limit_bytes=32 * 1024 * 1024),
        name="path_moments",
    )(side, *path, *forces, *speeds, *energies)


def path_terms(summary, images):
    lane = lax.broadcasted_iota(jnp.int32, (8, 128), 1)
    image = lax.broadcasted_iota(jnp.int32, (8, 128), 0)

    def column(k):
        picked = jnp.sum(jnp.where(lane == k, summary, 0.0), axis=1, keepdims=True)
        return jnp.broadcast_to(picked, (8, 128))

    e_here, ff, f_fwd, f_bwd, fwd_sq, bwd_sq, fwd_bwd, speed_sq = [column(k) for k in range(8)]
    e_prev = pltpu.roll(e_here, 1, 0)
    e_next = pltpu.roll(e_here, 7, 0)
    inner = (image > 0) & (image < images - 1)
    rise = e_next - e_here
    fall = e_here - e_prev
    larger = jnp.maximum(jnp.abs(rise), jnp.abs(fall))
    smaller = jnp.minimum(jnp.abs(rise), jnp.abs(fall))
    upward = (e_next > e_here) & (e_here > e_prev)
    downward = (e_next < e_here) & (e_here < e_prev)
    toward = e_next > e_prev
    weight_fwd = jnp.where(
        upward, 1.0, jnp.where(downward, 0.0, jnp.where(toward, larger, smaller))
    )
    weight_bwd = jnp.where(
        upward, 0.0, jnp.where(downward, 1.0, jnp.where(toward, smaller, larger))
    )
    tangent_sq = (
        weight_fwd * weight_fwd * fwd_sq
        + 2.0 * weight_fwd * weight_bwd * fwd_bwd
        + weight_bwd * weight_bwd * bwd_sq
    )
    norm_sq = tangent_sq + stabilizer
    force_tan = weight_fwd * f_fwd + weight_bwd * f_bwd
    spring = spring_const * (jnp.sqrt(fwd_sq + stabilizer) - jnp.sqrt(bwd_sq + stabilizer))
    coefficient = -force_tan / norm_sq + spring / jnp.sqrt(norm_sq)
    neb_sq = ff + 2.0 * coefficient * force_tan + coefficient * coefficient * tangent_sq

    def over_inner(value):
        return jnp.sum(jnp.where(inner, value, 0.0), axis=0, keepdims=True)

    force_norm = jnp.sqrt(over_inner(neb_sq) + stabilizer)
    speed_norm = jnp.sqrt(over_inner(speed_sq) + stabilizer)
    gain = jnp.broadcast_to(fire_mixing * (speed_norm / force_norm) + time_step, (8, 128))
    keep = jnp.where(inner, 1.0 - fire_mixing, 0.0)
    push = jnp.where(inner, gain, 0.0)
    along_fwd = jnp.where(inner, gain * coefficient * weight_fwd, 0.0)
    along_bwd = jnp.where(inner, gain * coefficient * weight_bwd, 0.0)
    return keep, push, along_fwd, along_bwd


def step_terms(image_ref, gathered_ref, images, terms):
    image = lax.broadcasted_iota(jnp.int32, (8, 128), 0)
    summary = jnp.zeros((8, 128), jnp.float32)
    slabs = gathered_ref.shape[0] // images
    for g in range(images):
        rows = gathered_ref[g * slabs : (g + 1) * slabs, :]
        row = jnp.broadcast_to(jnp.sum(rows, axis=0, keepdims=True), (8, 128))
        summary = summary + jnp.where(image == g, row, 0.0)
        summary = summary + jnp.where(image == (g ^ 1), pltpu.roll(row, 120, 1), 0.0)
    keep, push, along_fwd, along_bwd = path_terms(summary, images)
    here = image_ref[0]
    odd = here % 2 == 1
    values = (keep, push, jnp.where(odd, -along_bwd, along_fwd), jnp.where(odd, -along_fwd, along_bwd))
    for j in range(2):
        at = image == (here + j * (1 - 2 * (here % 2)))
        for k, value in enumerate(values):
            own = jnp.sum(jnp.where(at, value, 0.0), axis=0, keepdims=True)
            terms[j, k] = jnp.broadcast_to(own, (8, 128))


def new_speed(terms, j, speed, force, ahead, behind):
    return terms[j, 0] * speed + terms[j, 1] * force + terms[j, 2] * ahead + terms[j, 3] * behind


def update_kernel(images, image_ref, gathered_ref, *refs):
    path, forces, speeds, moved, new_speeds = refs[:4], refs[4:6], refs[6:8], refs[8:10], refs[10:12]
    terms = refs[12]
    planes = path[0].shape[1]

    @pl.when(pl.program_id(0) == 0)
    def _():
        step_terms(image_ref, gathered_ref, images, terms)

    def some(t, carry):
        for i in range(2):
            p = 2 * t + i
            for axis in range(3):
                at = [ref[axis, p] for ref in path]
                diff = [at[j + 1] - at[j] for j in range(3)]
                for j in range(2):
                    speed = new_speed(terms, j, speeds[j][axis, p], forces[j][axis, p], diff[j + 1], diff[j])
                    new_speeds[j][axis, p] = speed
                    moved[j][axis, p] = at[j + 1] + time_step * speed
        return carry

    lax.fori_loop(0, planes // 2, some, 0)


def update(image, gathered, path, forces, speeds, images, chunk):
    planes = path[0].shape[1]
    block = pl.BlockSpec((3, chunk, 8, 128), lambda t: (0, t, 0, 0))
    out = jax.ShapeDtypeStruct((3, planes, 8, 128), jnp.float32)
    results = pl.pallas_call(
        functools.partial(update_kernel, images),
        grid=(planes // chunk,),
        out_shape=(out,) * 4,
        in_specs=[
            pl.BlockSpec(memory_space=pltpu.SMEM),
            pl.BlockSpec(gathered.shape, lambda t: (0, 0)),
        ]
        + [block] * 8,
        out_specs=(block,) * 4,
        scratch_shapes=[pltpu.VMEM((2, 4, 8, 128), jnp.float32)],
        compiler_params=pltpu.CompilerParams(vmem_limit_bytes=32 * 1024 * 1024),
        name="fire_update",
    )(image, gathered, *path, *forces, *speeds)
    return results[:2], results[2:]


def last_partner_kernel(images, image_ref, gathered_ref, before, here, after, force, speed, new_ref, terms_ref, terms):
    planes = here.shape[1]

    @pl.when(pl.program_id(0) == 0)
    def _():
        step_terms(image_ref, gathered_ref, images, terms)
        terms_ref[...] = terms[...]

    def some(t, carry):
        for i in range(2):
            p = 2 * t + i
            for axis in range(3):
                at = here[axis, p]
                new_ref[axis, p] = new_speed(
                    terms, 1, speed[axis, p], force[axis, p], after[axis, p] - at, at - before[axis, p]
                )
        return carry

    lax.fori_loop(0, planes // 2, some, 0)


def last_partner(image, gathered, path, force, speed, images, chunk):
    planes = force.shape[1]
    block = pl.BlockSpec((3, chunk, 8, 128), lambda t: (0, t, 0, 0))
    return pl.pallas_call(
        functools.partial(last_partner_kernel, images),
        grid=(planes // chunk,),
        out_shape=(
            jax.ShapeDtypeStruct((3, planes, 8, 128), jnp.float32),
            jax.ShapeDtypeStruct((2, 4, 8, 128), jnp.float32),
        ),
        in_specs=[
            pl.BlockSpec(memory_space=pltpu.SMEM),
            pl.BlockSpec(gathered.shape, lambda t: (0, 0)),
        ]
        + [block] * 5,
        out_specs=(block, pl.BlockSpec((2, 4, 8, 128), lambda t: (0, 0, 0, 0))),
        scratch_shapes=[pltpu.VMEM((2, 4, 8, 128), jnp.float32)],
        compiler_params=pltpu.CompilerParams(vmem_limit_bytes=32 * 1024 * 1024),
        name="last_partner",
    )(image, gathered, *path, force, speed)


def last_own_kernel(side_ref, terms, before, here, after, force, speed, moved, new_ref):
    planes = here.shape[1]

    def some(t, carry):
        for i in range(2):
            p = 2 * t + i
            for axis in range(3):
                at = here[axis, p]
                new = new_speed(
                    terms, 0, speed[axis, p], force[axis, p], after[axis, p] - at, at - before[axis, p]
                )
                new_ref[axis, p] = new
                moved[axis, p] = at + time_step * new
        return carry

    lax.fori_loop(0, planes // 2, some, 0)


def last_own(side, terms, path, force, speed, chunk):
    planes = force.shape[1]
    steps = planes // chunk
    block = pl.BlockSpec((3, chunk, 8, 128), lambda t, side_ref: (0, t, 0, 0))
    half = pl.BlockSpec((3, chunk, 8, 128), lambda t, side_ref: (0, side_ref[0] * steps + t, 0, 0))
    out = jax.ShapeDtypeStruct((3, 2 * planes, 8, 128), jnp.float32)
    return pl.pallas_call(
        last_own_kernel,
        grid_spec=pltpu.PrefetchScalarGridSpec(
            num_scalar_prefetch=1,
            grid=(steps,),
            in_specs=[pl.BlockSpec((2, 4, 8, 128), lambda t, side_ref: (0, 0, 0, 0))] + [block] * 5,
            out_specs=(half, half),
        ),
        out_shape=(out, out),
        compiler_params=pltpu.CompilerParams(vmem_limit_bytes=32 * 1024 * 1024),
        name="last_own",
    )(side, terms, *path, force, speed)


def last_join_kernel(side_ref, here, speed, moved_in, speed_in, moved, new_ref):
    planes = here.shape[1]

    def some(t, carry):
        for i in range(4):
            for axis in range(3):
                p = 4 * t + i
                new = speed[axis, p]
                new_ref[axis, p] = new
                moved[axis, p] = here[axis, p] + time_step * new
        return carry

    lax.fori_loop(0, planes // 4, some, 0)


def last_join(side, here, speed, moved, speeds, chunk):
    planes = here.shape[1]
    steps = planes // chunk
    block = pl.BlockSpec((3, chunk, 8, 128), lambda t, side_ref: (0, t, 0, 0))
    half = pl.BlockSpec(
        (3, chunk, 8, 128), lambda t, side_ref: (0, (1 - side_ref[0]) * steps + t, 0, 0)
    )
    out = jax.ShapeDtypeStruct(moved.shape, jnp.float32)
    whole = pl.BlockSpec(memory_space=pl.ANY)
    return pl.pallas_call(
        last_join_kernel,
        grid_spec=pltpu.PrefetchScalarGridSpec(
            num_scalar_prefetch=1,
            grid=(steps,),
            in_specs=[block, block, whole, whole],
            out_specs=(half, half),
        ),
        out_shape=(out, out),
        input_output_aliases={3: 0, 4: 1},
        compiler_params=pltpu.CompilerParams(vmem_limit_bytes=32 * 1024 * 1024),
        name="last_join",
    )(side, here, speed, moved, speeds)


def local(displacement, velocity):
    planes = displacement.shape[2] // (SIDE * SIDE)
    half = planes // 2
    images, slabs = lax.axis_size("image"), lax.axis_size("domain")
    both = ("image", "domain")
    own_image = lax.axis_index("image").astype(jnp.int32)
    side = own_image % 2
    is_low = side == 0
    image_arg, side_arg = own_image.reshape(1), side.reshape(1)
    slab = displacement.reshape(3, planes, 8, 128)
    slab_speed = velocity.reshape(3, planes, 8, 128)

    def at(image, domain):
        return image * slabs + domain % slabs

    everyone = [(i, d) for i in range(images) for d in range(slabs)]
    outer_own = [(at(i, d), at(i, d + 1 - 2 * (i % 2))) for i, d in everyone]
    outer_partner = [(at(i, d), at(i ^ 1, d - 1 + 2 * (i % 2))) for i, d in everyone]
    across = [(i, i ^ 1) for i in range(images)]
    own_out = [(i, i - 2 + 4 * (i % 2)) for i in range(images)]
    own_out = [(a, b) for a, b in own_out if 0 <= b < images]
    partner_out = [(b, a) for a, b in own_out]
    upward = [(at(i, d), at(i ^ 1, d + i % 2)) for i, d in everyone]
    downward = [(b, a) for a, b in upward]

    def planes_from(array, start, count):
        return lax.dynamic_slice_in_dim(array, start, count, axis=1)

    end = planes - HALO
    halo_own = lax.ppermute(planes_from(slab, (1 - side) * end, HALO), both, outer_own)
    halo_partner = lax.ppermute(planes_from(slab, side * end, HALO), both, outer_partner)
    halo_inner = lax.ppermute(planes_from(slab, half - HALO + HALO * side, HALO), "image", across)
    own = planes_from(slab, half * side, half)
    own_speed = planes_from(slab_speed, half * side, half)
    piece = half // CHUNKS
    pieces = [
        lax.ppermute(planes_from(slab, half * (1 - side) + c * piece, piece), "image", across)
        for c in range(CHUNKS)
    ]
    beyond_own = lax.ppermute(own, "image", own_out)
    beyond_partner = jnp.concatenate(
        [lax.ppermute(part, "image", partner_out) for part in pieces], axis=1
    )
    partner = jnp.concatenate(pieces, axis=1)
    partner_speed = lax.ppermute(planes_from(slab_speed, half * (1 - side), half), "image", across)
    near_low, near_high = slab[:, half - HALO : half], slab[:, half : half + HALO]
    own_halo = (jnp.where(is_low, halo_own, near_low), jnp.where(is_low, near_high, halo_own))
    partner_halo = (
        jnp.where(is_low, halo_partner, halo_inner),
        jnp.where(is_low, halo_inner, halo_partner),
    )

    path = (beyond_partner, own, partner, beyond_own)
    speeds = (own_speed, partner_speed)
    halos = (own_halo, partner_halo)
    for step_index in range(FIRE_STEPS):
        results = [image_forces(part, *halo) for part, halo in zip(path[1:3], halos)]
        forces, energies = zip(*results)
        payload = moments(side_arg, path, forces, speeds, energies, images * slabs, MOMENT_CHUNK)
        gathered = lax.all_to_all(payload, both, 0, 0, tiled=True)
        if step_index == FIRE_STEPS - 1:
            break
        moved, speeds = update(image_arg, gathered, path, forces, speeds, images, UPDATE_CHUNK)
        tops = jnp.stack([part[:, half - HALO :] for part in moved])
        bottoms = jnp.stack([part[:, :HALO] for part in moved])
        low = lax.ppermute(tops, both, upward)
        high = lax.ppermute(bottoms, both, downward)
        halos = ((low[1], high[1]), (low[0], high[0]))
        path = (
            lax.ppermute(moved[1], "image", partner_out),
            moved[0],
            moved[1],
            lax.ppermute(moved[0], "image", own_out),
        )
        returned = lax.ppermute(moved[1], "image", across)
    last_speed, terms = last_partner(
        image_arg, gathered, path[1:], forces[1], speeds[1], images, UPDATE_CHUNK
    )
    returned_speed = lax.ppermute(last_speed, "image", across)
    moved, new_speeds = last_own(side_arg, terms, path[:3], forces[0], speeds[0], UPDATE_CHUNK)
    moved, new_speeds = last_join(side_arg, returned, returned_speed, moved, new_speeds, UPDATE_CHUNK)
    return (moved.reshape(displacement.shape), new_speeds.reshape(velocity.shape))


def solution(mesh):
    spec = P("image", None, "domain")
    return jax.shard_map(
        local,
        mesh=mesh,
        in_specs=(spec, spec),
        out_specs=(spec, spec),
        check_vma=False,
    )
```

```python
import functools
import math

import jax
import jax.numpy as jnp
from jax import lax
from jax.experimental import pallas as pl
from jax.experimental.pallas import tpu as pltpu
from jax.sharding import PartitionSpec as P

SIDE = 32
FIRE_STEPS = 2
QUANTITIES = 8
HALO = 2
PLACE_UNROLL = 16
EMBED_UNROLL = 48
FINISH_UNROLL = 16
REGIONS = 2
JOIN_STEPS = 2

lattice_const = 3.615
cutoff_sq = 9.61
nearest_sq = 6.533136
pair_scale = 30.0
pair_depth = 0.3
embed_scale = 1.2
bulk_root = 3.605551275463989
spring_const = 2.0
time_step = 0.1
fire_mixing = 0.1
stabilizer = 1e-06

reach_root = math.sqrt(cutoff_sq)
unit_half = 0.5 * lattice_const / reach_root
kappa = cutoff_sq / nearest_sq
dens_shift = (2.0 - kappa) / kappa
pair_shift = (2.5 - 2.0 * kappa) / (2.0 * kappa)
dens_scale = pair_scale * kappa
pair_energy_scale = pair_scale * pair_depth * 2.0 * kappa
dens_slope_shift = 0.75 * dens_shift
pair_slope_shift = 0.75 * pair_shift
dens_slope_scale = -4.0 * dens_scale / cutoff_sq
pair_slope_scale = -4.0 * pair_energy_scale / cutoff_sq
slope_ratio = dens_slope_scale / pair_slope_scale
force_scale = 2.0 * pair_slope_scale * reach_root


def shift(field, step_u, step_v, lanes):
    reach = step_u * SIDE + step_v
    turned = pltpu.roll(field, (-reach) % 128, 1)
    if step_u == 0:
        return turned
    carried = pltpu.roll(turned, (-step_u) % 8, 0)
    return jnp.where(lanes >= 128 - reach if reach > 0 else lanes < -reach, carried, turned)


def partners(field, step, lanes):
    return (
        shift(field, 0, step, lanes),
        shift(field, step, 0, lanes),
        shift(field, step, step, lanes),
    )


def gather_back(at_v, at_u, at_uv, step, lanes):
    return (
        shift(at_v, 0, -step, lanes)
        + shift(at_u, -step, 0, lanes)
        + shift(at_uv, -step, -step, lanes)
    )


def limits(step, u, v):
    far = jnp.float32(-1e30)
    in_u = (u + step >= 0) & (u + step < SIDE)
    in_v = (v + step >= 0) & (v + step < SIDE)
    one = jnp.ones_like(u, jnp.float32)
    return (
        jnp.where(in_v, one, far),
        jnp.where(in_u, one, far),
        jnp.where(in_u & in_v, one, far),
    )


def side_of(plane):
    return 1 if plane % 2 == 0 else -1


def force_kernel(starts, slots, side_ref, *refs):
    count = len(starts)
    sources = [ref if slot is None else ref.at[slot] for ref, slot in zip(refs, slots)]
    force_ref, energy_ref, pos, turned, seps, slopes, rho, back, embed, force_back = refs[count:]
    f32 = jnp.float32
    planes = force_ref.shape[1]
    lanes = lax.broadcasted_iota(jnp.int32, (8, 128), 1)
    subl = lax.broadcasted_iota(jnp.int32, (8, 128), 0)
    site_u = subl * 4 + lanes // SIDE
    site_v = lanes % SIDE
    inverse = f32(1.0 / reach_root)
    zero = jnp.zeros((8, 128), f32)

    def place(q, side, values):
        for axis in range(3):
            value = values[axis] * inverse
            pos[axis, q] = value
            for k, seen in enumerate(partners(value, side, lanes)):
                turned[axis, k, q] = seen

    for k, source in enumerate(sources):
        rows = source.shape[1]
        unroll = rows if rows <= 24 else PLACE_UNROLL

        def place_some(t, carry, source=source, start=at_side(starts[k], side_ref), unroll=unroll):
            for j in range(unroll):
                p = t * unroll + j
                place(start + p, side_of(j), [source[axis, p] for axis in range(3)])
            return carry

        lax.fori_loop(0, rows // unroll, place_some, 0)

    def separations(e, step):
        h = f32(unit_half)
        sh = f32(step * unit_half)
        own = [pos[axis, e] for axis in range(3)]
        nxt = [pos[axis, e + 1] for axis in range(3)]
        seen = [[turned[axis, k, e + 1] for k in range(3)] for axis in range(3)]
        own_x = own[0] - h
        y_of = (own[1] + sh, own[1], own[1] - sh)
        z_of = (own[2] - sh, own[2], own[2] + sh)
        cross = [
            (nxt[0] - own_x, nxt[1] - y_of[0], nxt[2] - z_of[1]),
            (seen[0][0] - own_x, seen[1][0] - y_of[1], seen[2][0] - z_of[2]),
            (seen[0][1] - own_x, seen[1][1] - y_of[1], seen[2][1] - z_of[0]),
            (seen[0][2] - own_x, seen[1][2] - y_of[2], seen[2][2] - z_of[1]),
        ]
        near_y = nxt[1] - sh
        near_zv = nxt[2] + sh
        near_zu = nxt[2] - sh
        inside = [
            (seen[0][0] - nxt[0], seen[1][0] - near_y, seen[2][0] - near_zv),
            (seen[0][1] - nxt[0], seen[1][1] - near_y, seen[2][1] - near_zu),
        ]
        return cross + inside

    def density(e, step, bounds, carry):
        rho_part, sum_f, sum_c = carry
        one = jnp.ones((8, 128), f32)
        tops = (one, bounds[0], bounds[1], bounds[2], bounds[0], bounds[1])
        dens, cubes = [], []
        for k, sep in enumerate(separations(e, step)):
            y = sep[0] * sep[0] + sep[1] * sep[1] + sep[2] * sep[2]
            c = jnp.maximum(tops[k] - y, 0.0)
            square = c * c
            cube = square * c
            dens.append(cube * (c + f32(dens_shift)))
            cubes.append(cube)
            for axis in range(3):
                seps[e, k, axis] = sep[axis]
            slopes[e, k, 0] = square * (c + f32(pair_slope_shift))
            slopes[e, k, 1] = square * (c + f32(dens_slope_shift))
        cross = (dens[0] + dens[1]) + (dens[2] + dens[3])
        inside = dens[4] + dens[5]
        rho[e] = rho_part + cross
        back[0, e + 1] = dens[1] + dens[4]
        back[1, e + 1] = dens[2] + dens[5]
        back[2, e + 1] = dens[3]
        weight = jnp.where((e >= 1) & (e <= planes), 1.0, 0.0).astype(f32)
        sum_f = sum_f + weight * (cross + inside)
        sum_c = sum_c + weight * (
            ((cubes[0] + cubes[1]) + (cubes[2] + cubes[3])) + (cubes[4] + cubes[5])
        )
        return (dens[0] + inside, sum_f, sum_c)

    down = limits(-1, site_u, site_v)
    up = limits(1, site_u, site_v)

    def density_pair(t, carry):
        carry = density(2 * t, -1, down, carry)
        return density(2 * t + 1, 1, up, carry)

    carry = lax.fori_loop(0, planes // 2 + 1, density_pair, (zero, zero, zero))
    _, sum_f, sum_c = density(planes + 2, -1, down, carry)

    def embedding(q, side):
        total = rho[q] + gather_back(back[0, q], back[1, q], back[2, q], side, lanes)
        w = 1.0 + f32(dens_scale) * total
        inv = lax.rsqrt(w)
        embed[0, q] = f32(-0.5 * embed_scale * slope_ratio) * inv
        return w * inv - f32(bulk_root)

    embedding(1, side_of(1))
    embedding(planes + HALO, side_of(0))

    def embed_some(t, total):
        for j in range(EMBED_UNROLL):
            total = total + embedding(HALO + t * EMBED_UNROLL + j, side_of(j))
        return total

    roots = lax.fori_loop(0, planes // EMBED_UNROLL, embed_some, zero)
    energy_ref[...] = f32(-embed_scale) * roots + f32(pair_energy_scale) * (
        sum_f + f32(pair_shift - dens_shift) * sum_c
    )

    def see(q, side):
        for k, seen in enumerate(partners(embed[0, q], side, lanes)):
            embed[1 + k, q] = seen

    see(planes + HALO, side_of(0))

    def see_some(t, carry):
        for j in range(EMBED_UNROLL):
            see(HALO + t * EMBED_UNROLL + j, side_of(j))
        return carry

    lax.fori_loop(0, planes // EMBED_UNROLL, see_some, 0)

    def force(e, keep, carry):
        own = embed[0, e]
        nxt = embed[0, e + 1]
        at_v, at_u, at_uv = [embed[1 + k, e + 1] for k in range(3)]
        partner = (own + nxt, own + at_v, own + at_u, own + at_uv, nxt + at_v, nxt + at_u)
        weight = [slopes[e, k, 0] + partner[k] * slopes[e, k, 1] for k in range(6)]
        out = []
        for axis in range(3):
            g = [weight[k] * seps[e, k, axis] for k in range(6)]
            if keep:
                force_ref[axis, e - HALO] = carry[axis] + ((g[0] + g[1]) + (g[2] + g[3]))
            force_back[axis, 0, e + 1] = g[1] + g[4]
            force_back[axis, 1, e + 1] = g[2] + g[5]
            force_back[axis, 2, e + 1] = g[3]
            out.append((g[4] + g[5]) - g[0])
        return tuple(out)

    def force_pair(t, carry):
        carry = force(HALO + 2 * t, True, carry)
        return force(HALO + 2 * t + 1, True, carry)

    lax.fori_loop(0, planes // 2, force_pair, force(1, False, (zero, zero, zero)))

    def finish(t, carry):
        for j in range(FINISH_UNROLL):
            p = t * FINISH_UNROLL + j
            for axis in range(3):
                parts = [force_back[axis, k, p + HALO] for k in range(3)]
                force_ref[axis, p] = f32(force_scale) * (
                    force_ref[axis, p] - gather_back(*parts, side_of(j), lanes)
                )
        return carry

    lax.fori_loop(0, planes // FINISH_UNROLL, finish, 0)


def image_forces(side, planes, sources):
    arrays, slots, starts = zip(*sources)
    vmem = pl.BlockSpec(memory_space=pltpu.VMEM)
    rows = planes + 2 * HALO
    return pl.pallas_call(
        functools.partial(force_kernel, starts, slots),
        out_shape=(
            jax.ShapeDtypeStruct((3, planes, 8, 128), jnp.float32),
            jax.ShapeDtypeStruct((8, 128), jnp.float32),
        ),
        in_specs=[pl.BlockSpec(memory_space=pltpu.SMEM)] + [vmem] * len(arrays),
        out_specs=(vmem, vmem),
        scratch_shapes=[
            pltpu.VMEM((3, rows, 8, 128), jnp.float32),
            pltpu.VMEM((3, 3, rows, 8, 128), jnp.float32),
            pltpu.VMEM((rows, 6, 3, 8, 128), jnp.float32),
            pltpu.VMEM((rows, 6, 2, 8, 128), jnp.float32),
            pltpu.VMEM((rows, 8, 128), jnp.float32),
            pltpu.VMEM((3, rows, 8, 128), jnp.float32),
            pltpu.VMEM((4, rows, 8, 128), jnp.float32),
            pltpu.VMEM((3, 3, rows, 8, 128), jnp.float32),
        ],
        compiler_params=pltpu.CompilerParams(vmem_limit_bytes=40 * 1024 * 1024),
        cost_estimate=pl.CostEstimate(
            flops=20_000_000, bytes_accessed=15_000_000, transcendentals=0
        ),
        name="slab_forces",
    )(side, *arrays)


def total_of(tile):
    return jnp.sum(jnp.sum(tile, axis=0, keepdims=True), axis=1, keepdims=True)


def piece_of(pieces, region):
    rows = sum(piece.shape[1] for piece in pieces) // REGIONS
    at = region * rows
    for piece in pieces:
        if at < piece.shape[1]:
            return piece, at, rows
        at -= piece.shape[1]


def over_planes(body, rows, unroll, carry=0):
    def some(t, carry):
        for j in range(unroll):
            carry = body(t * unroll + j, carry)
        return carry

    return lax.fori_loop(0, rows // unroll, some, carry)


def groups(refs, counts):
    out, at = [], 0
    for count in counts:
        out.append(refs[at : at + count])
        at += count
    return out, refs[at:]


def moment_kernel(counts, side_ref, *refs):
    path, refs = groups(refs, counts)
    forces, speeds, energies, out_ref = refs[:2], refs[2:4], refs[4:6], refs[6]
    zero = jnp.zeros((8, 128), jnp.float32)
    sums = (zero,) * 14
    for region in range(REGIONS):
        held = [piece_of(pieces, region) for pieces in path]
        rows = held[0][2]

        def one(p, carry):
            carry = list(carry)
            for axis in range(3):
                at = [ref[axis, start + p] for ref, start, _ in held]
                diff = [at[j + 1] - at[j] for j in range(3)]
                square = [d * d for d in diff]
                for j in range(2):
                    force = forces[j][axis, region * rows + p]
                    speed = speeds[j][axis, region * rows + p]
                    terms = (
                        force * force,
                        force * diff[j + 1],
                        force * diff[j],
                        square[j + 1],
                        square[j],
                        diff[j] * diff[j + 1],
                        speed * speed,
                    )
                    for k, term in enumerate(terms):
                        carry[7 * j + k] = carry[7 * j + k] + term
            return tuple(carry)

        sums = over_planes(one, rows, 2, sums)

    lane = lax.broadcasted_iota(jnp.int32, (1, 128), 1)
    odd = side_ref[0] == 1
    sign = jnp.where(odd, -1.0, 1.0).astype(jnp.float32)
    row = jnp.zeros((1, 128), jnp.float32)
    for j in range(2):
        ahead = [total_of(sums[7 * j + k]) for k in range(7)]
        values = (
            total_of(energies[j][...]),
            ahead[0],
            sign * jnp.where(odd, ahead[2], ahead[1]),
            sign * jnp.where(odd, ahead[1], ahead[2]),
            jnp.where(odd, ahead[4], ahead[3]),
            jnp.where(odd, ahead[3], ahead[4]),
            ahead[5],
            ahead[6],
        )
        for k, value in enumerate(values):
            row = row + jnp.where(lane == 8 * j + k, value, 0.0)
    out_ref[...] = jnp.broadcast_to(row, out_ref.shape)


VMEM = pl.BlockSpec(memory_space=pltpu.VMEM)
SMEM = pl.BlockSpec(memory_space=pltpu.SMEM)
PARAMS = pltpu.CompilerParams(vmem_limit_bytes=32 * 1024 * 1024)


def moments(side, path, forces, speeds, energies, copies):
    counts = [len(pieces) for pieces in path]
    arrays = [piece for pieces in path for piece in pieces] + [*forces, *speeds, *energies]
    return pl.pallas_call(
        functools.partial(moment_kernel, counts),
        out_shape=jax.ShapeDtypeStruct((copies, 128), jnp.float32),
        in_specs=[SMEM] + [VMEM] * len(arrays),
        out_specs=VMEM,
        compiler_params=PARAMS,
        name="path_moments",
    )(side, *arrays)


def path_terms(summary, images):
    lane = lax.broadcasted_iota(jnp.int32, (8, 128), 1)
    image = lax.broadcasted_iota(jnp.int32, (8, 128), 0)

    def column(k):
        picked = jnp.sum(jnp.where(lane == k, summary, 0.0), axis=1, keepdims=True)
        return jnp.broadcast_to(picked, (8, 128))

    e_here, ff, f_fwd, f_bwd, fwd_sq, bwd_sq, fwd_bwd, speed_sq = [column(k) for k in range(8)]
    e_prev = pltpu.roll(e_here, 1, 0)
    e_next = pltpu.roll(e_here, 7, 0)
    inner = (image > 0) & (image < images - 1)
    rise = e_next - e_here
    fall = e_here - e_prev
    larger = jnp.maximum(jnp.abs(rise), jnp.abs(fall))
    smaller = jnp.minimum(jnp.abs(rise), jnp.abs(fall))
    upward = (e_next > e_here) & (e_here > e_prev)
    downward = (e_next < e_here) & (e_here < e_prev)
    toward = e_next > e_prev
    weight_fwd = jnp.where(
        upward, 1.0, jnp.where(downward, 0.0, jnp.where(toward, larger, smaller))
    )
    weight_bwd = jnp.where(
        upward, 0.0, jnp.where(downward, 1.0, jnp.where(toward, smaller, larger))
    )
    tangent_sq = (
        weight_fwd * weight_fwd * fwd_sq
        + 2.0 * weight_fwd * weight_bwd * fwd_bwd
        + weight_bwd * weight_bwd * bwd_sq
    )
    norm_sq = tangent_sq + stabilizer
    force_tan = weight_fwd * f_fwd + weight_bwd * f_bwd
    spring = spring_const * (jnp.sqrt(fwd_sq + stabilizer) - jnp.sqrt(bwd_sq + stabilizer))
    coefficient = -force_tan / norm_sq + spring / jnp.sqrt(norm_sq)
    neb_sq = ff + 2.0 * coefficient * force_tan + coefficient * coefficient * tangent_sq

    def over_inner(value):
        return jnp.sum(jnp.where(inner, value, 0.0), axis=0, keepdims=True)

    force_norm = jnp.sqrt(over_inner(neb_sq) + stabilizer)
    speed_norm = jnp.sqrt(over_inner(speed_sq) + stabilizer)
    gain = jnp.broadcast_to(fire_mixing * (speed_norm / force_norm) + time_step, (8, 128))
    keep = jnp.where(inner, 1.0 - fire_mixing, 0.0)
    push = jnp.where(inner, gain, 0.0)
    along_fwd = jnp.where(inner, gain * coefficient * weight_fwd, 0.0)
    along_bwd = jnp.where(inner, gain * coefficient * weight_bwd, 0.0)
    return keep, push, along_fwd, along_bwd


def step_terms(image_ref, gathered_ref, images, terms):
    image = lax.broadcasted_iota(jnp.int32, (8, 128), 0)
    summary = jnp.zeros((8, 128), jnp.float32)
    slabs = gathered_ref.shape[0] // images
    for g in range(images):
        rows = gathered_ref[g * slabs : (g + 1) * slabs, :]
        row = jnp.broadcast_to(jnp.sum(rows, axis=0, keepdims=True), (8, 128))
        summary = summary + jnp.where(image == g, row, 0.0)
        summary = summary + jnp.where(image == (g ^ 1), pltpu.roll(row, 120, 1), 0.0)
    keep, push, along_fwd, along_bwd = path_terms(summary, images)
    here = image_ref[0]
    odd = here % 2 == 1
    values = (keep, push, jnp.where(odd, -along_bwd, along_fwd), jnp.where(odd, -along_fwd, along_bwd))
    for j in range(2):
        at = image == (here + j * (1 - 2 * (here % 2)))
        for k, value in enumerate(values):
            own = jnp.sum(jnp.where(at, value, 0.0), axis=0, keepdims=True)
            terms[j, k] = jnp.broadcast_to(own, (8, 128))


def new_speed(terms, j, speed, force, ahead, behind):
    return terms[j, 0] * speed + terms[j, 1] * force + terms[j, 2] * ahead + terms[j, 3] * behind


def update_kernel(counts, images, image_ref, gathered_ref, *refs):
    path, refs = groups(refs, counts)
    forces, speeds, moved, new_speeds = refs[:2], refs[2:4], refs[4:6], refs[6:8]
    tops, bottoms, terms = refs[8:11]
    step_terms(image_ref, gathered_ref, images, terms)
    for region in range(REGIONS):
        held = [piece_of(pieces, region) for pieces in path]
        rows = held[0][2]

        def one(p, carry):
            for axis in range(3):
                at = [ref[axis, start + p] for ref, start, _ in held]
                diff = [at[j + 1] - at[j] for j in range(3)]
                for j in range(2):
                    q = region * rows + p
                    speed = new_speed(terms, j, speeds[j][axis, q], forces[j][axis, q], diff[j + 1], diff[j])
                    new_speeds[j][axis, q] = speed
                    moved[j][axis, q] = at[j + 1] + time_step * speed
            return carry

        over_planes(one, rows, 2)
    planes = moved[0].shape[1]
    for j in range(2):
        tops[j] = moved[j][:, planes - HALO :]
        bottoms[j] = moved[j][:, :HALO]


def update(image, gathered, path, forces, speeds, images):
    counts = [len(pieces) for pieces in path]
    arrays = [piece for pieces in path for piece in pieces] + [*forces, *speeds]
    out = jax.ShapeDtypeStruct(forces[0].shape, jnp.float32)
    edge = jax.ShapeDtypeStruct((2, 3, HALO, 8, 128), jnp.float32)
    results = pl.pallas_call(
        functools.partial(update_kernel, counts, images),
        out_shape=(out,) * 4 + (edge,) * 2,
        in_specs=[SMEM] + [VMEM] * (1 + len(arrays)),
        out_specs=(VMEM,) * 6,
        scratch_shapes=[pltpu.VMEM((2, 4, 8, 128), jnp.float32)],
        compiler_params=PARAMS,
        name="fire_update",
    )(image, gathered, *arrays)
    return results[:2], results[2:4], results[4], results[5]


def last_partner_kernel(images, image_ref, gathered_ref, before, here, after, force, speed, *outs):
    parts, terms_ref = outs[:-1], outs[-1]
    step_terms(image_ref, gathered_ref, images, terms_ref)
    for region, part in enumerate(parts):
        rows = part.shape[1]

        def one(p, carry):
            q = region * rows + p
            for axis in range(3):
                at = here[axis, q]
                part[axis, p] = new_speed(
                    terms_ref, 1, speed[axis, q], force[axis, q], after[axis, q] - at, at - before[axis, q]
                )
            return carry

        over_planes(one, rows, 2)


def last_partner(image, gathered, path, force, speed, images):
    part = jax.ShapeDtypeStruct((3, force.shape[1] // REGIONS, 8, 128), jnp.float32)
    return pl.pallas_call(
        functools.partial(last_partner_kernel, images),
        out_shape=(part,) * REGIONS + (jax.ShapeDtypeStruct((2, 4, 8, 128), jnp.float32),),
        in_specs=[SMEM] + [VMEM] * 6,
        out_specs=(VMEM,) * (REGIONS + 1),
        compiler_params=PARAMS,
        name="last_partner",
    )(image, gathered, *path, force, speed)


def last_own_kernel(side_ref, terms, before, here, after, force, speed, moved, new_ref):
    def one(p, carry):
        for axis in range(3):
            at = here[axis, p]
            new = new_speed(
                terms, 0, speed[axis, p], force[axis, p], after[axis, p] - at, at - before[axis, p]
            )
            new_ref[axis, p] = new
            moved[axis, p] = at + time_step * new
        return carry

    over_planes(one, here.shape[1], 2)


def last_own(side, terms, path, force, speed):
    planes = force.shape[1]
    chunk = planes // REGIONS
    block = pl.BlockSpec((3, chunk, 8, 128), lambda t, side_ref: (0, t, 0, 0))
    half = pl.BlockSpec((3, chunk, 8, 128), lambda t, side_ref: (0, side_ref[0] * REGIONS + t, 0, 0))
    out = jax.ShapeDtypeStruct((3, 2 * planes, 8, 128), jnp.float32)
    return pl.pallas_call(
        last_own_kernel,
        grid_spec=pltpu.PrefetchScalarGridSpec(
            num_scalar_prefetch=1,
            grid=(REGIONS,),
            in_specs=[pl.BlockSpec((2, 4, 8, 128), lambda t, side_ref: (0, 0, 0, 0))] + [block] * 5,
            out_specs=(half, half),
        ),
        out_shape=(out, out),
        compiler_params=PARAMS,
        name="last_own",
    )(side, terms, *path, force, speed)


def last_join_kernel(side_ref, here, speed, moved_in, speed_in, moved, new_ref):
    def one(p, carry):
        for axis in range(3):
            new = speed[axis, p]
            new_ref[axis, p] = new
            moved[axis, p] = here[axis, p] + time_step * new
        return carry

    over_planes(one, speed.shape[1], 4)


def last_join(side, region, here, speed, moved, speeds):
    rows = speed.shape[1]
    chunk = rows // JOIN_STEPS
    first = region * JOIN_STEPS
    block = pl.BlockSpec((3, chunk, 8, 128), lambda t, side_ref: (0, t, 0, 0))
    here_block = pl.BlockSpec((3, chunk, 8, 128), lambda t, side_ref: (0, first + t, 0, 0))
    half = pl.BlockSpec(
        (3, chunk, 8, 128),
        lambda t, side_ref: (0, (1 - side_ref[0]) * REGIONS * JOIN_STEPS + first + t, 0, 0),
    )
    out = jax.ShapeDtypeStruct(moved.shape, jnp.float32)
    whole = pl.BlockSpec(memory_space=pl.ANY)
    return pl.pallas_call(
        last_join_kernel,
        grid_spec=pltpu.PrefetchScalarGridSpec(
            num_scalar_prefetch=1,
            grid=(JOIN_STEPS,),
            in_specs=[here_block, block, whole, whole],
            out_specs=(half, half),
        ),
        out_shape=(out, out),
        input_output_aliases={3: 0, 4: 1},
        compiler_params=PARAMS,
        name="last_join",
    )(side, here, speed, moved, speeds)


def cut_kernel(starts, side_ref, *refs):
    count = len(starts)
    source, outs, sems = refs[0], refs[1 : 1 + count], refs[1 + count]
    copies = []
    for k, out in enumerate(outs):
        rows = source.at[:, pl.ds(at_side(starts[k], side_ref), out.shape[1])]
        copies.append(pltpu.make_async_copy(rows, out, sems.at[k]))
    for copy in copies:
        copy.start()
    for copy in copies:
        copy.wait()


def at_side(pair, side_ref):
    even, odd = pair
    return even if even == odd else even + (odd - even) * side_ref[0]


def cut(side, array, starts, sizes):
    count = len(sizes)
    return pl.pallas_call(
        functools.partial(cut_kernel, starts),
        out_shape=tuple(jax.ShapeDtypeStruct((3, size, 8, 128), jnp.float32) for size in sizes),
        in_specs=[SMEM, pl.BlockSpec(memory_space=pltpu.HBM)],
        out_specs=(VMEM,) * count,
        scratch_shapes=[pltpu.SemaphoreType.DMA((count,))],
        compiler_params=PARAMS,
        name="cut",
    )(side, array)


def local(displacement, velocity):
    planes = displacement.shape[2] // (SIDE * SIDE)
    half = planes // 2
    images, slabs = lax.axis_size("image"), lax.axis_size("domain")
    both = ("image", "domain")
    own_image = lax.axis_index("image").astype(jnp.int32)
    side = own_image % 2
    image_arg, side_arg = own_image.reshape(1), side.reshape(1)
    slab = displacement.reshape(3, planes, 8, 128)
    slab_speed = velocity.reshape(3, planes, 8, 128)

    def at(image, domain):
        return image * slabs + domain % slabs

    everyone = [(i, d) for i in range(images) for d in range(slabs)]
    outer_own = [(at(i, d), at(i, d + 1 - 2 * (i % 2))) for i, d in everyone]
    outer_partner = [(at(i, d), at(i ^ 1, d - 1 + 2 * (i % 2))) for i, d in everyone]
    across = [(i, i ^ 1) for i in range(images)]
    own_out = [(i, i - 2 + 4 * (i % 2)) for i in range(images)]
    own_out = [(a, b) for a, b in own_out if 0 <= b < images]
    partner_out = [(b, a) for a, b in own_out]
    upward = [(at(i, d), at(i ^ 1, d + i % 2)) for i, d in everyone]
    downward = [(b, a) for a, b in upward]

    end, top = planes - HALO, half + HALO
    piece = half // REGIONS
    edge_own, edge_partner, edge_inner, near_inner, own, *far_pieces = cut(
        side_arg,
        slab,
        ((end, 0), (0, end), (half - HALO, half), (half, half - HALO), (0, half))
        + tuple((half + c * piece, c * piece) for c in range(REGIONS)),
        (HALO,) * 4 + (half,) + (piece,) * REGIONS,
    )
    halo_own = lax.ppermute(edge_own, both, outer_own)
    halo_partner = lax.ppermute(edge_partner, both, outer_partner)
    halo_inner = lax.ppermute(edge_inner, "image", across)
    *far_pieces, halo_own, halo_partner, halo_inner = lax.optimization_barrier(
        (*far_pieces, halo_own, halo_partner, halo_inner)
    )
    partner = [lax.ppermute(part, "image", across) for part in far_pieces]
    beyond_own = lax.ppermute(own, "image", own_out)
    outer, inner = (0, top), (top, 0)
    own_force, own_energy = image_forces(
        side_arg,
        half,
        ((own, None, (HALO, HALO)), (halo_own, None, outer), (near_inner, None, inner)),
    )
    own_speed, far_speed = cut(side_arg, slab_speed, ((0, half), (half, 0)), (half, half))
    far_speed, _ = lax.optimization_barrier((far_speed, own_energy))
    *partner[1:], _ = lax.optimization_barrier((*partner[1:], own_energy))
    beyond_partner = [lax.ppermute(part, "image", partner_out) for part in partner]
    halo_inner, beyond_partner[0] = lax.optimization_barrier((halo_inner, beyond_partner[0]))
    partner_speed = lax.ppermute(far_speed, "image", across)

    partner_sources = tuple(
        (part, None, (HALO + c * piece,) * 2) for c, part in enumerate(partner)
    ) + ((halo_partner, None, outer), (halo_inner, None, inner))
    path = (beyond_partner, [own], partner, [beyond_own])
    speeds = (own_speed, partner_speed)
    results = [(own_force, own_energy), image_forces(side_arg, half, partner_sources)]
    for step_index in range(FIRE_STEPS):
        if step_index > 0:
            results = [image_forces(side_arg, half, held) for held in sources]
        forces, energies = zip(*results)
        payload = moments(side_arg, path, forces, speeds, energies, images * slabs)
        gathered = lax.all_to_all(payload, both, 0, 0, tiled=True)
        if step_index == FIRE_STEPS - 1:
            break
        moved, speeds, tops, bottoms = update(image_arg, gathered, path, forces, speeds, images)
        low = lax.ppermute(tops, both, upward)
        high = lax.ppermute(bottoms, both, downward)
        sources = [
            (
                (moved[j], None, (HALO, HALO)),
                (low, 1 - j, (0, 0)),
                (high, 1 - j, (top, top)),
            )
            for j in range(2)
        ]
        path = (
            [lax.ppermute(moved[1], "image", partner_out)],
            [moved[0]],
            [moved[1]],
            [lax.ppermute(moved[0], "image", own_out)],
        )
        back_home, _ = lax.optimization_barrier((moved[1], low))
        returned = lax.ppermute(back_home, "image", across)
    whole = [pieces[0] for pieces in path]
    *last_speeds, terms = last_partner(
        image_arg, gathered, whole[1:], forces[1], speeds[1], images
    )
    last_speeds = [lax.ppermute(part, "image", across) for part in last_speeds]
    moved, new_speeds = last_own(side_arg, terms, whole[:3], forces[0], speeds[0])
    for region, part in enumerate(last_speeds):
        moved, new_speeds = last_join(side_arg, region, returned, part, moved, new_speeds)
    return (moved.reshape(displacement.shape), new_speeds.reshape(velocity.shape))


def solution(mesh):
    spec = P("image", None, "domain")
    return jax.shard_map(
        local,
        mesh=mesh,
        in_specs=(spec, spec),
        out_specs=(spec, spec),
        check_vma=False,
    )
```

```python
import functools
import math

import jax
import jax.numpy as jnp
from jax import lax
from jax.experimental import pallas as pl
from jax.experimental.pallas import tpu as pltpu
from jax.sharding import PartitionSpec as P

SIDE = 32
FIRE_STEPS = 2
QUANTITIES = 8
HALO = 2
PLACE_UNROLL = 16
EMBED_UNROLL = 48
FINISH_UNROLL = 16
REGIONS = 2
JOIN_STEPS = 2

lattice_const = 3.615
cutoff_sq = 9.61
nearest_sq = 6.533136
pair_scale = 30.0
pair_depth = 0.3
embed_scale = 1.2
bulk_root = 3.605551275463989
spring_const = 2.0
time_step = 0.1
fire_mixing = 0.1
stabilizer = 1e-06

reach_root = math.sqrt(cutoff_sq)
unit_half = 0.5 * lattice_const / reach_root
kappa = cutoff_sq / nearest_sq
dens_shift = (2.0 - kappa) / kappa
pair_shift = (2.5 - 2.0 * kappa) / (2.0 * kappa)
dens_scale = pair_scale * kappa
pair_energy_scale = pair_scale * pair_depth * 2.0 * kappa
dens_slope_shift = 0.75 * dens_shift
pair_slope_shift = 0.75 * pair_shift
dens_slope_scale = -4.0 * dens_scale / cutoff_sq
pair_slope_scale = -4.0 * pair_energy_scale / cutoff_sq
slope_ratio = dens_slope_scale / pair_slope_scale
force_scale = 2.0 * pair_slope_scale * reach_root


def shift(field, step_u, step_v, lanes):
    reach = step_u * SIDE + step_v
    turned = pltpu.roll(field, (-reach) % 128, 1)
    if step_u == 0:
        return turned
    carried = pltpu.roll(turned, (-step_u) % 8, 0)
    return jnp.where(lanes >= 128 - reach if reach > 0 else lanes < -reach, carried, turned)


def partners(field, step, lanes):
    return (
        shift(field, 0, step, lanes),
        shift(field, step, 0, lanes),
        shift(field, step, step, lanes),
    )


def gather_back(at_v, at_u, at_uv, step, lanes):
    return (
        shift(at_v, 0, -step, lanes)
        + shift(at_u, -step, 0, lanes)
        + shift(at_uv, -step, -step, lanes)
    )


def limits(step, u, v):
    far = jnp.float32(-1e30)
    in_u = (u + step >= 0) & (u + step < SIDE)
    in_v = (v + step >= 0) & (v + step < SIDE)
    one = jnp.ones_like(u, jnp.float32)
    return (
        jnp.where(in_v, one, far),
        jnp.where(in_u, one, far),
        jnp.where(in_u & in_v, one, far),
    )


def side_of(plane):
    return 1 if plane % 2 == 0 else -1


def force_kernel(starts, slots, side_ref, *refs):
    count = len(starts)
    sources = [ref if slot is None else ref.at[slot] for ref, slot in zip(refs, slots)]
    force_ref, energy_ref, pos, turned, seps, slopes, rho, back, embed, force_back = refs[count:]
    f32 = jnp.float32
    planes = force_ref.shape[1]
    lanes = lax.broadcasted_iota(jnp.int32, (8, 128), 1)
    subl = lax.broadcasted_iota(jnp.int32, (8, 128), 0)
    site_u = subl * 4 + lanes // SIDE
    site_v = lanes % SIDE
    inverse = f32(1.0 / reach_root)
    zero = jnp.zeros((8, 128), f32)

    def place(q, side, values):
        for axis in range(3):
            value = values[axis] * inverse
            pos[axis, q] = value
            for k, seen in enumerate(partners(value, side, lanes)):
                turned[axis, k, q] = seen

    for k, source in enumerate(sources):
        rows = source.shape[1]
        unroll = rows if rows <= 24 else PLACE_UNROLL

        def place_some(t, carry, source=source, start=at_side(starts[k], side_ref), unroll=unroll):
            for j in range(unroll):
                p = t * unroll + j
                place(start + p, side_of(j), [source[axis, p] for axis in range(3)])
            return carry

        lax.fori_loop(0, rows // unroll, place_some, 0)

    def separations(e, step):
        h = f32(unit_half)
        sh = f32(step * unit_half)
        own = [pos[axis, e] for axis in range(3)]
        nxt = [pos[axis, e + 1] for axis in range(3)]
        seen = [[turned[axis, k, e + 1] for k in range(3)] for axis in range(3)]
        own_x = own[0] - h
        y_of = (own[1] + sh, own[1], own[1] - sh)
        z_of = (own[2] - sh, own[2], own[2] + sh)
        cross = [
            (nxt[0] - own_x, nxt[1] - y_of[0], nxt[2] - z_of[1]),
            (seen[0][0] - own_x, seen[1][0] - y_of[1], seen[2][0] - z_of[2]),
            (seen[0][1] - own_x, seen[1][1] - y_of[1], seen[2][1] - z_of[0]),
            (seen[0][2] - own_x, seen[1][2] - y_of[2], seen[2][2] - z_of[1]),
        ]
        near_y = nxt[1] - sh
        near_zv = nxt[2] + sh
        near_zu = nxt[2] - sh
        inside = [
            (seen[0][0] - nxt[0], seen[1][0] - near_y, seen[2][0] - near_zv),
            (seen[0][1] - nxt[0], seen[1][1] - near_y, seen[2][1] - near_zu),
        ]
        return cross + inside

    def density(e, step, bounds, carry):
        rho_part, sum_f, sum_c = carry
        one = jnp.ones((8, 128), f32)
        tops = (one, bounds[0], bounds[1], bounds[2], bounds[0], bounds[1])
        dens, cubes = [], []
        for k, sep in enumerate(separations(e, step)):
            y = sep[0] * sep[0] + sep[1] * sep[1] + sep[2] * sep[2]
            c = jnp.maximum(tops[k] - y, 0.0)
            square = c * c
            cube = square * c
            dens.append(cube * (c + f32(dens_shift)))
            cubes.append(cube)
            for axis in range(3):
                seps[e, k, axis] = sep[axis]
            slopes[e, k, 0] = square * (c + f32(pair_slope_shift))
            slopes[e, k, 1] = square * (c + f32(dens_slope_shift))
        cross = (dens[0] + dens[1]) + (dens[2] + dens[3])
        inside = dens[4] + dens[5]
        rho[e] = rho_part + cross
        back[0, e + 1] = dens[1] + dens[4]
        back[1, e + 1] = dens[2] + dens[5]
        back[2, e + 1] = dens[3]
        weight = jnp.where((e >= 1) & (e <= planes), 1.0, 0.0).astype(f32)
        sum_f = sum_f + weight * (cross + inside)
        sum_c = sum_c + weight * (
            ((cubes[0] + cubes[1]) + (cubes[2] + cubes[3])) + (cubes[4] + cubes[5])
        )
        return (dens[0] + inside, sum_f, sum_c)

    down = limits(-1, site_u, site_v)
    up = limits(1, site_u, site_v)

    def density_pair(t, carry):
        carry = density(2 * t, -1, down, carry)
        return density(2 * t + 1, 1, up, carry)

    carry = lax.fori_loop(0, planes // 2 + 1, density_pair, (zero, zero, zero))
    _, sum_f, sum_c = density(planes + 2, -1, down, carry)

    def embedding(q, side):
        total = rho[q] + gather_back(back[0, q], back[1, q], back[2, q], side, lanes)
        w = 1.0 + f32(dens_scale) * total
        inv = lax.rsqrt(w)
        embed[0, q] = f32(-0.5 * embed_scale * slope_ratio) * inv
        return w * inv - f32(bulk_root)

    embedding(1, side_of(1))
    embedding(planes + HALO, side_of(0))

    def embed_some(t, total):
        for j in range(EMBED_UNROLL):
            total = total + embedding(HALO + t * EMBED_UNROLL + j, side_of(j))
        return total

    roots = lax.fori_loop(0, planes // EMBED_UNROLL, embed_some, zero)
    energy_ref[...] = f32(-embed_scale) * roots + f32(pair_energy_scale) * (
        sum_f + f32(pair_shift - dens_shift) * sum_c
    )

    def see(q, side):
        for k, seen in enumerate(partners(embed[0, q], side, lanes)):
            embed[1 + k, q] = seen

    see(planes + HALO, side_of(0))

    def see_some(t, carry):
        for j in range(EMBED_UNROLL):
            see(HALO + t * EMBED_UNROLL + j, side_of(j))
        return carry

    lax.fori_loop(0, planes // EMBED_UNROLL, see_some, 0)

    def force(e, keep, carry):
        own = embed[0, e]
        nxt = embed[0, e + 1]
        at_v, at_u, at_uv = [embed[1 + k, e + 1] for k in range(3)]
        partner = (own + nxt, own + at_v, own + at_u, own + at_uv, nxt + at_v, nxt + at_u)
        weight = [slopes[e, k, 0] + partner[k] * slopes[e, k, 1] for k in range(6)]
        out = []
        for axis in range(3):
            g = [weight[k] * seps[e, k, axis] for k in range(6)]
            if keep:
                force_ref[axis, e - HALO] = carry[axis] + ((g[0] + g[1]) + (g[2] + g[3]))
            force_back[axis, 0, e + 1] = g[1] + g[4]
            force_back[axis, 1, e + 1] = g[2] + g[5]
            force_back[axis, 2, e + 1] = g[3]
            out.append((g[4] + g[5]) - g[0])
        return tuple(out)

    def force_pair(t, carry):
        carry = force(HALO + 2 * t, True, carry)
        return force(HALO + 2 * t + 1, True, carry)

    lax.fori_loop(0, planes // 2, force_pair, force(1, False, (zero, zero, zero)))

    def finish(t, carry):
        for j in range(FINISH_UNROLL):
            p = t * FINISH_UNROLL + j
            for axis in range(3):
                parts = [force_back[axis, k, p + HALO] for k in range(3)]
                force_ref[axis, p] = f32(force_scale) * (
                    force_ref[axis, p] - gather_back(*parts, side_of(j), lanes)
                )
        return carry

    lax.fori_loop(0, planes // FINISH_UNROLL, finish, 0)


def image_forces(side, planes, sources):
    arrays, slots, starts = zip(*sources)
    vmem = pl.BlockSpec(memory_space=pltpu.VMEM)
    rows = planes + 2 * HALO
    return pl.pallas_call(
        functools.partial(force_kernel, starts, slots),
        out_shape=(
            jax.ShapeDtypeStruct((3, planes, 8, 128), jnp.float32),
            jax.ShapeDtypeStruct((8, 128), jnp.float32),
        ),
        in_specs=[pl.BlockSpec(memory_space=pltpu.SMEM)] + [vmem] * len(arrays),
        out_specs=(vmem, vmem),
        scratch_shapes=[
            pltpu.VMEM((3, rows, 8, 128), jnp.float32),
            pltpu.VMEM((3, 3, rows, 8, 128), jnp.float32),
            pltpu.VMEM((rows, 6, 3, 8, 128), jnp.float32),
            pltpu.VMEM((rows, 6, 2, 8, 128), jnp.float32),
            pltpu.VMEM((rows, 8, 128), jnp.float32),
            pltpu.VMEM((3, rows, 8, 128), jnp.float32),
            pltpu.VMEM((4, rows, 8, 128), jnp.float32),
            pltpu.VMEM((3, 3, rows, 8, 128), jnp.float32),
        ],
        compiler_params=pltpu.CompilerParams(vmem_limit_bytes=40 * 1024 * 1024),
        cost_estimate=pl.CostEstimate(
            flops=20_000_000, bytes_accessed=15_000_000, transcendentals=0
        ),
        name="slab_forces",
    )(side, *arrays)


def total_of(tile):
    return jnp.sum(jnp.sum(tile, axis=0, keepdims=True), axis=1, keepdims=True)


def piece_of(pieces, region):
    rows = sum(piece.shape[1] for piece in pieces) // REGIONS
    at = region * rows
    for piece in pieces:
        if at < piece.shape[1]:
            return piece, at, rows
        at -= piece.shape[1]


def over_planes(body, rows, unroll, carry=0):
    def some(t, carry):
        for j in range(unroll):
            carry = body(t * unroll + j, carry)
        return carry

    return lax.fori_loop(0, rows // unroll, some, carry)


def groups(refs, counts):
    out, at = [], 0
    for count in counts:
        out.append(refs[at : at + count])
        at += count
    return out, refs[at:]


def moment_kernel(counts, side_ref, *refs):
    path, refs = groups(refs, counts)
    forces, energies, speed_sq, out_ref = refs[:2], refs[2:4], refs[4:6], refs[6]
    zero = jnp.zeros((8, 128), jnp.float32)
    sums = (zero,) * 12
    for region in range(REGIONS):
        held = [piece_of(pieces, region) for pieces in path]
        rows = held[0][2]

        def one(p, carry):
            carry = list(carry)
            for axis in range(3):
                at = [ref[axis, start + p] for ref, start, _ in held]
                diff = [at[j + 1] - at[j] for j in range(3)]
                square = [d * d for d in diff]
                for j in range(2):
                    force = forces[j][axis, region * rows + p]
                    terms = (
                        force * force,
                        force * diff[j + 1],
                        force * diff[j],
                        square[j + 1],
                        square[j],
                        diff[j] * diff[j + 1],
                    )
                    for k, term in enumerate(terms):
                        carry[6 * j + k] = carry[6 * j + k] + term
            return tuple(carry)

        sums = over_planes(one, rows, 2, sums)

    lane = lax.broadcasted_iota(jnp.int32, (1, 128), 1)
    odd = side_ref[0] == 1
    sign = jnp.where(odd, -1.0, 1.0).astype(jnp.float32)
    row = jnp.zeros((1, 128), jnp.float32)
    for j in range(2):
        ahead = [total_of(sums[6 * j + k]) for k in range(6)]
        values = (
            total_of(energies[j][...]),
            ahead[0],
            sign * jnp.where(odd, ahead[2], ahead[1]),
            sign * jnp.where(odd, ahead[1], ahead[2]),
            jnp.where(odd, ahead[4], ahead[3]),
            jnp.where(odd, ahead[3], ahead[4]),
            ahead[5],
            total_of(speed_sq[j][...]),
        )
        for k, value in enumerate(values):
            row = row + jnp.where(lane == 8 * j + k, value, 0.0)
    out_ref[...] = jnp.broadcast_to(row, out_ref.shape)


VMEM = pl.BlockSpec(memory_space=pltpu.VMEM)
SMEM = pl.BlockSpec(memory_space=pltpu.SMEM)
PARAMS = pltpu.CompilerParams(vmem_limit_bytes=32 * 1024 * 1024)
TILE = jax.ShapeDtypeStruct((8, 128), jnp.float32)


def moments(side, path, forces, energies, speed_sq, copies):
    counts = [len(pieces) for pieces in path]
    arrays = [piece for pieces in path for piece in pieces] + [*forces, *energies, *speed_sq]
    return pl.pallas_call(
        functools.partial(moment_kernel, counts),
        out_shape=jax.ShapeDtypeStruct((copies, 128), jnp.float32),
        in_specs=[SMEM] + [VMEM] * len(arrays),
        out_specs=VMEM,
        compiler_params=PARAMS,
        name="path_moments",
    )(side, *arrays)


def path_terms(summary, images):
    lane = lax.broadcasted_iota(jnp.int32, (8, 128), 1)
    image = lax.broadcasted_iota(jnp.int32, (8, 128), 0)

    def column(k):
        picked = jnp.sum(jnp.where(lane == k, summary, 0.0), axis=1, keepdims=True)
        return jnp.broadcast_to(picked, (8, 128))

    e_here, ff, f_fwd, f_bwd, fwd_sq, bwd_sq, fwd_bwd, speed_sq = [column(k) for k in range(8)]
    e_prev = pltpu.roll(e_here, 1, 0)
    e_next = pltpu.roll(e_here, 7, 0)
    inner = (image > 0) & (image < images - 1)
    rise = e_next - e_here
    fall = e_here - e_prev
    larger = jnp.maximum(jnp.abs(rise), jnp.abs(fall))
    smaller = jnp.minimum(jnp.abs(rise), jnp.abs(fall))
    upward = (e_next > e_here) & (e_here > e_prev)
    downward = (e_next < e_here) & (e_here < e_prev)
    toward = e_next > e_prev
    weight_fwd = jnp.where(
        upward, 1.0, jnp.where(downward, 0.0, jnp.where(toward, larger, smaller))
    )
    weight_bwd = jnp.where(
        upward, 0.0, jnp.where(downward, 1.0, jnp.where(toward, smaller, larger))
    )
    tangent_sq = (
        weight_fwd * weight_fwd * fwd_sq
        + 2.0 * weight_fwd * weight_bwd * fwd_bwd
        + weight_bwd * weight_bwd * bwd_sq
    )
    norm_sq = tangent_sq + stabilizer
    force_tan = weight_fwd * f_fwd + weight_bwd * f_bwd
    spring = spring_const * (jnp.sqrt(fwd_sq + stabilizer) - jnp.sqrt(bwd_sq + stabilizer))
    coefficient = -force_tan / norm_sq + spring / jnp.sqrt(norm_sq)
    neb_sq = ff + 2.0 * coefficient * force_tan + coefficient * coefficient * tangent_sq

    def over_inner(value):
        return jnp.sum(jnp.where(inner, value, 0.0), axis=0, keepdims=True)

    force_norm = jnp.sqrt(over_inner(neb_sq) + stabilizer)
    speed_norm = jnp.sqrt(over_inner(speed_sq) + stabilizer)
    gain = jnp.broadcast_to(fire_mixing * (speed_norm / force_norm) + time_step, (8, 128))
    keep = jnp.where(inner, 1.0 - fire_mixing, 0.0)
    push = jnp.where(inner, gain, 0.0)
    along_fwd = jnp.where(inner, gain * coefficient * weight_fwd, 0.0)
    along_bwd = jnp.where(inner, gain * coefficient * weight_bwd, 0.0)
    return keep, push, along_fwd, along_bwd


def step_terms(image_ref, gathered_ref, images, terms):
    image = lax.broadcasted_iota(jnp.int32, (8, 128), 0)
    summary = jnp.zeros((8, 128), jnp.float32)
    slabs = gathered_ref.shape[0] // images
    for g in range(images):
        rows = gathered_ref[g * slabs : (g + 1) * slabs, :]
        row = jnp.broadcast_to(jnp.sum(rows, axis=0, keepdims=True), (8, 128))
        summary = summary + jnp.where(image == g, row, 0.0)
        summary = summary + jnp.where(image == (g ^ 1), pltpu.roll(row, 120, 1), 0.0)
    keep, push, along_fwd, along_bwd = path_terms(summary, images)
    here = image_ref[0]
    odd = here % 2 == 1
    values = (keep, push, jnp.where(odd, -along_bwd, along_fwd), jnp.where(odd, -along_fwd, along_bwd))
    for j in range(2):
        at = image == (here + j * (1 - 2 * (here % 2)))
        for k, value in enumerate(values):
            own = jnp.sum(jnp.where(at, value, 0.0), axis=0, keepdims=True)
            terms[j, k] = jnp.broadcast_to(own, (8, 128))


def new_speed(terms, j, speed, force, ahead, behind):
    return terms[j, 0] * speed + terms[j, 1] * force + terms[j, 2] * ahead + terms[j, 3] * behind


def update_kernel(counts, images, image_ref, gathered_ref, *refs):
    path, refs = groups(refs, counts)
    forces, speeds, moved, new_speeds = refs[:2], refs[2:4], refs[4:6], refs[6:8]
    tops, bottoms, speed_sq, terms = refs[8], refs[9], refs[10:12], refs[12]
    step_terms(image_ref, gathered_ref, images, terms)
    sums = (jnp.zeros((8, 128), jnp.float32),) * 2
    for region in range(REGIONS):
        held = [piece_of(pieces, region) for pieces in path]
        rows = held[0][2]

        def one(p, carry):
            carry = list(carry)
            for axis in range(3):
                at = [ref[axis, start + p] for ref, start, _ in held]
                diff = [at[j + 1] - at[j] for j in range(3)]
                for j in range(2):
                    q = region * rows + p
                    speed = new_speed(terms, j, speeds[j][axis, q], forces[j][axis, q], diff[j + 1], diff[j])
                    new_speeds[j][axis, q] = speed
                    moved[j][axis, q] = at[j + 1] + time_step * speed
                    carry[j] = carry[j] + speed * speed
            return tuple(carry)

        sums = over_planes(one, rows, 2, sums)
    speed_sq[0][...], speed_sq[1][...] = sums
    planes = moved[0].shape[1]
    for j in range(2):
        tops[j] = moved[j][:, planes - HALO :]
        bottoms[j] = moved[j][:, :HALO]


def update(image, gathered, path, forces, speeds, images):
    counts = [len(pieces) for pieces in path]
    arrays = [piece for pieces in path for piece in pieces] + [*forces, *speeds]
    out = jax.ShapeDtypeStruct(forces[0].shape, jnp.float32)
    edge = jax.ShapeDtypeStruct((2, 3, HALO, 8, 128), jnp.float32)
    results = pl.pallas_call(
        functools.partial(update_kernel, counts, images),
        out_shape=(out,) * 4 + (edge,) * 2 + (TILE,) * 2,
        in_specs=[SMEM] + [VMEM] * (1 + len(arrays)),
        out_specs=(VMEM,) * 8,
        scratch_shapes=[pltpu.VMEM((2, 4, 8, 128), jnp.float32)],
        compiler_params=PARAMS,
        name="fire_update",
    )(image, gathered, *arrays)
    return results[:2], results[2:4], results[4], results[5], results[6:]


def last_partner_kernel(images, image_ref, gathered_ref, before, here, after, force, speed, *outs):
    parts, terms_ref = outs[:-1], outs[-1]
    step_terms(image_ref, gathered_ref, images, terms_ref)
    for region, part in enumerate(parts):
        rows = part.shape[1]

        def one(p, carry):
            q = region * rows + p
            for axis in range(3):
                at = here[axis, q]
                part[axis, p] = new_speed(
                    terms_ref, 1, speed[axis, q], force[axis, q], after[axis, q] - at, at - before[axis, q]
                )
            return carry

        over_planes(one, rows, 2)


def last_partner(image, gathered, path, force, speed, images):
    part = jax.ShapeDtypeStruct((3, force.shape[1] // REGIONS, 8, 128), jnp.float32)
    return pl.pallas_call(
        functools.partial(last_partner_kernel, images),
        out_shape=(part,) * REGIONS + (jax.ShapeDtypeStruct((2, 4, 8, 128), jnp.float32),),
        in_specs=[SMEM] + [VMEM] * 6,
        out_specs=(VMEM,) * (REGIONS + 1),
        compiler_params=PARAMS,
        name="last_partner",
    )(image, gathered, *path, force, speed)


def last_own_kernel(side_ref, terms, before, here, after, force, speed, moved, new_ref):
    def one(p, carry):
        for axis in range(3):
            at = here[axis, p]
            new = new_speed(
                terms, 0, speed[axis, p], force[axis, p], after[axis, p] - at, at - before[axis, p]
            )
            new_ref[axis, p] = new
            moved[axis, p] = at + time_step * new
        return carry

    over_planes(one, here.shape[1], 2)


def last_own(side, terms, path, force, speed):
    planes = force.shape[1]
    chunk = planes // REGIONS
    block = pl.BlockSpec((3, chunk, 8, 128), lambda t, side_ref: (0, t, 0, 0))
    half = pl.BlockSpec((3, chunk, 8, 128), lambda t, side_ref: (0, side_ref[0] * REGIONS + t, 0, 0))
    out = jax.ShapeDtypeStruct((3, 2 * planes, 8, 128), jnp.float32)
    return pl.pallas_call(
        last_own_kernel,
        grid_spec=pltpu.PrefetchScalarGridSpec(
            num_scalar_prefetch=1,
            grid=(REGIONS,),
            in_specs=[pl.BlockSpec((2, 4, 8, 128), lambda t, side_ref: (0, 0, 0, 0))] + [block] * 5,
            out_specs=(half, half),
        ),
        out_shape=(out, out),
        compiler_params=PARAMS,
        name="last_own",
    )(side, terms, *path, force, speed)


def last_join_kernel(side_ref, here, speed, moved_in, speed_in, moved, new_ref):
    def one(p, carry):
        for axis in range(3):
            new = speed[axis, p]
            new_ref[axis, p] = new
            moved[axis, p] = here[axis, p] + time_step * new
        return carry

    over_planes(one, speed.shape[1], 4)


def last_join(side, region, here, speed, moved, speeds):
    rows = speed.shape[1]
    chunk = rows // JOIN_STEPS
    first = region * JOIN_STEPS
    block = pl.BlockSpec((3, chunk, 8, 128), lambda t, side_ref: (0, t, 0, 0))
    here_block = pl.BlockSpec((3, chunk, 8, 128), lambda t, side_ref: (0, first + t, 0, 0))
    half = pl.BlockSpec(
        (3, chunk, 8, 128),
        lambda t, side_ref: (0, (1 - side_ref[0]) * REGIONS * JOIN_STEPS + first + t, 0, 0),
    )
    out = jax.ShapeDtypeStruct(moved.shape, jnp.float32)
    whole = pl.BlockSpec(memory_space=pl.ANY)
    return pl.pallas_call(
        last_join_kernel,
        grid_spec=pltpu.PrefetchScalarGridSpec(
            num_scalar_prefetch=1,
            grid=(JOIN_STEPS,),
            in_specs=[here_block, block, whole, whole],
            out_specs=(half, half),
        ),
        out_shape=(out, out),
        input_output_aliases={3: 0, 4: 1},
        compiler_params=PARAMS,
        name="last_join",
    )(side, here, speed, moved, speeds)


def cut_kernel(starts, squares, side_ref, *refs):
    count = len(starts)
    source, outs, sems = refs[0], refs[1 : 1 + count], refs[-1]
    copies = []
    for k, out in enumerate(outs):
        rows = source.at[:, pl.ds(at_side(starts[k], side_ref), out.shape[1])]
        copies.append(pltpu.make_async_copy(rows, out, sems.at[k]))
    for copy in copies:
        copy.start()
    for copy in copies:
        copy.wait()
    if squares:
        total = jnp.zeros((8, 128), jnp.float32)
        for out in outs:

            def one(p, total, out=out):
                return total + sum(out[axis, p] * out[axis, p] for axis in range(3))

            total = over_planes(one, out.shape[1], 4, total)
        refs[1 + count][...] = total


def at_side(pair, side_ref):
    even, odd = pair
    return even if even == odd else even + (odd - even) * side_ref[0]


def cut(side, array, starts, sizes, squares=False):
    count = len(sizes)
    return pl.pallas_call(
        functools.partial(cut_kernel, starts, squares),
        out_shape=tuple(jax.ShapeDtypeStruct((3, size, 8, 128), jnp.float32) for size in sizes)
        + (TILE,) * squares,
        in_specs=[SMEM, pl.BlockSpec(memory_space=pltpu.HBM)],
        out_specs=(VMEM,) * (count + squares),
        scratch_shapes=[pltpu.SemaphoreType.DMA((count,))],
        compiler_params=PARAMS,
        name="cut",
    )(side, array)


def local(displacement, velocity):
    planes = displacement.shape[2] // (SIDE * SIDE)
    half = planes // 2
    images, slabs = lax.axis_size("image"), lax.axis_size("domain")
    both = ("image", "domain")
    own_image = lax.axis_index("image").astype(jnp.int32)
    side = own_image % 2
    image_arg, side_arg = own_image.reshape(1), side.reshape(1)
    slab = displacement.reshape(3, planes, 8, 128)
    slab_speed = velocity.reshape(3, planes, 8, 128)

    def at(image, domain):
        return image * slabs + domain % slabs

    everyone = [(i, d) for i in range(images) for d in range(slabs)]
    outer_own = [(at(i, d), at(i, d + 1 - 2 * (i % 2))) for i, d in everyone]
    outer_partner = [(at(i, d), at(i ^ 1, d - 1 + 2 * (i % 2))) for i, d in everyone]
    across = [(i, i ^ 1) for i in range(images)]
    own_out = [(i, i - 2 + 4 * (i % 2)) for i in range(images)]
    own_out = [(a, b) for a, b in own_out if 0 <= b < images]
    partner_out = [(b, a) for a, b in own_out]
    upward = [(at(i, d), at(i ^ 1, d + i % 2)) for i, d in everyone]
    downward = [(b, a) for a, b in upward]

    end, top = planes - HALO, half + HALO
    piece = half // REGIONS
    edge_own, edge_partner, edge_inner, near_inner, own, *far_pieces = cut(
        side_arg,
        slab,
        ((end, 0), (0, end), (half - HALO, half), (half, half - HALO), (0, half))
        + tuple((half + c * piece, c * piece) for c in range(REGIONS)),
        (HALO,) * 4 + (half,) + (piece,) * REGIONS,
    )
    halo_own = lax.ppermute(edge_own, both, outer_own)
    halo_partner = lax.ppermute(edge_partner, both, outer_partner)
    halo_inner = lax.ppermute(edge_inner, "image", across)
    *far_pieces[1:], halo_own, halo_partner, halo_inner = lax.optimization_barrier(
        (*far_pieces[1:], halo_own, halo_partner, halo_inner)
    )
    partner = [lax.ppermute(part, "image", across) for part in far_pieces]
    beyond_own = lax.ppermute(own, "image", own_out)
    outer, inner = (0, top), (top, 0)
    own_force, own_energy = image_forces(
        side_arg,
        half,
        ((own, None, (HALO, HALO)), (halo_own, None, outer), (near_inner, None, inner)),
    )
    own_speed, far_speed, slab_sq = cut(
        side_arg, slab_speed, ((0, half), (half, 0)), (half, half), True
    )
    far_speed, _ = lax.optimization_barrier((far_speed, own_energy))
    *partner[1:], _ = lax.optimization_barrier((*partner[1:], own_energy))
    beyond_partner = [lax.ppermute(part, "image", partner_out) for part in partner]
    halo_inner, beyond_partner[0] = lax.optimization_barrier((halo_inner, beyond_partner[0]))
    partner_speed = lax.ppermute(far_speed, "image", across)

    partner_sources = tuple(
        (part, None, (HALO + c * piece,) * 2) for c, part in enumerate(partner)
    ) + ((halo_partner, None, outer), (halo_inner, None, inner))
    path = (beyond_partner, [own], partner, [beyond_own])
    speeds = (own_speed, partner_speed)
    speed_sq = (slab_sq, jnp.zeros_like(slab_sq))
    results = [(own_force, own_energy), image_forces(side_arg, half, partner_sources)]
    for step_index in range(FIRE_STEPS):
        if step_index > 0:
            results = [image_forces(side_arg, half, held) for held in sources]
            back_home, _ = lax.optimization_barrier((back_home, results[0][1]))
            returned = lax.ppermute(back_home, "image", across)
        forces, energies = zip(*results)
        payload = moments(side_arg, path, forces, energies, speed_sq, images * slabs)
        gathered = lax.all_to_all(payload, both, 0, 0, tiled=True)
        if step_index == FIRE_STEPS - 1:
            break
        moved, speeds, tops, bottoms, speed_sq = update(image_arg, gathered, path, forces, speeds, images)
        low = lax.ppermute(tops, both, upward)
        high = lax.ppermute(bottoms, both, downward)
        sources = [
            (
                (moved[j], None, (HALO, HALO)),
                (low, 1 - j, (0, 0)),
                (high, 1 - j, (top, top)),
            )
            for j in range(2)
        ]
        path = (
            [lax.ppermute(moved[1], "image", partner_out)],
            [moved[0]],
            [moved[1]],
            [lax.ppermute(moved[0], "image", own_out)],
        )
        back_home = moved[1]
    whole = [pieces[0] for pieces in path]
    *last_speeds, terms = last_partner(
        image_arg, gathered, whole[1:], forces[1], speeds[1], images
    )
    last_speeds = [lax.ppermute(part, "image", across) for part in last_speeds]
    moved, new_speeds = last_own(side_arg, terms, whole[:3], forces[0], speeds[0])
    for region, part in enumerate(last_speeds):
        moved, new_speeds = last_join(side_arg, region, returned, part, moved, new_speeds)
    return (moved.reshape(displacement.shape), new_speeds.reshape(velocity.shape))


def solution(mesh):
    spec = P("image", None, "domain")
    return jax.shard_map(
        local,
        mesh=mesh,
        in_specs=(spec, spec),
        out_specs=(spec, spec),
        check_vma=False,
    )
```

```python
import functools
import math

import jax
import jax.numpy as jnp
from jax import lax
from jax.experimental import pallas as pl
from jax.experimental.pallas import tpu as pltpu
from jax.sharding import PartitionSpec as P

SIDE = 32
FIRE_STEPS = 2
QUANTITIES = 8
HALO = 2
PLACE_UNROLL = 16
EMBED_UNROLL = 48
FINISH_UNROLL = 16
REGIONS = 2
JOIN_STEPS = 2

lattice_const = 3.615
cutoff_sq = 9.61
nearest_sq = 6.533136
pair_scale = 30.0
pair_depth = 0.3
embed_scale = 1.2
bulk_root = 3.605551275463989
spring_const = 2.0
time_step = 0.1
fire_mixing = 0.1
stabilizer = 1e-06

reach_root = math.sqrt(cutoff_sq)
unit_half = 0.5 * lattice_const / reach_root
kappa = cutoff_sq / nearest_sq
dens_shift = (2.0 - kappa) / kappa
pair_shift = (2.5 - 2.0 * kappa) / (2.0 * kappa)
dens_scale = pair_scale * kappa
pair_energy_scale = pair_scale * pair_depth * 2.0 * kappa
dens_slope_shift = 0.75 * dens_shift
pair_slope_shift = 0.75 * pair_shift
dens_slope_scale = -4.0 * dens_scale / cutoff_sq
pair_slope_scale = -4.0 * pair_energy_scale / cutoff_sq
slope_ratio = dens_slope_scale / pair_slope_scale
force_scale = 2.0 * pair_slope_scale * reach_root


def shift(field, step_u, step_v, lanes):
    reach = step_u * SIDE + step_v
    turned = pltpu.roll(field, (-reach) % 128, 1)
    if step_u == 0:
        return turned
    carried = pltpu.roll(turned, (-step_u) % 8, 0)
    return jnp.where(lanes >= 128 - reach if reach > 0 else lanes < -reach, carried, turned)


def partners(field, step, lanes):
    return (
        shift(field, 0, step, lanes),
        shift(field, step, 0, lanes),
        shift(field, step, step, lanes),
    )


def gather_back(at_v, at_u, at_uv, step, lanes):
    return (
        shift(at_v, 0, -step, lanes)
        + shift(at_u, -step, 0, lanes)
        + shift(at_uv, -step, -step, lanes)
    )


def limits(step, u, v):
    far = jnp.float32(-1e30)
    in_u = (u + step >= 0) & (u + step < SIDE)
    in_v = (v + step >= 0) & (v + step < SIDE)
    one = jnp.ones_like(u, jnp.float32)
    return (
        jnp.where(in_v, one, far),
        jnp.where(in_u, one, far),
        jnp.where(in_u & in_v, one, far),
    )


def side_of(plane):
    return 1 if plane % 2 == 0 else -1


def force_kernel(starts, slots, side_ref, *refs):
    count = len(starts)
    sources = [ref if slot is None else ref.at[slot] for ref, slot in zip(refs, slots)]
    force_ref, energy_ref, pos, turned, seps, slopes, rho, back, embed, force_back = refs[count:]
    f32 = jnp.float32
    planes = force_ref.shape[1]
    lanes = lax.broadcasted_iota(jnp.int32, (8, 128), 1)
    subl = lax.broadcasted_iota(jnp.int32, (8, 128), 0)
    site_u = subl * 4 + lanes // SIDE
    site_v = lanes % SIDE
    inverse = f32(1.0 / reach_root)
    zero = jnp.zeros((8, 128), f32)

    def place(q, side, values):
        for axis in range(3):
            value = values[axis] * inverse
            pos[axis, q] = value
            for k, seen in enumerate(partners(value, side, lanes)):
                turned[axis, k, q] = seen

    for k, source in enumerate(sources):
        rows = source.shape[1]
        unroll = rows if rows <= 24 else PLACE_UNROLL

        def place_some(t, carry, source=source, start=at_side(starts[k], side_ref), unroll=unroll):
            for j in range(unroll):
                p = t * unroll + j
                place(start + p, side_of(j), [source[axis, p] for axis in range(3)])
            return carry

        lax.fori_loop(0, rows // unroll, place_some, 0)

    def separations(e, step):
        h = f32(unit_half)
        sh = f32(step * unit_half)
        own = [pos[axis, e] for axis in range(3)]
        nxt = [pos[axis, e + 1] for axis in range(3)]
        seen = [[turned[axis, k, e + 1] for k in range(3)] for axis in range(3)]
        own_x = own[0] - h
        y_of = (own[1] + sh, own[1], own[1] - sh)
        z_of = (own[2] - sh, own[2], own[2] + sh)
        cross = [
            (nxt[0] - own_x, nxt[1] - y_of[0], nxt[2] - z_of[1]),
            (seen[0][0] - own_x, seen[1][0] - y_of[1], seen[2][0] - z_of[2]),
            (seen[0][1] - own_x, seen[1][1] - y_of[1], seen[2][1] - z_of[0]),
            (seen[0][2] - own_x, seen[1][2] - y_of[2], seen[2][2] - z_of[1]),
        ]
        near_y = nxt[1] - sh
        near_zv = nxt[2] + sh
        near_zu = nxt[2] - sh
        inside = [
            (seen[0][0] - nxt[0], seen[1][0] - near_y, seen[2][0] - near_zv),
            (seen[0][1] - nxt[0], seen[1][1] - near_y, seen[2][1] - near_zu),
        ]
        return cross + inside

    def density(e, step, bounds, carry):
        rho_part, sum_f, sum_c = carry
        one = jnp.ones((8, 128), f32)
        tops = (one, bounds[0], bounds[1], bounds[2], bounds[0], bounds[1])
        dens, cubes = [], []
        for k, sep in enumerate(separations(e, step)):
            y = sep[0] * sep[0] + sep[1] * sep[1] + sep[2] * sep[2]
            c = jnp.maximum(tops[k] - y, 0.0)
            square = c * c
            cube = square * c
            dens.append(cube * (c + f32(dens_shift)))
            cubes.append(cube)
            for axis in range(3):
                seps[e, k, axis] = sep[axis]
            slopes[e, k, 0] = square * (c + f32(pair_slope_shift))
            slopes[e, k, 1] = square * (c + f32(dens_slope_shift))
        cross = (dens[0] + dens[1]) + (dens[2] + dens[3])
        inside = dens[4] + dens[5]
        rho[e] = rho_part + cross
        back[0, e + 1] = dens[1] + dens[4]
        back[1, e + 1] = dens[2] + dens[5]
        back[2, e + 1] = dens[3]
        weight = jnp.where((e >= 1) & (e <= planes), 1.0, 0.0).astype(f32)
        sum_f = sum_f + weight * (cross + inside)
        sum_c = sum_c + weight * (
            ((cubes[0] + cubes[1]) + (cubes[2] + cubes[3])) + (cubes[4] + cubes[5])
        )
        return (dens[0] + inside, sum_f, sum_c)

    down = limits(-1, site_u, site_v)
    up = limits(1, site_u, site_v)

    def density_pair(t, carry):
        carry = density(2 * t, -1, down, carry)
        return density(2 * t + 1, 1, up, carry)

    carry = lax.fori_loop(0, planes // 2 + 1, density_pair, (zero, zero, zero))
    _, sum_f, sum_c = density(planes + 2, -1, down, carry)

    def embedding(q, side):
        total = rho[q] + gather_back(back[0, q], back[1, q], back[2, q], side, lanes)
        w = 1.0 + f32(dens_scale) * total
        inv = lax.rsqrt(w)
        embed[0, q] = f32(-0.5 * embed_scale * slope_ratio) * inv
        return w * inv - f32(bulk_root)

    embedding(1, side_of(1))
    embedding(planes + HALO, side_of(0))

    def embed_some(t, total):
        for j in range(EMBED_UNROLL):
            total = total + embedding(HALO + t * EMBED_UNROLL + j, side_of(j))
        return total

    roots = lax.fori_loop(0, planes // EMBED_UNROLL, embed_some, zero)
    energy_ref[...] = f32(-embed_scale) * roots + f32(pair_energy_scale) * (
        sum_f + f32(pair_shift - dens_shift) * sum_c
    )

    def see(q, side):
        for k, seen in enumerate(partners(embed[0, q], side, lanes)):
            embed[1 + k, q] = seen

    see(planes + HALO, side_of(0))

    def see_some(t, carry):
        for j in range(EMBED_UNROLL):
            see(HALO + t * EMBED_UNROLL + j, side_of(j))
        return carry

    lax.fori_loop(0, planes // EMBED_UNROLL, see_some, 0)

    def force(e, keep, carry):
        own = embed[0, e]
        nxt = embed[0, e + 1]
        at_v, at_u, at_uv = [embed[1 + k, e + 1] for k in range(3)]
        partner = (own + nxt, own + at_v, own + at_u, own + at_uv, nxt + at_v, nxt + at_u)
        weight = [slopes[e, k, 0] + partner[k] * slopes[e, k, 1] for k in range(6)]
        out = []
        for axis in range(3):
            g = [weight[k] * seps[e, k, axis] for k in range(6)]
            if keep:
                force_ref[axis, e - HALO] = carry[axis] + ((g[0] + g[1]) + (g[2] + g[3]))
            force_back[axis, 0, e + 1] = g[1] + g[4]
            force_back[axis, 1, e + 1] = g[2] + g[5]
            force_back[axis, 2, e + 1] = g[3]
            out.append((g[4] + g[5]) - g[0])
        return tuple(out)

    def force_pair(t, carry):
        carry = force(HALO + 2 * t, True, carry)
        return force(HALO + 2 * t + 1, True, carry)

    lax.fori_loop(0, planes // 2, force_pair, force(1, False, (zero, zero, zero)))

    def finish(t, carry):
        for j in range(FINISH_UNROLL):
            p = t * FINISH_UNROLL + j
            for axis in range(3):
                parts = [force_back[axis, k, p + HALO] for k in range(3)]
                force_ref[axis, p] = f32(force_scale) * (
                    force_ref[axis, p] - gather_back(*parts, side_of(j), lanes)
                )
        return carry

    lax.fori_loop(0, planes // FINISH_UNROLL, finish, 0)


def image_forces(side, planes, sources):
    arrays, slots, starts = zip(*sources)
    vmem = pl.BlockSpec(memory_space=pltpu.VMEM)
    rows = planes + 2 * HALO
    return pl.pallas_call(
        functools.partial(force_kernel, starts, slots),
        out_shape=(
            jax.ShapeDtypeStruct((3, planes, 8, 128), jnp.float32),
            jax.ShapeDtypeStruct((8, 128), jnp.float32),
        ),
        in_specs=[pl.BlockSpec(memory_space=pltpu.SMEM)] + [vmem] * len(arrays),
        out_specs=(vmem, vmem),
        scratch_shapes=[
            pltpu.VMEM((3, rows, 8, 128), jnp.float32),
            pltpu.VMEM((3, 3, rows, 8, 128), jnp.float32),
            pltpu.VMEM((rows, 6, 3, 8, 128), jnp.float32),
            pltpu.VMEM((rows, 6, 2, 8, 128), jnp.float32),
            pltpu.VMEM((rows, 8, 128), jnp.float32),
            pltpu.VMEM((3, rows, 8, 128), jnp.float32),
            pltpu.VMEM((4, rows, 8, 128), jnp.float32),
            pltpu.VMEM((3, 3, rows, 8, 128), jnp.float32),
        ],
        compiler_params=pltpu.CompilerParams(vmem_limit_bytes=20 * 1024 * 1024),
        cost_estimate=pl.CostEstimate(
            flops=20_000_000, bytes_accessed=15_000_000, transcendentals=0
        ),
        name="slab_forces",
    )(side, *arrays)


def total_of(tile):
    return jnp.sum(jnp.sum(tile, axis=0, keepdims=True), axis=1, keepdims=True)


def piece_of(pieces, region):
    rows = sum(piece.shape[1] for piece in pieces) // REGIONS
    at = region * rows
    for piece in pieces:
        if at < piece.shape[1]:
            return piece, at, rows
        at -= piece.shape[1]


def over_planes(body, rows, unroll, carry=0):
    def some(t, carry):
        for j in range(unroll):
            carry = body(t * unroll + j, carry)
        return carry

    return lax.fori_loop(0, rows // unroll, some, carry)


def groups(refs, counts):
    out, at = [], 0
    for count in counts:
        out.append(refs[at : at + count])
        at += count
    return out, refs[at:]


def moment_kernel(counts, side_ref, *refs):
    path, refs = groups(refs, counts)
    forces, energies, speed_sq, out_ref = refs[:2], refs[2:4], refs[4:6], refs[6]
    zero = jnp.zeros((8, 128), jnp.float32)
    sums = (zero,) * 12
    for region in range(REGIONS):
        held = [piece_of(pieces, region) for pieces in path]
        rows = held[0][2]

        def one(p, carry):
            carry = list(carry)
            for axis in range(3):
                at = [ref[axis, start + p] for ref, start, _ in held]
                diff = [at[j + 1] - at[j] for j in range(3)]
                square = [d * d for d in diff]
                for j in range(2):
                    force = forces[j][axis, region * rows + p]
                    terms = (
                        force * force,
                        force * diff[j + 1],
                        force * diff[j],
                        square[j + 1],
                        square[j],
                        diff[j] * diff[j + 1],
                    )
                    for k, term in enumerate(terms):
                        carry[6 * j + k] = carry[6 * j + k] + term
            return tuple(carry)

        sums = over_planes(one, rows, 2, sums)

    lane = lax.broadcasted_iota(jnp.int32, (1, 128), 1)
    odd = side_ref[0] == 1
    sign = jnp.where(odd, -1.0, 1.0).astype(jnp.float32)
    row = jnp.zeros((1, 128), jnp.float32)
    for j in range(2):
        ahead = [total_of(sums[6 * j + k]) for k in range(6)]
        values = (
            total_of(energies[j][...]),
            ahead[0],
            sign * jnp.where(odd, ahead[2], ahead[1]),
            sign * jnp.where(odd, ahead[1], ahead[2]),
            jnp.where(odd, ahead[4], ahead[3]),
            jnp.where(odd, ahead[3], ahead[4]),
            ahead[5],
            total_of(speed_sq[j][...]),
        )
        for k, value in enumerate(values):
            row = row + jnp.where(lane == 8 * j + k, value, 0.0)
    out_ref[...] = jnp.broadcast_to(row, out_ref.shape)


VMEM = pl.BlockSpec(memory_space=pltpu.VMEM)
SMEM = pl.BlockSpec(memory_space=pltpu.SMEM)
PARAMS = pltpu.CompilerParams(vmem_limit_bytes=16 * 1024 * 1024)
TILE = jax.ShapeDtypeStruct((8, 128), jnp.float32)


def moments(side, path, forces, energies, speed_sq, copies):
    counts = [len(pieces) for pieces in path]
    arrays = [piece for pieces in path for piece in pieces] + [*forces, *energies, *speed_sq]
    return pl.pallas_call(
        functools.partial(moment_kernel, counts),
        out_shape=jax.ShapeDtypeStruct((copies, 128), jnp.float32),
        in_specs=[SMEM] + [VMEM] * len(arrays),
        out_specs=VMEM,
        compiler_params=PARAMS,
        name="path_moments",
    )(side, *arrays)


def path_terms(summary, images):
    lane = lax.broadcasted_iota(jnp.int32, (8, 128), 1)
    image = lax.broadcasted_iota(jnp.int32, (8, 128), 0)

    def column(k):
        picked = jnp.sum(jnp.where(lane == k, summary, 0.0), axis=1, keepdims=True)
        return jnp.broadcast_to(picked, (8, 128))

    e_here, ff, f_fwd, f_bwd, fwd_sq, bwd_sq, fwd_bwd, speed_sq = [column(k) for k in range(8)]
    e_prev = pltpu.roll(e_here, 1, 0)
    e_next = pltpu.roll(e_here, 7, 0)
    inner = (image > 0) & (image < images - 1)
    rise = e_next - e_here
    fall = e_here - e_prev
    larger = jnp.maximum(jnp.abs(rise), jnp.abs(fall))
    smaller = jnp.minimum(jnp.abs(rise), jnp.abs(fall))
    upward = (e_next > e_here) & (e_here > e_prev)
    downward = (e_next < e_here) & (e_here < e_prev)
    toward = e_next > e_prev
    weight_fwd = jnp.where(
        upward, 1.0, jnp.where(downward, 0.0, jnp.where(toward, larger, smaller))
    )
    weight_bwd = jnp.where(
        upward, 0.0, jnp.where(downward, 1.0, jnp.where(toward, smaller, larger))
    )
    tangent_sq = (
        weight_fwd * weight_fwd * fwd_sq
        + 2.0 * weight_fwd * weight_bwd * fwd_bwd
        + weight_bwd * weight_bwd * bwd_sq
    )
    norm_sq = tangent_sq + stabilizer
    force_tan = weight_fwd * f_fwd + weight_bwd * f_bwd
    spring = spring_const * (jnp.sqrt(fwd_sq + stabilizer) - jnp.sqrt(bwd_sq + stabilizer))
    coefficient = -force_tan / norm_sq + spring / jnp.sqrt(norm_sq)
    neb_sq = ff + 2.0 * coefficient * force_tan + coefficient * coefficient * tangent_sq

    def over_inner(value):
        return jnp.sum(jnp.where(inner, value, 0.0), axis=0, keepdims=True)

    force_norm = jnp.sqrt(over_inner(neb_sq) + stabilizer)
    speed_norm = jnp.sqrt(over_inner(speed_sq) + stabilizer)
    gain = jnp.broadcast_to(fire_mixing * (speed_norm / force_norm) + time_step, (8, 128))
    keep = jnp.where(inner, 1.0 - fire_mixing, 0.0)
    push = jnp.where(inner, gain, 0.0)
    along_fwd = jnp.where(inner, gain * coefficient * weight_fwd, 0.0)
    along_bwd = jnp.where(inner, gain * coefficient * weight_bwd, 0.0)
    return keep, push, along_fwd, along_bwd


def step_terms(image_ref, gathered_ref, images, terms):
    image = lax.broadcasted_iota(jnp.int32, (8, 128), 0)
    summary = jnp.zeros((8, 128), jnp.float32)
    slabs = gathered_ref.shape[0] // images
    for g in range(images):
        rows = gathered_ref[g * slabs : (g + 1) * slabs, :]
        row = jnp.broadcast_to(jnp.sum(rows, axis=0, keepdims=True), (8, 128))
        summary = summary + jnp.where(image == g, row, 0.0)
        summary = summary + jnp.where(image == (g ^ 1), pltpu.roll(row, 120, 1), 0.0)
    keep, push, along_fwd, along_bwd = path_terms(summary, images)
    here = image_ref[0]
    odd = here % 2 == 1
    values = (keep, push, jnp.where(odd, -along_bwd, along_fwd), jnp.where(odd, -along_fwd, along_bwd))
    for j in range(2):
        at = image == (here + j * (1 - 2 * (here % 2)))
        for k, value in enumerate(values):
            own = jnp.sum(jnp.where(at, value, 0.0), axis=0, keepdims=True)
            terms[j, k] = jnp.broadcast_to(own, (8, 128))


def new_speed(terms, j, speed, force, ahead, behind):
    return terms[j, 0] * speed + terms[j, 1] * force + terms[j, 2] * ahead + terms[j, 3] * behind


def update_kernel(counts, images, image_ref, gathered_ref, slab_speed, *refs):
    path, refs = groups(refs, counts)
    forces, partner_speed, moved, new_speeds = refs[:2], refs[2], refs[3:5], refs[5:7]
    tops, bottoms, speed_sq, (terms, own_speed, sem) = refs[7], refs[8], refs[9:11], refs[11:]
    speeds = (own_speed, partner_speed)
    half = own_speed.shape[1]
    copy = pltpu.make_async_copy(
        slab_speed.at[:, pl.ds(image_ref[0] % 2 * half, half)], own_speed, sem
    )
    copy.start()
    step_terms(image_ref, gathered_ref, images, terms)
    copy.wait()
    sums = (jnp.zeros((8, 128), jnp.float32),) * 2
    for region in range(REGIONS):
        held = [piece_of(pieces, region) for pieces in path]
        rows = held[0][2]

        def one(p, carry):
            carry = list(carry)
            for axis in range(3):
                at = [ref[axis, start + p] for ref, start, _ in held]
                diff = [at[j + 1] - at[j] for j in range(3)]
                for j in range(2):
                    q = region * rows + p
                    speed = new_speed(terms, j, speeds[j][axis, q], forces[j][axis, q], diff[j + 1], diff[j])
                    new_speeds[j][axis, q] = speed
                    moved[j][axis, q] = at[j + 1] + time_step * speed
                    carry[j] = carry[j] + speed * speed
            return tuple(carry)

        sums = over_planes(one, rows, 2, sums)
    speed_sq[0][...], speed_sq[1][...] = sums
    planes = moved[0].shape[1]
    for j in range(2):
        tops[j] = moved[j][:, planes - HALO :]
        bottoms[j] = moved[j][:, :HALO]


def update(image, gathered, path, forces, slab_speed, partner_speed, images):
    counts = [len(pieces) for pieces in path]
    arrays = [piece for pieces in path for piece in pieces] + [*forces, partner_speed]
    out = jax.ShapeDtypeStruct(forces[0].shape, jnp.float32)
    edge = jax.ShapeDtypeStruct((2, 3, HALO, 8, 128), jnp.float32)
    results = pl.pallas_call(
        functools.partial(update_kernel, counts, images),
        out_shape=(out,) * 4 + (edge,) * 2 + (TILE,) * 2,
        in_specs=[SMEM, VMEM, pl.BlockSpec(memory_space=pltpu.HBM)] + [VMEM] * len(arrays),
        out_specs=(VMEM,) * 8,
        scratch_shapes=[
            pltpu.VMEM((2, 4, 8, 128), jnp.float32),
            pltpu.VMEM(forces[0].shape, jnp.float32),
            pltpu.SemaphoreType.DMA,
        ],
        compiler_params=PARAMS,
        name="fire_update",
    )(image, gathered, slab_speed, *arrays)
    return results[:2], results[2:4], results[4], results[5], results[6:]


def last_partner_kernel(images, image_ref, gathered_ref, before, here, after, force, speed, *outs):
    parts, terms_ref = outs[:-1], outs[-1]
    step_terms(image_ref, gathered_ref, images, terms_ref)
    for region, part in enumerate(parts):
        rows = part.shape[1]

        def one(p, carry):
            q = region * rows + p
            for axis in range(3):
                at = here[axis, q]
                part[axis, p] = new_speed(
                    terms_ref, 1, speed[axis, q], force[axis, q], after[axis, q] - at, at - before[axis, q]
                )
            return carry

        over_planes(one, rows, 2)


def last_partner(image, gathered, path, force, speed, images):
    part = jax.ShapeDtypeStruct((3, force.shape[1] // REGIONS, 8, 128), jnp.float32)
    return pl.pallas_call(
        functools.partial(last_partner_kernel, images),
        out_shape=(part,) * REGIONS + (jax.ShapeDtypeStruct((2, 4, 8, 128), jnp.float32),),
        in_specs=[SMEM] + [VMEM] * 6,
        out_specs=(VMEM,) * (REGIONS + 1),
        compiler_params=PARAMS,
        name="last_partner",
    )(image, gathered, *path, force, speed)


def last_own_kernel(side_ref, terms, before, here, after, force, speed, moved, new_ref):
    def one(p, carry):
        for axis in range(3):
            at = here[axis, p]
            new = new_speed(
                terms, 0, speed[axis, p], force[axis, p], after[axis, p] - at, at - before[axis, p]
            )
            new_ref[axis, p] = new
            moved[axis, p] = at + time_step * new
        return carry

    over_planes(one, here.shape[1], 2)


def last_own(side, terms, path, force, speed):
    planes = force.shape[1]
    chunk = planes // REGIONS
    block = pl.BlockSpec((3, chunk, 8, 128), lambda t, side_ref: (0, t, 0, 0))
    half = pl.BlockSpec((3, chunk, 8, 128), lambda t, side_ref: (0, side_ref[0] * REGIONS + t, 0, 0))
    out = jax.ShapeDtypeStruct((3, 2 * planes, 8, 128), jnp.float32)
    return pl.pallas_call(
        last_own_kernel,
        grid_spec=pltpu.PrefetchScalarGridSpec(
            num_scalar_prefetch=1,
            grid=(REGIONS,),
            in_specs=[pl.BlockSpec((2, 4, 8, 128), lambda t, side_ref: (0, 0, 0, 0))] + [block] * 5,
            out_specs=(half, half),
        ),
        out_shape=(out, out),
        compiler_params=PARAMS,
        name="last_own",
    )(side, terms, *path, force, speed)


def last_join_kernel(side_ref, here, speed, moved_in, speed_in, moved, new_ref):
    def one(p, carry):
        for axis in range(3):
            new = speed[axis, p]
            new_ref[axis, p] = new
            moved[axis, p] = here[axis, p] + time_step * new
        return carry

    over_planes(one, speed.shape[1], 4)


def last_join(side, region, here, speed, moved, speeds):
    rows = speed.shape[1]
    chunk = rows // JOIN_STEPS
    first = region * JOIN_STEPS
    block = pl.BlockSpec((3, chunk, 8, 128), lambda t, side_ref: (0, t, 0, 0))
    here_block = pl.BlockSpec((3, chunk, 8, 128), lambda t, side_ref: (0, first + t, 0, 0))
    half = pl.BlockSpec(
        (3, chunk, 8, 128),
        lambda t, side_ref: (0, (1 - side_ref[0]) * REGIONS * JOIN_STEPS + first + t, 0, 0),
    )
    out = jax.ShapeDtypeStruct(moved.shape, jnp.float32)
    whole = pl.BlockSpec(memory_space=pl.ANY)
    return pl.pallas_call(
        last_join_kernel,
        grid_spec=pltpu.PrefetchScalarGridSpec(
            num_scalar_prefetch=1,
            grid=(JOIN_STEPS,),
            in_specs=[here_block, block, whole, whole],
            out_specs=(half, half),
        ),
        out_shape=(out, out),
        input_output_aliases={3: 0, 4: 1},
        compiler_params=PARAMS,
        name="last_join",
    )(side, here, speed, moved, speeds)


def cut_kernel(starts, squares, side_ref, *refs):
    count = len(starts)
    source, outs, sems = refs[0], refs[1 : 1 + count], refs[-1]
    copies = []
    for k, out in enumerate(outs):
        rows = source.at[:, pl.ds(at_side(starts[k], side_ref), out.shape[1])]
        copies.append(pltpu.make_async_copy(rows, out, sems.at[k]))
    for copy in copies:
        copy.start()
    for copy in copies:
        copy.wait()
    if squares:

        def one(p, total):
            return total + sum(source[axis, p] * source[axis, p] for axis in range(3))

        refs[1 + count][...] = over_planes(one, source.shape[1], 4, jnp.zeros((8, 128), jnp.float32))


def at_side(pair, side_ref):
    even, odd = pair
    return even if even == odd else even + (odd - even) * side_ref[0]


def cut(side, array, starts, sizes, squares=False):
    count = len(sizes)
    return pl.pallas_call(
        functools.partial(cut_kernel, starts, squares),
        out_shape=tuple(jax.ShapeDtypeStruct((3, size, 8, 128), jnp.float32) for size in sizes)
        + (TILE,) * squares,
        in_specs=[SMEM, VMEM if squares else pl.BlockSpec(memory_space=pltpu.HBM)],
        out_specs=(VMEM,) * (count + squares),
        scratch_shapes=[pltpu.SemaphoreType.DMA((count,))],
        compiler_params=PARAMS,
        name="cut",
    )(side, array)


def local(displacement, velocity):
    planes = displacement.shape[2] // (SIDE * SIDE)
    half = planes // 2
    images, slabs = lax.axis_size("image"), lax.axis_size("domain")
    both = ("image", "domain")
    own_image = lax.axis_index("image").astype(jnp.int32)
    side = own_image % 2
    image_arg, side_arg = own_image.reshape(1), side.reshape(1)
    slab = displacement.reshape(3, planes, 8, 128)
    slab_speed = velocity.reshape(3, planes, 8, 128)

    def at(image, domain):
        return image * slabs + domain % slabs

    everyone = [(i, d) for i in range(images) for d in range(slabs)]
    outer_own = [(at(i, d), at(i, d + 1 - 2 * (i % 2))) for i, d in everyone]
    outer_partner = [(at(i, d), at(i ^ 1, d - 1 + 2 * (i % 2))) for i, d in everyone]
    across = [(i, i ^ 1) for i in range(images)]
    own_out = [(i, i - 2 + 4 * (i % 2)) for i in range(images)]
    own_out = [(a, b) for a, b in own_out if 0 <= b < images]
    partner_out = [(b, a) for a, b in own_out]
    upward = [(at(i, d), at(i ^ 1, d + i % 2)) for i, d in everyone]
    downward = [(b, a) for a, b in upward]

    end, top = planes - HALO, half + HALO
    piece = half // REGIONS
    edge_own, edge_partner, edge_inner, near_inner, own, *far_pieces = cut(
        side_arg,
        slab,
        ((end, 0), (0, end), (half - HALO, half), (half, half - HALO), (0, half))
        + tuple((half + c * piece, c * piece) for c in range(REGIONS)),
        (HALO,) * 4 + (half,) + (piece,) * REGIONS,
    )
    halo_own = lax.ppermute(edge_own, both, outer_own)
    halo_partner = lax.ppermute(edge_partner, both, outer_partner)
    halo_inner = lax.ppermute(edge_inner, "image", across)
    *far_pieces[1:], halo_own, halo_partner, halo_inner = lax.optimization_barrier(
        (*far_pieces[1:], halo_own, halo_partner, halo_inner)
    )
    partner = [lax.ppermute(part, "image", across) for part in far_pieces]
    beyond_own = lax.ppermute(own, "image", own_out)
    outer, inner = (0, top), (top, 0)
    beyond_partner = [lax.ppermute(part, "image", partner_out) for part in partner]
    partner_force, partner_energy = image_forces(
        side_arg,
        half,
        tuple((part, None, (HALO + c * piece,) * 2) for c, part in enumerate(partner))
        + ((halo_partner, None, outer), (halo_inner, None, inner)),
    )
    held, near_inner, beyond_partner[0], _ = lax.optimization_barrier(
        (own, near_inner, beyond_partner[0], partner_energy)
    )
    own_force, own_energy = image_forces(
        side_arg,
        half,
        ((held, None, (HALO, HALO)), (halo_own, None, outer), (near_inner, None, inner)),
    )
    far_speed, slab_sq = cut(side_arg, slab_speed, ((half, 0),), (half,), True)
    far_speed, _ = lax.optimization_barrier((far_speed, beyond_partner[0]))
    partner_speed = lax.ppermute(far_speed, "image", across)

    path = (beyond_partner, [own], partner, [beyond_own])
    speeds = (slab_speed, partner_speed)
    speed_sq = (slab_sq, jnp.zeros_like(slab_sq))
    results = [(own_force, own_energy), (partner_force, partner_energy)]
    for step_index in range(FIRE_STEPS):
        if step_index > 0:
            results = [image_forces(side_arg, half, held) for held in sources]
            back_home, _ = lax.optimization_barrier((back_home, results[0][1]))
            returned = lax.ppermute(back_home, "image", across)
        forces, energies = zip(*results)
        payload = moments(side_arg, path, forces, energies, speed_sq, images * slabs)
        gathered = lax.all_to_all(payload, both, 0, 0, tiled=True)
        if step_index == FIRE_STEPS - 1:
            break
        moved, speeds, tops, bottoms, speed_sq = update(
            image_arg, gathered, path, forces, *speeds, images
        )
        low = lax.ppermute(tops, both, upward)
        high = lax.ppermute(bottoms, both, downward)
        sources = [
            (
                (moved[j], None, (HALO, HALO)),
                (low, 1 - j, (0, 0)),
                (high, 1 - j, (top, top)),
            )
            for j in range(2)
        ]
        path = (
            [lax.ppermute(moved[1], "image", partner_out)],
            [moved[0]],
            [moved[1]],
            [lax.ppermute(moved[0], "image", own_out)],
        )
        back_home = moved[1]
    whole = [pieces[0] for pieces in path]
    *last_speeds, terms = last_partner(
        image_arg, gathered, whole[1:], forces[1], speeds[1], images
    )
    last_speeds = [lax.ppermute(part, "image", across) for part in last_speeds]
    moved, new_speeds = last_own(side_arg, terms, whole[:3], forces[0], speeds[0])
    for region, part in enumerate(last_speeds):
        moved, new_speeds = last_join(side_arg, region, returned, part, moved, new_speeds)
    return (moved.reshape(displacement.shape), new_speeds.reshape(velocity.shape))


def solution(mesh):
    spec = P("image", None, "domain")
    return jax.shard_map(
        local,
        mesh=mesh,
        in_specs=(spec, spec),
        out_specs=(spec, spec),
        check_vma=False,
    )
```

```python
import functools
import math

import jax
import jax.numpy as jnp
from jax import lax
from jax.experimental import pallas as pl
from jax.experimental.pallas import tpu as pltpu
from jax.sharding import PartitionSpec as P

SIDE = 32
FIRE_STEPS = 2
QUANTITIES = 8
HALO = 2
EMBED_UNROLL = 48
FINISH_UNROLL = 16
REGIONS = 2
PIECES = (16, 32)
JOIN_STEPS = 2

lattice_const = 3.615
cutoff_sq = 9.61
nearest_sq = 6.533136
pair_scale = 30.0
pair_depth = 0.3
embed_scale = 1.2
bulk_root = 3.605551275463989
spring_const = 2.0
time_step = 0.1
fire_mixing = 0.1
stabilizer = 1e-06

reach_root = math.sqrt(cutoff_sq)
unit_half = 0.5 * lattice_const / reach_root
kappa = cutoff_sq / nearest_sq
dens_shift = (2.0 - kappa) / kappa
pair_shift = (2.5 - 2.0 * kappa) / (2.0 * kappa)
dens_scale = pair_scale * kappa
pair_energy_scale = pair_scale * pair_depth * 2.0 * kappa
dens_slope_shift = 0.75 * dens_shift
pair_slope_shift = 0.75 * pair_shift
dens_slope_scale = -4.0 * dens_scale / cutoff_sq
pair_slope_scale = -4.0 * pair_energy_scale / cutoff_sq
slope_ratio = dens_slope_scale / pair_slope_scale
force_scale = 2.0 * pair_slope_scale * reach_root


def shift(field, step_u, step_v, lanes):
    reach = step_u * SIDE + step_v
    turned = pltpu.roll(field, (-reach) % 128, 1)
    if step_u == 0:
        return turned
    carried = pltpu.roll(turned, (-step_u) % 8, 0)
    return jnp.where(lanes >= 128 - reach if reach > 0 else lanes < -reach, carried, turned)


def partners(field, step, lanes):
    return (
        shift(field, 0, step, lanes),
        shift(field, step, 0, lanes),
        shift(field, step, step, lanes),
    )


def gather_back(at_v, at_u, at_uv, step, lanes):
    return (
        shift(at_v, 0, -step, lanes)
        + shift(at_u, -step, 0, lanes)
        + shift(at_uv, -step, -step, lanes)
    )


def limits(step, u, v):
    far = jnp.float32(-1e30)
    in_u = (u + step >= 0) & (u + step < SIDE)
    in_v = (v + step >= 0) & (v + step < SIDE)
    one = jnp.ones_like(u, jnp.float32)
    return (
        jnp.where(in_v, one, far),
        jnp.where(in_u, one, far),
        jnp.where(in_u & in_v, one, far),
    )


def side_of(plane):
    return 1 if plane % 2 == 0 else -1


def force_kernel(layouts, side_ref, *refs):
    count = sum(len(layout) for layout in layouts)
    images = len(layouts)
    arrays, outs, scratch = refs[:count], refs[count : count + 2 * images], refs[count + 2 * images :]
    at = 0
    for j, layout in enumerate(layouts):
        sources = [
            (ref if slot is None else ref.at[slot], row, size, at_side(start, side_ref))
            for ref, (slot, row, size, start) in zip(arrays[at:], layout)
        ]
        at += len(layout)
        slab_forces(sources, outs[2 * j], outs[2 * j + 1], *scratch)


def slab_forces(sources, force_ref, energy_ref, pos, turned, seps, slopes, rho, back, embed, force_back):
    f32 = jnp.float32
    planes = force_ref.shape[1]
    lanes = lax.broadcasted_iota(jnp.int32, (8, 128), 1)
    subl = lax.broadcasted_iota(jnp.int32, (8, 128), 0)
    site_u = subl * 4 + lanes // SIDE
    site_v = lanes % SIDE
    inverse = f32(1.0 / reach_root)
    zero = jnp.zeros((8, 128), f32)

    def place(q, side, values):
        for axis in range(3):
            value = values[axis] * inverse
            pos[axis, q] = value
            for k, seen in enumerate(partners(value, side, lanes)):
                turned[axis, k, q] = seen

    for source, row, size, start in sources:
        unroll = max(n for n in range(2, 25, 2) if size % n == 0)

        def place_some(t, carry, source=source, row=row, start=start, unroll=unroll):
            for j in range(unroll):
                p = t * unroll + j
                place(start + p, side_of(j), [source[axis, row + p] for axis in range(3)])
            return carry

        lax.fori_loop(0, size // unroll, place_some, 0)

    def separations(e, step):
        h = f32(unit_half)
        sh = f32(step * unit_half)
        own = [pos[axis, e] for axis in range(3)]
        nxt = [pos[axis, e + 1] for axis in range(3)]
        seen = [[turned[axis, k, e + 1] for k in range(3)] for axis in range(3)]
        own_x = own[0] - h
        y_of = (own[1] + sh, own[1], own[1] - sh)
        z_of = (own[2] - sh, own[2], own[2] + sh)
        cross = [
            (nxt[0] - own_x, nxt[1] - y_of[0], nxt[2] - z_of[1]),
            (seen[0][0] - own_x, seen[1][0] - y_of[1], seen[2][0] - z_of[2]),
            (seen[0][1] - own_x, seen[1][1] - y_of[1], seen[2][1] - z_of[0]),
            (seen[0][2] - own_x, seen[1][2] - y_of[2], seen[2][2] - z_of[1]),
        ]
        near_y = nxt[1] - sh
        near_zv = nxt[2] + sh
        near_zu = nxt[2] - sh
        inside = [
            (seen[0][0] - nxt[0], seen[1][0] - near_y, seen[2][0] - near_zv),
            (seen[0][1] - nxt[0], seen[1][1] - near_y, seen[2][1] - near_zu),
        ]
        return cross + inside

    def density(e, step, bounds, carry):
        rho_part, sum_f, sum_c = carry
        one = jnp.ones((8, 128), f32)
        tops = (one, bounds[0], bounds[1], bounds[2], bounds[0], bounds[1])
        dens, cubes = [], []
        for k, sep in enumerate(separations(e, step)):
            y = sep[0] * sep[0] + sep[1] * sep[1] + sep[2] * sep[2]
            c = jnp.maximum(tops[k] - y, 0.0)
            square = c * c
            cube = square * c
            dens.append(cube * (c + f32(dens_shift)))
            cubes.append(cube)
            for axis in range(3):
                seps[e, k, axis] = sep[axis]
            slopes[e, k, 0] = square * (c + f32(pair_slope_shift))
            slopes[e, k, 1] = square * (c + f32(dens_slope_shift))
        cross = (dens[0] + dens[1]) + (dens[2] + dens[3])
        inside = dens[4] + dens[5]
        rho[e] = rho_part + cross
        back[0, e + 1] = dens[1] + dens[4]
        back[1, e + 1] = dens[2] + dens[5]
        back[2, e + 1] = dens[3]
        weight = jnp.where((e >= 1) & (e <= planes), 1.0, 0.0).astype(f32)
        sum_f = sum_f + weight * (cross + inside)
        sum_c = sum_c + weight * (
            ((cubes[0] + cubes[1]) + (cubes[2] + cubes[3])) + (cubes[4] + cubes[5])
        )
        return (dens[0] + inside, sum_f, sum_c)

    down = limits(-1, site_u, site_v)
    up = limits(1, site_u, site_v)

    def density_pair(t, carry):
        carry = density(2 * t, -1, down, carry)
        return density(2 * t + 1, 1, up, carry)

    carry = lax.fori_loop(0, planes // 2 + 1, density_pair, (zero, zero, zero))
    _, sum_f, sum_c = density(planes + 2, -1, down, carry)

    def embedding(q, side):
        total = rho[q] + gather_back(back[0, q], back[1, q], back[2, q], side, lanes)
        w = 1.0 + f32(dens_scale) * total
        inv = lax.rsqrt(w)
        embed[0, q] = f32(-0.5 * embed_scale * slope_ratio) * inv
        return w * inv - f32(bulk_root)

    embedding(1, side_of(1))
    embedding(planes + HALO, side_of(0))

    def embed_some(t, total):
        for j in range(EMBED_UNROLL):
            total = total + embedding(HALO + t * EMBED_UNROLL + j, side_of(j))
        return total

    roots = lax.fori_loop(0, planes // EMBED_UNROLL, embed_some, zero)
    energy_ref[...] = f32(-embed_scale) * roots + f32(pair_energy_scale) * (
        sum_f + f32(pair_shift - dens_shift) * sum_c
    )

    def see(q, side):
        for k, seen in enumerate(partners(embed[0, q], side, lanes)):
            embed[1 + k, q] = seen

    see(planes + HALO, side_of(0))

    def see_some(t, carry):
        for j in range(EMBED_UNROLL):
            see(HALO + t * EMBED_UNROLL + j, side_of(j))
        return carry

    lax.fori_loop(0, planes // EMBED_UNROLL, see_some, 0)

    def force(e, keep, carry):
        own = embed[0, e]
        nxt = embed[0, e + 1]
        at_v, at_u, at_uv = [embed[1 + k, e + 1] for k in range(3)]
        partner = (own + nxt, own + at_v, own + at_u, own + at_uv, nxt + at_v, nxt + at_u)
        weight = [slopes[e, k, 0] + partner[k] * slopes[e, k, 1] for k in range(6)]
        out = []
        for axis in range(3):
            g = [weight[k] * seps[e, k, axis] for k in range(6)]
            if keep:
                force_ref[axis, e - HALO] = carry[axis] + ((g[0] + g[1]) + (g[2] + g[3]))
            force_back[axis, 0, e + 1] = g[1] + g[4]
            force_back[axis, 1, e + 1] = g[2] + g[5]
            force_back[axis, 2, e + 1] = g[3]
            out.append((g[4] + g[5]) - g[0])
        return tuple(out)

    def force_pair(t, carry):
        carry = force(HALO + 2 * t, True, carry)
        return force(HALO + 2 * t + 1, True, carry)

    lax.fori_loop(0, planes // 2, force_pair, force(1, False, (zero, zero, zero)))

    def finish(t, carry):
        for j in range(FINISH_UNROLL):
            p = t * FINISH_UNROLL + j
            for axis in range(3):
                parts = [force_back[axis, k, p + HALO] for k in range(3)]
                force_ref[axis, p] = f32(force_scale) * (
                    force_ref[axis, p] - gather_back(*parts, side_of(j), lanes)
                )
        return carry

    lax.fori_loop(0, planes // FINISH_UNROLL, finish, 0)


def image_forces(side, planes, images):
    vmem = pl.BlockSpec(memory_space=pltpu.VMEM)
    rows = planes + 2 * HALO
    arrays = [source[0] for sources in images for source in sources]
    layouts = [[source[1:] for source in sources] for sources in images]
    results = pl.pallas_call(
        functools.partial(force_kernel, layouts),
        out_shape=(
            jax.ShapeDtypeStruct((3, planes, 8, 128), jnp.float32),
            jax.ShapeDtypeStruct((8, 128), jnp.float32),
        )
        * len(images),
        in_specs=[pl.BlockSpec(memory_space=pltpu.SMEM)] + [vmem] * len(arrays),
        out_specs=(vmem,) * (2 * len(images)),
        scratch_shapes=[
            pltpu.VMEM((3, rows, 8, 128), jnp.float32),
            pltpu.VMEM((3, 3, rows, 8, 128), jnp.float32),
            pltpu.VMEM((rows, 6, 3, 8, 128), jnp.float32),
            pltpu.VMEM((rows, 6, 2, 8, 128), jnp.float32),
            pltpu.VMEM((rows, 8, 128), jnp.float32),
            pltpu.VMEM((3, rows, 8, 128), jnp.float32),
            pltpu.VMEM((4, rows, 8, 128), jnp.float32),
            pltpu.VMEM((3, 3, rows, 8, 128), jnp.float32),
        ],
        compiler_params=pltpu.CompilerParams(vmem_limit_bytes=20 * 1024 * 1024),
        cost_estimate=pl.CostEstimate(
            flops=40_000_000, bytes_accessed=30_000_000, transcendentals=0
        ),
        name="slab_forces",
    )(side, *arrays)
    return results[::2], results[1::2]


def total_of(tile):
    return jnp.sum(jnp.sum(tile, axis=0, keepdims=True), axis=1, keepdims=True)


def regions_of(path):
    at = 0
    for k, rows in enumerate(PIECES):
        yield at, rows, [(pieces[k], 0) if len(pieces) > 1 else (pieces[0], at) for pieces in path]
        at += rows


def over_planes(body, rows, unroll, carry=0):
    def some(t, carry):
        for j in range(unroll):
            carry = body(t * unroll + j, carry)
        return carry

    return lax.fori_loop(0, rows // unroll, some, carry)


def groups(refs, counts):
    out, at = [], 0
    for count in counts:
        out.append(refs[at : at + count])
        at += count
    return out, refs[at:]


def moment_kernel(counts, side_ref, *refs):
    path, refs = groups(refs, counts)
    forces, energies, speed_sq, out_ref = refs[:2], refs[2:4], refs[4:6], refs[6]
    zero = jnp.zeros((8, 128), jnp.float32)
    sums = (zero,) * 12
    for first, rows, held in regions_of(path):

        def one(p, carry):
            carry = list(carry)
            for axis in range(3):
                at = [ref[axis, start + p] for ref, start in held]
                diff = [at[j + 1] - at[j] for j in range(3)]
                square = [d * d for d in diff]
                for j in range(2):
                    force = forces[j][axis, first + p]
                    terms = (
                        force * force,
                        force * diff[j + 1],
                        force * diff[j],
                        square[j + 1],
                        square[j],
                        diff[j] * diff[j + 1],
                    )
                    for k, term in enumerate(terms):
                        carry[6 * j + k] = carry[6 * j + k] + term
            return tuple(carry)

        sums = over_planes(one, rows, 2, sums)

    lane = lax.broadcasted_iota(jnp.int32, (1, 128), 1)
    odd = side_ref[0] == 1
    sign = jnp.where(odd, -1.0, 1.0).astype(jnp.float32)
    row = jnp.zeros((1, 128), jnp.float32)
    for j in range(2):
        ahead = [total_of(sums[6 * j + k]) for k in range(6)]
        values = (
            total_of(energies[j][...]),
            ahead[0],
            sign * jnp.where(odd, ahead[2], ahead[1]),
            sign * jnp.where(odd, ahead[1], ahead[2]),
            jnp.where(odd, ahead[4], ahead[3]),
            jnp.where(odd, ahead[3], ahead[4]),
            ahead[5],
            total_of(speed_sq[j][...]),
        )
        for k, value in enumerate(values):
            row = row + jnp.where(lane == 8 * j + k, value, 0.0)
    out_ref[...] = jnp.broadcast_to(row, out_ref.shape)


VMEM = pl.BlockSpec(memory_space=pltpu.VMEM)
SMEM = pl.BlockSpec(memory_space=pltpu.SMEM)
PARAMS = pltpu.CompilerParams(vmem_limit_bytes=16 * 1024 * 1024)
TILE = jax.ShapeDtypeStruct((8, 128), jnp.float32)


def moments(side, path, forces, energies, speed_sq, copies):
    counts = [len(pieces) for pieces in path]
    arrays = [piece for pieces in path for piece in pieces] + [*forces, *energies, *speed_sq]
    return pl.pallas_call(
        functools.partial(moment_kernel, counts),
        out_shape=jax.ShapeDtypeStruct((copies, 128), jnp.float32),
        in_specs=[SMEM] + [VMEM] * len(arrays),
        out_specs=VMEM,
        compiler_params=PARAMS,
        name="path_moments",
    )(side, *arrays)


def path_terms(summary, images):
    lane = lax.broadcasted_iota(jnp.int32, (8, 128), 1)
    image = lax.broadcasted_iota(jnp.int32, (8, 128), 0)

    def column(k):
        picked = jnp.sum(jnp.where(lane == k, summary, 0.0), axis=1, keepdims=True)
        return jnp.broadcast_to(picked, (8, 128))

    e_here, ff, f_fwd, f_bwd, fwd_sq, bwd_sq, fwd_bwd, speed_sq = [column(k) for k in range(8)]
    e_prev = pltpu.roll(e_here, 1, 0)
    e_next = pltpu.roll(e_here, 7, 0)
    inner = (image > 0) & (image < images - 1)
    rise = e_next - e_here
    fall = e_here - e_prev
    larger = jnp.maximum(jnp.abs(rise), jnp.abs(fall))
    smaller = jnp.minimum(jnp.abs(rise), jnp.abs(fall))
    upward = (e_next > e_here) & (e_here > e_prev)
    downward = (e_next < e_here) & (e_here < e_prev)
    toward = e_next > e_prev
    weight_fwd = jnp.where(
        upward, 1.0, jnp.where(downward, 0.0, jnp.where(toward, larger, smaller))
    )
    weight_bwd = jnp.where(
        upward, 0.0, jnp.where(downward, 1.0, jnp.where(toward, smaller, larger))
    )
    tangent_sq = (
        weight_fwd * weight_fwd * fwd_sq
        + 2.0 * weight_fwd * weight_bwd * fwd_bwd
        + weight_bwd * weight_bwd * bwd_sq
    )
    norm_sq = tangent_sq + stabilizer
    force_tan = weight_fwd * f_fwd + weight_bwd * f_bwd
    spring = spring_const * (jnp.sqrt(fwd_sq + stabilizer) - jnp.sqrt(bwd_sq + stabilizer))
    coefficient = -force_tan / norm_sq + spring / jnp.sqrt(norm_sq)
    neb_sq = ff + 2.0 * coefficient * force_tan + coefficient * coefficient * tangent_sq

    def over_inner(value):
        return jnp.sum(jnp.where(inner, value, 0.0), axis=0, keepdims=True)

    force_norm = jnp.sqrt(over_inner(neb_sq) + stabilizer)
    speed_norm = jnp.sqrt(over_inner(speed_sq) + stabilizer)
    gain = jnp.broadcast_to(fire_mixing * (speed_norm / force_norm) + time_step, (8, 128))
    keep = jnp.where(inner, 1.0 - fire_mixing, 0.0)
    push = jnp.where(inner, gain, 0.0)
    along_fwd = jnp.where(inner, gain * coefficient * weight_fwd, 0.0)
    along_bwd = jnp.where(inner, gain * coefficient * weight_bwd, 0.0)
    return keep, push, along_fwd, along_bwd


def step_terms(image_ref, gathered_ref, images, terms):
    image = lax.broadcasted_iota(jnp.int32, (8, 128), 0)
    summary = jnp.zeros((8, 128), jnp.float32)
    slabs = gathered_ref.shape[0] // images
    for g in range(images):
        rows = gathered_ref[g * slabs : (g + 1) * slabs, :]
        row = jnp.broadcast_to(jnp.sum(rows, axis=0, keepdims=True), (8, 128))
        summary = summary + jnp.where(image == g, row, 0.0)
        summary = summary + jnp.where(image == (g ^ 1), pltpu.roll(row, 120, 1), 0.0)
    keep, push, along_fwd, along_bwd = path_terms(summary, images)
    here = image_ref[0]
    odd = here % 2 == 1
    values = (keep, push, jnp.where(odd, -along_bwd, along_fwd), jnp.where(odd, -along_fwd, along_bwd))
    for j in range(2):
        at = image == (here + j * (1 - 2 * (here % 2)))
        for k, value in enumerate(values):
            own = jnp.sum(jnp.where(at, value, 0.0), axis=0, keepdims=True)
            terms[j, k] = jnp.broadcast_to(own, (8, 128))


def new_speed(terms, j, speed, force, ahead, behind):
    return terms[j, 0] * speed + terms[j, 1] * force + terms[j, 2] * ahead + terms[j, 3] * behind


def update_kernel(counts, images, image_ref, gathered_ref, slab_speed, *refs):
    path, refs = groups(refs, counts)
    forces, partner_speed, moved, new_speeds = refs[:2], refs[2], refs[3:5], refs[5:7]
    tops, bottoms, speed_sq, (terms, own_speed, sem) = refs[7], refs[8], refs[9:11], refs[11:]
    speeds = (own_speed, partner_speed)
    half = own_speed.shape[1]
    copy = pltpu.make_async_copy(
        slab_speed.at[:, pl.ds(image_ref[0] % 2 * half, half)], own_speed, sem
    )
    copy.start()
    step_terms(image_ref, gathered_ref, images, terms)
    copy.wait()
    sums = (jnp.zeros((8, 128), jnp.float32),) * 2
    for first, rows, held in regions_of(path):

        def one(p, carry):
            carry = list(carry)
            for axis in range(3):
                at = [ref[axis, start + p] for ref, start in held]
                diff = [at[j + 1] - at[j] for j in range(3)]
                for j in range(2):
                    q = first + p
                    speed = new_speed(terms, j, speeds[j][axis, q], forces[j][axis, q], diff[j + 1], diff[j])
                    new_speeds[j][axis, q] = speed
                    moved[j][axis, q] = at[j + 1] + time_step * speed
                    carry[j] = carry[j] + speed * speed
            return tuple(carry)

        sums = over_planes(one, rows, 2, sums)
    speed_sq[0][...], speed_sq[1][...] = sums
    planes = moved[0].shape[1]
    for j in range(2):
        tops[j] = moved[j][:, planes - HALO :]
        bottoms[j] = moved[j][:, :HALO]


def update(image, gathered, path, forces, slab_speed, partner_speed, images):
    counts = [len(pieces) for pieces in path]
    arrays = [piece for pieces in path for piece in pieces] + [*forces, partner_speed]
    out = jax.ShapeDtypeStruct(forces[0].shape, jnp.float32)
    edge = jax.ShapeDtypeStruct((2, 3, HALO, 8, 128), jnp.float32)
    results = pl.pallas_call(
        functools.partial(update_kernel, counts, images),
        out_shape=(out,) * 4 + (edge,) * 2 + (TILE,) * 2,
        in_specs=[SMEM, VMEM, pl.BlockSpec(memory_space=pltpu.HBM)] + [VMEM] * len(arrays),
        out_specs=(VMEM,) * 8,
        scratch_shapes=[
            pltpu.VMEM((2, 4, 8, 128), jnp.float32),
            pltpu.VMEM(forces[0].shape, jnp.float32),
            pltpu.SemaphoreType.DMA,
        ],
        compiler_params=PARAMS,
        name="fire_update",
    )(image, gathered, slab_speed, *arrays)
    return results[:2], results[2:4], results[4], results[5], results[6:]


def last_partner_kernel(images, image_ref, gathered_ref, before, here, after, force, speed, *outs):
    parts, terms_ref = outs[:-1], outs[-1]
    step_terms(image_ref, gathered_ref, images, terms_ref)
    for region, part in enumerate(parts):
        rows = part.shape[1]

        def one(p, carry):
            q = region * rows + p
            for axis in range(3):
                at = here[axis, q]
                part[axis, p] = new_speed(
                    terms_ref, 1, speed[axis, q], force[axis, q], after[axis, q] - at, at - before[axis, q]
                )
            return carry

        over_planes(one, rows, 2)


def last_partner(image, gathered, path, force, speed, images):
    part = jax.ShapeDtypeStruct((3, force.shape[1] // REGIONS, 8, 128), jnp.float32)
    return pl.pallas_call(
        functools.partial(last_partner_kernel, images),
        out_shape=(part,) * REGIONS + (jax.ShapeDtypeStruct((2, 4, 8, 128), jnp.float32),),
        in_specs=[SMEM] + [VMEM] * 6,
        out_specs=(VMEM,) * (REGIONS + 1),
        compiler_params=PARAMS,
        name="last_partner",
    )(image, gathered, *path, force, speed)


def last_own_kernel(side_ref, terms, before, here, after, force, speed, moved, new_ref):
    def one(p, carry):
        for axis in range(3):
            at = here[axis, p]
            new = new_speed(
                terms, 0, speed[axis, p], force[axis, p], after[axis, p] - at, at - before[axis, p]
            )
            new_ref[axis, p] = new
            moved[axis, p] = at + time_step * new
        return carry

    over_planes(one, here.shape[1], 2)


def last_own(side, terms, path, force, speed):
    planes = force.shape[1]
    chunk = planes // REGIONS
    block = pl.BlockSpec((3, chunk, 8, 128), lambda t, side_ref: (0, t, 0, 0))
    half = pl.BlockSpec((3, chunk, 8, 128), lambda t, side_ref: (0, side_ref[0] * REGIONS + t, 0, 0))
    out = jax.ShapeDtypeStruct((3, 2 * planes, 8, 128), jnp.float32)
    return pl.pallas_call(
        last_own_kernel,
        grid_spec=pltpu.PrefetchScalarGridSpec(
            num_scalar_prefetch=1,
            grid=(REGIONS,),
            in_specs=[pl.BlockSpec((2, 4, 8, 128), lambda t, side_ref: (0, 0, 0, 0))] + [block] * 5,
            out_specs=(half, half),
        ),
        out_shape=(out, out),
        compiler_params=PARAMS,
        name="last_own",
    )(side, terms, *path, force, speed)


def last_join_kernel(side_ref, here, speed, moved_in, speed_in, moved, new_ref):
    def one(p, carry):
        for axis in range(3):
            new = speed[axis, p]
            new_ref[axis, p] = new
            moved[axis, p] = here[axis, p] + time_step * new
        return carry

    over_planes(one, speed.shape[1], 4)


def last_join(side, region, here, speed, moved, speeds):
    rows = speed.shape[1]
    chunk = rows // JOIN_STEPS
    first = region * JOIN_STEPS
    block = pl.BlockSpec((3, chunk, 8, 128), lambda t, side_ref: (0, t, 0, 0))
    here_block = pl.BlockSpec((3, chunk, 8, 128), lambda t, side_ref: (0, first + t, 0, 0))
    half = pl.BlockSpec(
        (3, chunk, 8, 128),
        lambda t, side_ref: (0, (1 - side_ref[0]) * REGIONS * JOIN_STEPS + first + t, 0, 0),
    )
    out = jax.ShapeDtypeStruct(moved.shape, jnp.float32)
    whole = pl.BlockSpec(memory_space=pl.ANY)
    return pl.pallas_call(
        last_join_kernel,
        grid_spec=pltpu.PrefetchScalarGridSpec(
            num_scalar_prefetch=1,
            grid=(JOIN_STEPS,),
            in_specs=[here_block, block, whole, whole],
            out_specs=(half, half),
        ),
        out_shape=(out, out),
        input_output_aliases={3: 0, 4: 1},
        compiler_params=PARAMS,
        name="last_join",
    )(side, here, speed, moved, speeds)


def cut_kernel(blocks, squares, side_ref, *refs):
    count = len(blocks)
    source, outs, sems = refs[0], refs[1 : 1 + count], refs[-1]
    copies = []
    for k, out in enumerate(outs):
        at = 0
        for start, size in blocks[k]:
            rows = source.at[:, pl.ds(at_side(start, side_ref), size)]
            copies.append(
                pltpu.make_async_copy(rows, out.at[:, pl.ds(at, size)], sems.at[len(copies)])
            )
            at += size
    for copy in copies:
        copy.start()
    for copy in copies:
        copy.wait()
    if squares:

        def one(p, total):
            return total + sum(source[axis, p] * source[axis, p] for axis in range(3))

        refs[1 + count][...] = over_planes(one, source.shape[1], 4, jnp.zeros((8, 128), jnp.float32))


def at_side(pair, side_ref):
    even, odd = pair
    return even if even == odd else even + (odd - even) * side_ref[0]


def cut(side, array, blocks, squares=False):
    count = len(blocks)
    sizes = [sum(size for _, size in block) for block in blocks]
    return pl.pallas_call(
        functools.partial(cut_kernel, blocks, squares),
        out_shape=tuple(jax.ShapeDtypeStruct((3, size, 8, 128), jnp.float32) for size in sizes)
        + (TILE,) * squares,
        in_specs=[SMEM, VMEM if squares else pl.BlockSpec(memory_space=pltpu.HBM)],
        out_specs=(VMEM,) * (count + squares),
        scratch_shapes=[pltpu.SemaphoreType.DMA((sum(len(block) for block in blocks),))],
        compiler_params=PARAMS,
        name="cut",
    )(side, array)


def local(displacement, velocity):
    planes = displacement.shape[2] // (SIDE * SIDE)
    half = planes // 2
    images, slabs = lax.axis_size("image"), lax.axis_size("domain")
    both = ("image", "domain")
    own_image = lax.axis_index("image").astype(jnp.int32)
    side = own_image % 2
    image_arg, side_arg = own_image.reshape(1), side.reshape(1)
    slab = displacement.reshape(3, planes, 8, 128)
    slab_speed = velocity.reshape(3, planes, 8, 128)

    def at(image, domain):
        return image * slabs + domain % slabs

    everyone = [(i, d) for i in range(images) for d in range(slabs)]
    outward = [(at(i, d), at(i, d + 1 - 2 * (i % 2))) for i, d in everyone]
    across = [(i, i ^ 1) for i in range(images)]
    own_out = [(i, i - 2 + 4 * (i % 2)) for i in range(images)]
    own_out = [(a, b) for a, b in own_out if 0 <= b < images]
    partner_out = [(b, a) for a, b in own_out]
    upward = [(at(i, d), at(i ^ 1, d + i % 2)) for i, d in everyone]
    downward = [(b, a) for a, b in upward]

    end, top = planes - HALO, half + HALO
    piece = PIECES[0]
    outer, inner = (0, top), (top, 0)
    edge_own, near_inner, own, lead, rest = cut(
        side_arg,
        slab,
        (
            (((end, 0), HALO),),
            (((half, half - HALO), HALO),),
            (((0, half), half),),
            (((half, 0), piece), ((half - HALO, half), HALO), ((0, end), HALO)),
            (((half + piece, piece), PIECES[1]),),
        ),
    )
    partner = [lax.ppermute(part, "image", across) for part in (lead, rest)]
    beyond_own = lax.ppermute(own, "image", own_out)
    edges = jnp.concatenate([edge_own, partner[0][:, piece + HALO :]], axis=1)
    halo = lax.ppermute(edges, both, outward)
    beyond_partner = [lax.ppermute(part, "image", partner_out) for part in partner]
    own_source = (
        (own, None, 0, half, (HALO, HALO)),
        (halo, None, 0, HALO, outer),
        (near_inner, None, 0, HALO, inner),
    )
    partner_source = (
        (partner[0], None, 0, piece, (HALO, HALO)),
        (partner[0], None, piece, HALO, inner),
        (partner[1], None, 0, PIECES[1], (HALO + piece,) * 2),
        (halo, None, HALO, HALO, outer),
    )
    forces, energies = image_forces(side_arg, half, (own_source, partner_source))
    far_speed, slab_sq = cut(side_arg, slab_speed, ((((half, 0), half),),), True)
    far_speed, *_ = lax.optimization_barrier((far_speed, halo, beyond_partner[0]))
    partner_speed = lax.ppermute(far_speed, "image", across)

    path = (beyond_partner, [own], partner, [beyond_own])
    speeds = (slab_speed, partner_speed)
    speed_sq = (slab_sq, jnp.zeros_like(slab_sq))
    for step_index in range(FIRE_STEPS):
        if step_index > 0:
            forces, energies = image_forces(side_arg, half, sources)
        payload = moments(side_arg, path, forces, energies, speed_sq, images * slabs)
        gathered = lax.all_to_all(payload, both, 0, 0, tiled=True)
        if step_index == FIRE_STEPS - 1:
            break
        moved, speeds, tops, bottoms, speed_sq = update(
            image_arg, gathered, path, forces, *speeds, images
        )
        low = lax.ppermute(tops, both, upward)
        high = lax.ppermute(bottoms, both, downward)
        sources = [
            (
                (moved[j], None, 0, half, (HALO, HALO)),
                (low, 1 - j, 0, HALO, (0, 0)),
                (high, 1 - j, 0, HALO, (top, top)),
            )
            for j in range(2)
        ]
        path = (
            [lax.ppermute(moved[1], "image", partner_out)],
            [moved[0]],
            [moved[1]],
            [lax.ppermute(moved[0], "image", own_out)],
        )
        back_home, _, _ = lax.optimization_barrier((moved[1], low, high))
        returned = lax.ppermute(back_home, "image", across)
    whole = [pieces[0] for pieces in path]
    *last_speeds, terms = last_partner(
        image_arg, gathered, whole[1:], forces[1], speeds[1], images
    )
    last_speeds = [lax.ppermute(part, "image", across) for part in last_speeds]
    moved, new_speeds = last_own(side_arg, terms, whole[:3], forces[0], speeds[0])
    for region, part in enumerate(last_speeds):
        moved, new_speeds = last_join(side_arg, region, returned, part, moved, new_speeds)
    return (moved.reshape(displacement.shape), new_speeds.reshape(velocity.shape))


def solution(mesh):
    spec = P("image", None, "domain")
    return jax.shard_map(
        local,
        mesh=mesh,
        in_specs=(spec, spec),
        out_specs=(spec, spec),
        check_vma=False,
    )
```

```python
import functools
import math

import jax
import jax.numpy as jnp
from jax import lax
from jax.experimental import pallas as pl
from jax.experimental.pallas import tpu as pltpu
from jax.sharding import PartitionSpec as P

SIDE = 32
FIRE_STEPS = 2
QUANTITIES = 8
HALO = 2
EMBED_UNROLL = 48
FINISH_UNROLL = 16
REGIONS = 2
PIECES = (16, 32)
JOIN_STEPS = 2

lattice_const = 3.615
cutoff_sq = 9.61
nearest_sq = 6.533136
pair_scale = 30.0
pair_depth = 0.3
embed_scale = 1.2
bulk_root = 3.605551275463989
spring_const = 2.0
time_step = 0.1
fire_mixing = 0.1
stabilizer = 1e-06

reach_root = math.sqrt(cutoff_sq)
unit_half = 0.5 * lattice_const / reach_root
kappa = cutoff_sq / nearest_sq
dens_shift = (2.0 - kappa) / kappa
pair_shift = (2.5 - 2.0 * kappa) / (2.0 * kappa)
dens_scale = pair_scale * kappa
pair_energy_scale = pair_scale * pair_depth * 2.0 * kappa
dens_slope_shift = 0.75 * dens_shift
pair_slope_shift = 0.75 * pair_shift
dens_slope_scale = -4.0 * dens_scale / cutoff_sq
pair_slope_scale = -4.0 * pair_energy_scale / cutoff_sq
slope_ratio = dens_slope_scale / pair_slope_scale
force_scale = 2.0 * pair_slope_scale * reach_root


def shift(field, step_u, step_v, lanes):
    reach = step_u * SIDE + step_v
    turned = pltpu.roll(field, (-reach) % 128, 1)
    if step_u == 0:
        return turned
    carried = pltpu.roll(turned, (-step_u) % 8, 0)
    return jnp.where(lanes >= 128 - reach if reach > 0 else lanes < -reach, carried, turned)


def partners(field, step, lanes):
    return (
        shift(field, 0, step, lanes),
        shift(field, step, 0, lanes),
        shift(field, step, step, lanes),
    )


def gather_back(at_v, at_u, at_uv, step, lanes):
    return (
        shift(at_v, 0, -step, lanes)
        + shift(at_u, -step, 0, lanes)
        + shift(at_uv, -step, -step, lanes)
    )


def limits(step, u, v):
    far = jnp.float32(-1e30)
    in_u = (u + step >= 0) & (u + step < SIDE)
    in_v = (v + step >= 0) & (v + step < SIDE)
    one = jnp.ones_like(u, jnp.float32)
    return (
        jnp.where(in_v, one, far),
        jnp.where(in_u, one, far),
        jnp.where(in_u & in_v, one, far),
    )


def side_of(plane):
    return 1 if plane % 2 == 0 else -1


def force_kernel(layouts, side_ref, *refs):
    count = sum(len(layout) for layout in layouts)
    images = len(layouts)
    arrays, outs, scratch = refs[:count], refs[count : count + 2 * images], refs[count + 2 * images :]
    at = 0
    for j, layout in enumerate(layouts):
        sources = [
            (ref if slot is None else ref.at[slot], row, size, at_side(start, side_ref))
            for ref, (slot, row, size, start) in zip(arrays[at:], layout)
        ]
        at += len(layout)
        slab_forces(sources, outs[2 * j], outs[2 * j + 1], *scratch)


def slab_forces(sources, force_ref, energy_ref, pos, turned, seps, slopes, rho, back, embed, force_back):
    f32 = jnp.float32
    planes = force_ref.shape[1]
    lanes = lax.broadcasted_iota(jnp.int32, (8, 128), 1)
    subl = lax.broadcasted_iota(jnp.int32, (8, 128), 0)
    site_u = subl * 4 + lanes // SIDE
    site_v = lanes % SIDE
    inverse = f32(1.0 / reach_root)
    zero = jnp.zeros((8, 128), f32)

    def place(q, side, values):
        for axis in range(3):
            value = values[axis] * inverse
            pos[axis, q] = value
            for k, seen in enumerate(partners(value, side, lanes)):
                turned[axis, k, q] = seen

    for source, row, size, start in sources:
        unroll = max(n for n in range(2, 25, 2) if size % n == 0)

        def place_some(t, carry, source=source, row=row, start=start, unroll=unroll):
            for j in range(unroll):
                p = t * unroll + j
                place(start + p, side_of(j), [source[axis, row + p] for axis in range(3)])
            return carry

        lax.fori_loop(0, size // unroll, place_some, 0)

    def separations(e, step):
        h = f32(unit_half)
        sh = f32(step * unit_half)
        own = [pos[axis, e] for axis in range(3)]
        nxt = [pos[axis, e + 1] for axis in range(3)]
        seen = [[turned[axis, k, e + 1] for k in range(3)] for axis in range(3)]
        own_x = own[0] - h
        y_of = (own[1] + sh, own[1], own[1] - sh)
        z_of = (own[2] - sh, own[2], own[2] + sh)
        cross = [
            (nxt[0] - own_x, nxt[1] - y_of[0], nxt[2] - z_of[1]),
            (seen[0][0] - own_x, seen[1][0] - y_of[1], seen[2][0] - z_of[2]),
            (seen[0][1] - own_x, seen[1][1] - y_of[1], seen[2][1] - z_of[0]),
            (seen[0][2] - own_x, seen[1][2] - y_of[2], seen[2][2] - z_of[1]),
        ]
        near_y = nxt[1] - sh
        near_zv = nxt[2] + sh
        near_zu = nxt[2] - sh
        inside = [
            (seen[0][0] - nxt[0], seen[1][0] - near_y, seen[2][0] - near_zv),
            (seen[0][1] - nxt[0], seen[1][1] - near_y, seen[2][1] - near_zu),
        ]
        return cross + inside

    def density(e, step, bounds, carry):
        rho_part, sum_f, sum_c = carry
        one = jnp.ones((8, 128), f32)
        tops = (one, bounds[0], bounds[1], bounds[2], bounds[0], bounds[1])
        dens, cubes = [], []
        for k, sep in enumerate(separations(e, step)):
            y = sep[0] * sep[0] + sep[1] * sep[1] + sep[2] * sep[2]
            c = jnp.maximum(tops[k] - y, 0.0)
            square = c * c
            cube = square * c
            dens.append(cube * (c + f32(dens_shift)))
            cubes.append(cube)
            for axis in range(3):
                seps[e, k, axis] = sep[axis]
            slopes[e, k, 0] = square * (c + f32(pair_slope_shift))
            slopes[e, k, 1] = square * (c + f32(dens_slope_shift))
        cross = (dens[0] + dens[1]) + (dens[2] + dens[3])
        inside = dens[4] + dens[5]
        rho[e] = rho_part + cross
        back[0, e + 1] = dens[1] + dens[4]
        back[1, e + 1] = dens[2] + dens[5]
        back[2, e + 1] = dens[3]
        weight = jnp.where((e >= 1) & (e <= planes), 1.0, 0.0).astype(f32)
        sum_f = sum_f + weight * (cross + inside)
        sum_c = sum_c + weight * (
            ((cubes[0] + cubes[1]) + (cubes[2] + cubes[3])) + (cubes[4] + cubes[5])
        )
        return (dens[0] + inside, sum_f, sum_c)

    down = limits(-1, site_u, site_v)
    up = limits(1, site_u, site_v)

    def density_pair(t, carry):
        carry = density(2 * t, -1, down, carry)
        return density(2 * t + 1, 1, up, carry)

    carry = lax.fori_loop(0, planes // 2 + 1, density_pair, (zero, zero, zero))
    _, sum_f, sum_c = density(planes + 2, -1, down, carry)

    def embedding(q, side):
        total = rho[q] + gather_back(back[0, q], back[1, q], back[2, q], side, lanes)
        w = 1.0 + f32(dens_scale) * total
        inv = lax.rsqrt(w)
        embed[0, q] = f32(-0.5 * embed_scale * slope_ratio) * inv
        return w * inv - f32(bulk_root)

    embedding(1, side_of(1))
    embedding(planes + HALO, side_of(0))

    def embed_some(t, total):
        for j in range(EMBED_UNROLL):
            total = total + embedding(HALO + t * EMBED_UNROLL + j, side_of(j))
        return total

    roots = lax.fori_loop(0, planes // EMBED_UNROLL, embed_some, zero)
    energy_ref[...] = f32(-embed_scale) * roots + f32(pair_energy_scale) * (
        sum_f + f32(pair_shift - dens_shift) * sum_c
    )

    def see(q, side):
        for k, seen in enumerate(partners(embed[0, q], side, lanes)):
            embed[1 + k, q] = seen

    see(planes + HALO, side_of(0))

    def see_some(t, carry):
        for j in range(EMBED_UNROLL):
            see(HALO + t * EMBED_UNROLL + j, side_of(j))
        return carry

    lax.fori_loop(0, planes // EMBED_UNROLL, see_some, 0)

    def force(e, keep, carry):
        own = embed[0, e]
        nxt = embed[0, e + 1]
        at_v, at_u, at_uv = [embed[1 + k, e + 1] for k in range(3)]
        partner = (own + nxt, own + at_v, own + at_u, own + at_uv, nxt + at_v, nxt + at_u)
        weight = [slopes[e, k, 0] + partner[k] * slopes[e, k, 1] for k in range(6)]
        out = []
        for axis in range(3):
            g = [weight[k] * seps[e, k, axis] for k in range(6)]
            if keep:
                force_ref[axis, e - HALO] = carry[axis] + ((g[0] + g[1]) + (g[2] + g[3]))
            force_back[axis, 0, e + 1] = g[1] + g[4]
            force_back[axis, 1, e + 1] = g[2] + g[5]
            force_back[axis, 2, e + 1] = g[3]
            out.append((g[4] + g[5]) - g[0])
        return tuple(out)

    def force_pair(t, carry):
        carry = force(HALO + 2 * t, True, carry)
        return force(HALO + 2 * t + 1, True, carry)

    lax.fori_loop(0, planes // 2, force_pair, force(1, False, (zero, zero, zero)))

    def finish(t, carry):
        for j in range(FINISH_UNROLL):
            p = t * FINISH_UNROLL + j
            for axis in range(3):
                parts = [force_back[axis, k, p + HALO] for k in range(3)]
                force_ref[axis, p] = f32(force_scale) * (
                    force_ref[axis, p] - gather_back(*parts, side_of(j), lanes)
                )
        return carry

    lax.fori_loop(0, planes // FINISH_UNROLL, finish, 0)


def image_forces(side, planes, images):
    vmem = pl.BlockSpec(memory_space=pltpu.VMEM)
    rows = planes + 2 * HALO
    arrays = [source[0] for sources in images for source in sources]
    layouts = [[source[1:] for source in sources] for sources in images]
    results = pl.pallas_call(
        functools.partial(force_kernel, layouts),
        out_shape=(
            jax.ShapeDtypeStruct((3, planes, 8, 128), jnp.float32),
            jax.ShapeDtypeStruct((8, 128), jnp.float32),
        )
        * len(images),
        in_specs=[pl.BlockSpec(memory_space=pltpu.SMEM)] + [vmem] * len(arrays),
        out_specs=(vmem,) * (2 * len(images)),
        scratch_shapes=[
            pltpu.VMEM((3, rows, 8, 128), jnp.float32),
            pltpu.VMEM((3, 3, rows, 8, 128), jnp.float32),
            pltpu.VMEM((rows, 6, 3, 8, 128), jnp.float32),
            pltpu.VMEM((rows, 6, 2, 8, 128), jnp.float32),
            pltpu.VMEM((rows, 8, 128), jnp.float32),
            pltpu.VMEM((3, rows, 8, 128), jnp.float32),
            pltpu.VMEM((4, rows, 8, 128), jnp.float32),
            pltpu.VMEM((3, 3, rows, 8, 128), jnp.float32),
        ],
        compiler_params=pltpu.CompilerParams(vmem_limit_bytes=20 * 1024 * 1024),
        cost_estimate=pl.CostEstimate(
            flops=40_000_000, bytes_accessed=30_000_000, transcendentals=0
        ),
        name="slab_forces",
    )(side, *arrays)
    return results[::2], results[1::2]


def total_of(tile):
    return jnp.sum(jnp.sum(tile, axis=0, keepdims=True), axis=1, keepdims=True)


def regions_of(path):
    at = 0
    for k, rows in enumerate(PIECES):
        yield at, rows, [(pieces[k], 0) if len(pieces) > 1 else (pieces[0], at) for pieces in path]
        at += rows


def over_planes(body, rows, unroll, carry=0):
    def some(t, carry):
        for j in range(unroll):
            carry = body(t * unroll + j, carry)
        return carry

    return lax.fori_loop(0, rows // unroll, some, carry)


def groups(refs, counts):
    out, at = [], 0
    for count in counts:
        out.append(refs[at : at + count])
        at += count
    return out, refs[at:]


def moment_kernel(counts, side_ref, *refs):
    path, refs = groups(refs, counts)
    forces, energies, speed_sq, out_ref = refs[:2], refs[2:4], refs[4:6], refs[6]
    zero = jnp.zeros((8, 128), jnp.float32)
    sums = (zero,) * 12
    for first, rows, held in regions_of(path):

        def one(p, carry):
            carry = list(carry)
            for axis in range(3):
                at = [ref[axis, start + p] for ref, start in held]
                diff = [at[j + 1] - at[j] for j in range(3)]
                square = [d * d for d in diff]
                for j in range(2):
                    force = forces[j][axis, first + p]
                    terms = (
                        force * force,
                        force * diff[j + 1],
                        force * diff[j],
                        square[j + 1],
                        square[j],
                        diff[j] * diff[j + 1],
                    )
                    for k, term in enumerate(terms):
                        carry[6 * j + k] = carry[6 * j + k] + term
            return tuple(carry)

        sums = over_planes(one, rows, 2, sums)

    lane = lax.broadcasted_iota(jnp.int32, (1, 128), 1)
    odd = side_ref[0] == 1
    sign = jnp.where(odd, -1.0, 1.0).astype(jnp.float32)
    row = jnp.zeros((1, 128), jnp.float32)
    for j in range(2):
        ahead = [total_of(sums[6 * j + k]) for k in range(6)]
        values = (
            total_of(energies[j][...]),
            ahead[0],
            sign * jnp.where(odd, ahead[2], ahead[1]),
            sign * jnp.where(odd, ahead[1], ahead[2]),
            jnp.where(odd, ahead[4], ahead[3]),
            jnp.where(odd, ahead[3], ahead[4]),
            ahead[5],
            total_of(speed_sq[j][...]),
        )
        for k, value in enumerate(values):
            row = row + jnp.where(lane == 8 * j + k, value, 0.0)
    out_ref[...] = jnp.broadcast_to(row, out_ref.shape)


VMEM = pl.BlockSpec(memory_space=pltpu.VMEM)
SMEM = pl.BlockSpec(memory_space=pltpu.SMEM)
PARAMS = pltpu.CompilerParams(vmem_limit_bytes=16 * 1024 * 1024)
TILE = jax.ShapeDtypeStruct((8, 128), jnp.float32)


def moments(side, path, forces, energies, speed_sq, copies):
    counts = [len(pieces) for pieces in path]
    arrays = [piece for pieces in path for piece in pieces] + [*forces, *energies, *speed_sq]
    return pl.pallas_call(
        functools.partial(moment_kernel, counts),
        out_shape=jax.ShapeDtypeStruct((copies, 128), jnp.float32),
        in_specs=[SMEM] + [VMEM] * len(arrays),
        out_specs=VMEM,
        compiler_params=PARAMS,
        name="path_moments",
    )(side, *arrays)


def path_terms(summary, images):
    lane = lax.broadcasted_iota(jnp.int32, (8, 128), 1)
    image = lax.broadcasted_iota(jnp.int32, (8, 128), 0)

    def column(k):
        picked = jnp.sum(jnp.where(lane == k, summary, 0.0), axis=1, keepdims=True)
        return jnp.broadcast_to(picked, (8, 128))

    e_here, ff, f_fwd, f_bwd, fwd_sq, bwd_sq, fwd_bwd, speed_sq = [column(k) for k in range(8)]
    e_prev = pltpu.roll(e_here, 1, 0)
    e_next = pltpu.roll(e_here, 7, 0)
    inner = (image > 0) & (image < images - 1)
    rise = e_next - e_here
    fall = e_here - e_prev
    larger = jnp.maximum(jnp.abs(rise), jnp.abs(fall))
    smaller = jnp.minimum(jnp.abs(rise), jnp.abs(fall))
    upward = (e_next > e_here) & (e_here > e_prev)
    downward = (e_next < e_here) & (e_here < e_prev)
    toward = e_next > e_prev
    weight_fwd = jnp.where(
        upward, 1.0, jnp.where(downward, 0.0, jnp.where(toward, larger, smaller))
    )
    weight_bwd = jnp.where(
        upward, 0.0, jnp.where(downward, 1.0, jnp.where(toward, smaller, larger))
    )
    tangent_sq = (
        weight_fwd * weight_fwd * fwd_sq
        + 2.0 * weight_fwd * weight_bwd * fwd_bwd
        + weight_bwd * weight_bwd * bwd_sq
    )
    norm_sq = tangent_sq + stabilizer
    force_tan = weight_fwd * f_fwd + weight_bwd * f_bwd
    spring = spring_const * (jnp.sqrt(fwd_sq + stabilizer) - jnp.sqrt(bwd_sq + stabilizer))
    coefficient = -force_tan / norm_sq + spring / jnp.sqrt(norm_sq)
    neb_sq = ff + 2.0 * coefficient * force_tan + coefficient * coefficient * tangent_sq

    def over_inner(value):
        return jnp.sum(jnp.where(inner, value, 0.0), axis=0, keepdims=True)

    force_norm = jnp.sqrt(over_inner(neb_sq) + stabilizer)
    speed_norm = jnp.sqrt(over_inner(speed_sq) + stabilizer)
    gain = jnp.broadcast_to(fire_mixing * (speed_norm / force_norm) + time_step, (8, 128))
    keep = jnp.where(inner, 1.0 - fire_mixing, 0.0)
    push = jnp.where(inner, gain, 0.0)
    along_fwd = jnp.where(inner, gain * coefficient * weight_fwd, 0.0)
    along_bwd = jnp.where(inner, gain * coefficient * weight_bwd, 0.0)
    return keep, push, along_fwd, along_bwd


def step_terms(image_ref, gathered_ref, images, terms):
    image = lax.broadcasted_iota(jnp.int32, (8, 128), 0)
    summary = jnp.zeros((8, 128), jnp.float32)
    slabs = gathered_ref.shape[0] // images
    for g in range(images):
        rows = gathered_ref[g * slabs : (g + 1) * slabs, :]
        row = jnp.broadcast_to(jnp.sum(rows, axis=0, keepdims=True), (8, 128))
        summary = summary + jnp.where(image == g, row, 0.0)
        summary = summary + jnp.where(image == (g ^ 1), pltpu.roll(row, 120, 1), 0.0)
    keep, push, along_fwd, along_bwd = path_terms(summary, images)
    here = image_ref[0]
    odd = here % 2 == 1
    values = (keep, push, jnp.where(odd, -along_bwd, along_fwd), jnp.where(odd, -along_fwd, along_bwd))
    for j in range(2):
        at = image == (here + j * (1 - 2 * (here % 2)))
        for k, value in enumerate(values):
            own = jnp.sum(jnp.where(at, value, 0.0), axis=0, keepdims=True)
            terms[j, k] = jnp.broadcast_to(own, (8, 128))


def new_speed(terms, j, speed, force, ahead, behind):
    return terms[j, 0] * speed + terms[j, 1] * force + terms[j, 2] * ahead + terms[j, 3] * behind


def update_kernel(counts, images, image_ref, gathered_ref, slab_speed, *refs):
    path, refs = groups(refs, counts)
    forces, partner_speed, moved, new_speeds = refs[:2], refs[2], refs[3:5], refs[5:7]
    tops, bottoms, speed_sq, (terms, own_speed, sem) = refs[7], refs[8], refs[9:11], refs[11:]
    speeds = (own_speed, partner_speed)
    half = own_speed.shape[1]
    copy = pltpu.make_async_copy(
        slab_speed.at[:, pl.ds(image_ref[0] % 2 * half, half)], own_speed, sem
    )
    copy.start()
    step_terms(image_ref, gathered_ref, images, terms)
    copy.wait()
    sums = (jnp.zeros((8, 128), jnp.float32),) * 2
    for first, rows, held in regions_of(path):

        def one(p, carry):
            carry = list(carry)
            for axis in range(3):
                at = [ref[axis, start + p] for ref, start in held]
                diff = [at[j + 1] - at[j] for j in range(3)]
                for j in range(2):
                    q = first + p
                    speed = new_speed(terms, j, speeds[j][axis, q], forces[j][axis, q], diff[j + 1], diff[j])
                    new_speeds[j][axis, q] = speed
                    moved[j][axis, q] = at[j + 1] + time_step * speed
                    carry[j] = carry[j] + speed * speed
            return tuple(carry)

        sums = over_planes(one, rows, 2, sums)
    speed_sq[0][...], speed_sq[1][...] = sums
    planes = moved[0].shape[1]
    for j in range(2):
        tops[j] = moved[j][:, planes - HALO :]
        bottoms[j] = moved[j][:, :HALO]


def update(image, gathered, path, forces, slab_speed, partner_speed, images):
    counts = [len(pieces) for pieces in path]
    arrays = [piece for pieces in path for piece in pieces] + [*forces, partner_speed]
    out = jax.ShapeDtypeStruct(forces[0].shape, jnp.float32)
    edge = jax.ShapeDtypeStruct((2, 3, HALO, 8, 128), jnp.float32)
    results = pl.pallas_call(
        functools.partial(update_kernel, counts, images),
        out_shape=(out,) * 4 + (edge,) * 2 + (TILE,) * 2,
        in_specs=[SMEM, VMEM, pl.BlockSpec(memory_space=pltpu.HBM)] + [VMEM] * len(arrays),
        out_specs=(VMEM,) * 8,
        scratch_shapes=[
            pltpu.VMEM((2, 4, 8, 128), jnp.float32),
            pltpu.VMEM(forces[0].shape, jnp.float32),
            pltpu.SemaphoreType.DMA,
        ],
        compiler_params=PARAMS,
        name="fire_update",
    )(image, gathered, slab_speed, *arrays)
    return results[:2], results[2:4], results[4], results[5], results[6:]


def last_partner_kernel(images, image_ref, gathered_ref, before, here, after, force, speed, *outs):
    parts, terms_ref = outs[:-1], outs[-1]
    step_terms(image_ref, gathered_ref, images, terms_ref)
    for region, part in enumerate(parts):
        rows = part.shape[1]

        def one(p, carry):
            q = region * rows + p
            for axis in range(3):
                at = here[axis, q]
                part[axis, p] = new_speed(
                    terms_ref, 1, speed[axis, q], force[axis, q], after[axis, q] - at, at - before[axis, q]
                )
            return carry

        over_planes(one, rows, 2)


def last_partner(image, gathered, path, force, speed, images):
    part = jax.ShapeDtypeStruct((3, force.shape[1] // REGIONS, 8, 128), jnp.float32)
    return pl.pallas_call(
        functools.partial(last_partner_kernel, images),
        out_shape=(part,) * REGIONS + (jax.ShapeDtypeStruct((2, 4, 8, 128), jnp.float32),),
        in_specs=[SMEM] + [VMEM] * 6,
        out_specs=(VMEM,) * (REGIONS + 1),
        compiler_params=PARAMS,
        name="last_partner",
    )(image, gathered, *path, force, speed)


def last_own_kernel(side_ref, terms, before, here, after, force, speed, moved, new_ref):
    def one(p, carry):
        for axis in range(3):
            at = here[axis, p]
            new = new_speed(
                terms, 0, speed[axis, p], force[axis, p], after[axis, p] - at, at - before[axis, p]
            )
            new_ref[axis, p] = new
            moved[axis, p] = at + time_step * new
        return carry

    over_planes(one, here.shape[1], 2)


def last_own(side, terms, path, force, speed):
    planes = force.shape[1]
    chunk = planes // REGIONS
    block = pl.BlockSpec((3, chunk, 8, 128), lambda t, side_ref: (0, t, 0, 0))
    half = pl.BlockSpec((3, chunk, 8, 128), lambda t, side_ref: (0, side_ref[0] * REGIONS + t, 0, 0))
    out = jax.ShapeDtypeStruct((3, 2 * planes, 8, 128), jnp.float32)
    return pl.pallas_call(
        last_own_kernel,
        grid_spec=pltpu.PrefetchScalarGridSpec(
            num_scalar_prefetch=1,
            grid=(REGIONS,),
            in_specs=[pl.BlockSpec((2, 4, 8, 128), lambda t, side_ref: (0, 0, 0, 0))] + [block] * 5,
            out_specs=(half, half),
        ),
        out_shape=(out, out),
        compiler_params=PARAMS,
        name="last_own",
    )(side, terms, *path, force, speed)


def last_join_kernel(side_ref, here, speed, moved_in, speed_in, moved, new_ref):
    def one(p, carry):
        for axis in range(3):
            new = speed[axis, p]
            new_ref[axis, p] = new
            moved[axis, p] = here[axis, p] + time_step * new
        return carry

    over_planes(one, speed.shape[1], 4)


def last_join(side, region, here, speed, moved, speeds):
    rows = speed.shape[1]
    chunk = rows // JOIN_STEPS
    first = region * JOIN_STEPS
    block = pl.BlockSpec((3, chunk, 8, 128), lambda t, side_ref: (0, t, 0, 0))
    here_block = pl.BlockSpec((3, chunk, 8, 128), lambda t, side_ref: (0, first + t, 0, 0))
    half = pl.BlockSpec(
        (3, chunk, 8, 128),
        lambda t, side_ref: (0, (1 - side_ref[0]) * REGIONS * JOIN_STEPS + first + t, 0, 0),
    )
    out = jax.ShapeDtypeStruct(moved.shape, jnp.float32)
    whole = pl.BlockSpec(memory_space=pl.ANY)
    return pl.pallas_call(
        last_join_kernel,
        grid_spec=pltpu.PrefetchScalarGridSpec(
            num_scalar_prefetch=1,
            grid=(JOIN_STEPS,),
            in_specs=[here_block, block, whole, whole],
            out_specs=(half, half),
        ),
        out_shape=(out, out),
        input_output_aliases={3: 0, 4: 1},
        compiler_params=PARAMS,
        name="last_join",
    )(side, here, speed, moved, speeds)


def cut_kernel(blocks, squares, side_ref, *refs):
    count = len(blocks)
    source, outs, sems = refs[0], refs[1 : 1 + count], refs[-1]
    copies = []
    for k, out in enumerate(outs):
        at = 0
        for start, size in blocks[k]:
            rows = source.at[:, pl.ds(at_side(start, side_ref), size)]
            copies.append(
                pltpu.make_async_copy(rows, out.at[:, pl.ds(at, size)], sems.at[len(copies)])
            )
            at += size
    for copy in copies:
        copy.start()
    for copy in copies:
        copy.wait()
    if squares:

        def one(p, total):
            return total + sum(source[axis, p] * source[axis, p] for axis in range(3))

        refs[1 + count][...] = over_planes(one, source.shape[1], 4, jnp.zeros((8, 128), jnp.float32))


def at_side(pair, side_ref):
    even, odd = pair
    return even if even == odd else even + (odd - even) * side_ref[0]


def cut(side, array, blocks, squares=False):
    count = len(blocks)
    sizes = [sum(size for _, size in block) for block in blocks]
    return pl.pallas_call(
        functools.partial(cut_kernel, blocks, squares),
        out_shape=tuple(jax.ShapeDtypeStruct((3, size, 8, 128), jnp.float32) for size in sizes)
        + (TILE,) * squares,
        in_specs=[SMEM, VMEM if squares else pl.BlockSpec(memory_space=pltpu.HBM)],
        out_specs=(VMEM,) * (count + squares),
        scratch_shapes=[pltpu.SemaphoreType.DMA((sum(len(block) for block in blocks),))],
        compiler_params=PARAMS,
        name="cut",
    )(side, array)


def local(displacement, velocity):
    planes = displacement.shape[2] // (SIDE * SIDE)
    half = planes // 2
    images, slabs = lax.axis_size("image"), lax.axis_size("domain")
    both = ("image", "domain")
    own_image = lax.axis_index("image").astype(jnp.int32)
    side = own_image % 2
    image_arg, side_arg = own_image.reshape(1), side.reshape(1)
    slab = displacement.reshape(3, planes, 8, 128)
    slab_speed = velocity.reshape(3, planes, 8, 128)

    def at(image, domain):
        return image * slabs + domain % slabs

    everyone = [(i, d) for i in range(images) for d in range(slabs)]
    outward = [(at(i, d), at(i, d + 1 - 2 * (i % 2))) for i, d in everyone]
    across = [(i, i ^ 1) for i in range(images)]
    own_out = [(i, i - 2 + 4 * (i % 2)) for i in range(images)]
    own_out = [(a, b) for a, b in own_out if 0 <= b < images]
    partner_out = [(b, a) for a, b in own_out]
    upward = [(at(i, d), at(i ^ 1, d + i % 2)) for i, d in everyone]
    downward = [(b, a) for a, b in upward]

    end, top = planes - HALO, half + HALO
    piece = PIECES[0]
    outer, inner = (0, top), (top, 0)
    edge_own, near_inner, own, lead, rest = cut(
        side_arg,
        slab,
        (
            (((end, 0), HALO),),
            (((half, half - HALO), HALO),),
            (((0, half), half),),
            (((half, 0), piece), ((half - HALO, half), HALO), ((0, end), HALO)),
            (((half + piece, piece), PIECES[1]),),
        ),
    )
    partner = [lax.ppermute(part, "image", across) for part in (lead, rest)]
    beyond_own = lax.ppermute(own, "image", own_out)
    edges = jnp.concatenate([edge_own, partner[0][:, piece + HALO :]], axis=1)
    halo = lax.ppermute(edges, both, outward)
    beyond_partner = [lax.ppermute(part, "image", partner_out) for part in partner]
    own_source = (
        (own, None, 0, half, (HALO, HALO)),
        (halo, None, 0, HALO, outer),
        (near_inner, None, 0, HALO, inner),
    )
    partner_source = (
        (partner[0], None, 0, piece, (HALO, HALO)),
        (partner[0], None, piece, HALO, inner),
        (partner[1], None, 0, PIECES[1], (HALO + piece,) * 2),
        (halo, None, HALO, HALO, outer),
    )
    forces, energies = image_forces(side_arg, half, (own_source, partner_source))
    far_speed, slab_sq = cut(side_arg, slab_speed, ((((half, 0), half),),), True)
    far_speed, *_ = lax.optimization_barrier((far_speed, halo, beyond_partner[0], beyond_own))
    partner_speed = lax.ppermute(far_speed, "image", across)

    path = (beyond_partner, [own], partner, [beyond_own])
    speeds = (slab_speed, partner_speed)
    speed_sq = (slab_sq, jnp.zeros_like(slab_sq))
    for step_index in range(FIRE_STEPS):
        if step_index > 0:
            forces, energies = image_forces(side_arg, half, sources)
        payload = moments(side_arg, path, forces, energies, speed_sq, images * slabs)
        gathered = lax.all_to_all(payload, both, 0, 0, tiled=True)
        if step_index == FIRE_STEPS - 1:
            break
        moved, speeds, tops, bottoms, speed_sq = update(
            image_arg, gathered, path, forces, *speeds, images
        )
        low = lax.ppermute(tops, both, upward)
        high = lax.ppermute(bottoms, both, downward)
        sources = [
            (
                (moved[j], None, 0, half, (HALO, HALO)),
                (low, 1 - j, 0, HALO, (0, 0)),
                (high, 1 - j, 0, HALO, (top, top)),
            )
            for j in range(2)
        ]
        path = (
            [lax.ppermute(moved[1], "image", partner_out)],
            [moved[0]],
            [moved[1]],
            [lax.ppermute(moved[0], "image", own_out)],
        )
        back_home, _, _ = lax.optimization_barrier((moved[1], low, high))
        returned = lax.ppermute(back_home, "image", across)
    whole = [pieces[0] for pieces in path]
    *last_speeds, terms = last_partner(
        image_arg, gathered, whole[1:], forces[1], speeds[1], images
    )
    last_speeds = [lax.ppermute(part, "image", across) for part in last_speeds]
    moved, new_speeds = last_own(side_arg, terms, whole[:3], forces[0], speeds[0])
    for region, part in enumerate(last_speeds):
        moved, new_speeds = last_join(side_arg, region, returned, part, moved, new_speeds)
    return (moved.reshape(displacement.shape), new_speeds.reshape(velocity.shape))


def solution(mesh):
    spec = P("image", None, "domain")
    return jax.shard_map(
        local,
        mesh=mesh,
        in_specs=(spec, spec),
        out_specs=(spec, spec),
        check_vma=False,
    )
```

```python
import functools
import math

import jax
import jax.numpy as jnp
from jax import lax
from jax.experimental import pallas as pl
from jax.experimental.pallas import tpu as pltpu
from jax.sharding import PartitionSpec as P

SIDE = 32
FIRE_STEPS = 2
QUANTITIES = 8
HALO = 2
EMBED_UNROLL = 48
FINISH_UNROLL = 16
REGIONS = 2
PIECES = (24, 24)
JOIN_STEPS = 2

lattice_const = 3.615
cutoff_sq = 9.61
nearest_sq = 6.533136
pair_scale = 30.0
pair_depth = 0.3
embed_scale = 1.2
bulk_root = 3.605551275463989
spring_const = 2.0
time_step = 0.1
fire_mixing = 0.1
stabilizer = 1e-06

reach_root = math.sqrt(cutoff_sq)
unit_half = 0.5 * lattice_const / reach_root
kappa = cutoff_sq / nearest_sq
dens_shift = (2.0 - kappa) / kappa
pair_shift = (2.5 - 2.0 * kappa) / (2.0 * kappa)
dens_scale = pair_scale * kappa
pair_energy_scale = pair_scale * pair_depth * 2.0 * kappa
dens_slope_shift = 0.75 * dens_shift
pair_slope_shift = 0.75 * pair_shift
dens_slope_scale = -4.0 * dens_scale / cutoff_sq
pair_slope_scale = -4.0 * pair_energy_scale / cutoff_sq
slope_ratio = dens_slope_scale / pair_slope_scale
force_scale = 2.0 * pair_slope_scale * reach_root


def shift(field, step_u, step_v, lanes):
    reach = step_u * SIDE + step_v
    turned = pltpu.roll(field, (-reach) % 128, 1)
    if step_u == 0:
        return turned
    carried = pltpu.roll(turned, (-step_u) % 8, 0)
    return jnp.where(lanes >= 128 - reach if reach > 0 else lanes < -reach, carried, turned)


def partners(field, step, lanes):
    return (
        shift(field, 0, step, lanes),
        shift(field, step, 0, lanes),
        shift(field, step, step, lanes),
    )


def gather_back(at_v, at_u, at_uv, step, lanes):
    return (
        shift(at_v, 0, -step, lanes)
        + shift(at_u, -step, 0, lanes)
        + shift(at_uv, -step, -step, lanes)
    )


def limits(step, u, v):
    far = jnp.float32(-1e30)
    in_u = (u + step >= 0) & (u + step < SIDE)
    in_v = (v + step >= 0) & (v + step < SIDE)
    one = jnp.ones_like(u, jnp.float32)
    return (
        jnp.where(in_v, one, far),
        jnp.where(in_u, one, far),
        jnp.where(in_u & in_v, one, far),
    )


def side_of(plane):
    return 1 if plane % 2 == 0 else -1


def force_kernel(layouts, side_ref, *refs):
    count = sum(len(layout) for layout in layouts)
    images = len(layouts)
    arrays, outs, scratch = refs[:count], refs[count : count + 2 * images], refs[count + 2 * images :]
    at = 0
    for j, layout in enumerate(layouts):
        sources = [
            (ref if slot is None else ref.at[slot], row, size, at_side(start, side_ref))
            for ref, (slot, row, size, start) in zip(arrays[at:], layout)
        ]
        at += len(layout)
        slab_forces(sources, outs[2 * j], outs[2 * j + 1], *scratch)


def slab_forces(sources, force_ref, energy_ref, pos, turned, seps, slopes, rho, back, embed, force_back):
    f32 = jnp.float32
    planes = force_ref.shape[1]
    lanes = lax.broadcasted_iota(jnp.int32, (8, 128), 1)
    subl = lax.broadcasted_iota(jnp.int32, (8, 128), 0)
    site_u = subl * 4 + lanes // SIDE
    site_v = lanes % SIDE
    inverse = f32(1.0 / reach_root)
    zero = jnp.zeros((8, 128), f32)

    def place(q, side, values):
        for axis in range(3):
            value = values[axis] * inverse
            pos[axis, q] = value
            for k, seen in enumerate(partners(value, side, lanes)):
                turned[axis, k, q] = seen

    for source, row, size, start in sources:
        unroll = max(n for n in range(2, 25, 2) if size % n == 0)

        def place_some(t, carry, source=source, row=row, start=start, unroll=unroll):
            for j in range(unroll):
                p = t * unroll + j
                place(start + p, side_of(j), [source[axis, row + p] for axis in range(3)])
            return carry

        lax.fori_loop(0, size // unroll, place_some, 0)

    def separations(e, step):
        h = f32(unit_half)
        sh = f32(step * unit_half)
        own = [pos[axis, e] for axis in range(3)]
        nxt = [pos[axis, e + 1] for axis in range(3)]
        seen = [[turned[axis, k, e + 1] for k in range(3)] for axis in range(3)]
        own_x = own[0] - h
        y_of = (own[1] + sh, own[1], own[1] - sh)
        z_of = (own[2] - sh, own[2], own[2] + sh)
        cross = [
            (nxt[0] - own_x, nxt[1] - y_of[0], nxt[2] - z_of[1]),
            (seen[0][0] - own_x, seen[1][0] - y_of[1], seen[2][0] - z_of[2]),
            (seen[0][1] - own_x, seen[1][1] - y_of[1], seen[2][1] - z_of[0]),
            (seen[0][2] - own_x, seen[1][2] - y_of[2], seen[2][2] - z_of[1]),
        ]
        near_y = nxt[1] - sh
        near_zv = nxt[2] + sh
        near_zu = nxt[2] - sh
        inside = [
            (seen[0][0] - nxt[0], seen[1][0] - near_y, seen[2][0] - near_zv),
            (seen[0][1] - nxt[0], seen[1][1] - near_y, seen[2][1] - near_zu),
        ]
        return cross + inside

    def density(e, step, bounds, carry):
        rho_part, sum_f, sum_c = carry
        one = jnp.ones((8, 128), f32)
        tops = (one, bounds[0], bounds[1], bounds[2], bounds[0], bounds[1])
        dens, cubes = [], []
        for k, sep in enumerate(separations(e, step)):
            y = sep[0] * sep[0] + sep[1] * sep[1] + sep[2] * sep[2]
            c = jnp.maximum(tops[k] - y, 0.0)
            square = c * c
            cube = square * c
            dens.append(cube * (c + f32(dens_shift)))
            cubes.append(cube)
            for axis in range(3):
                seps[e, k, axis] = sep[axis]
            slopes[e, k, 0] = square * (c + f32(pair_slope_shift))
            slopes[e, k, 1] = square * (c + f32(dens_slope_shift))
        cross = (dens[0] + dens[1]) + (dens[2] + dens[3])
        inside = dens[4] + dens[5]
        rho[e] = rho_part + cross
        back[0, e + 1] = dens[1] + dens[4]
        back[1, e + 1] = dens[2] + dens[5]
        back[2, e + 1] = dens[3]
        weight = jnp.where((e >= 1) & (e <= planes), 1.0, 0.0).astype(f32)
        sum_f = sum_f + weight * (cross + inside)
        sum_c = sum_c + weight * (
            ((cubes[0] + cubes[1]) + (cubes[2] + cubes[3])) + (cubes[4] + cubes[5])
        )
        return (dens[0] + inside, sum_f, sum_c)

    down = limits(-1, site_u, site_v)
    up = limits(1, site_u, site_v)

    def density_pair(t, carry):
        carry = density(2 * t, -1, down, carry)
        return density(2 * t + 1, 1, up, carry)

    carry = lax.fori_loop(0, planes // 2 + 1, density_pair, (zero, zero, zero))
    _, sum_f, sum_c = density(planes + 2, -1, down, carry)

    def embedding(q, side):
        total = rho[q] + gather_back(back[0, q], back[1, q], back[2, q], side, lanes)
        w = 1.0 + f32(dens_scale) * total
        inv = lax.rsqrt(w)
        embed[0, q] = f32(-0.5 * embed_scale * slope_ratio) * inv
        return w * inv - f32(bulk_root)

    embedding(1, side_of(1))
    embedding(planes + HALO, side_of(0))

    def embed_some(t, total):
        for j in range(EMBED_UNROLL):
            total = total + embedding(HALO + t * EMBED_UNROLL + j, side_of(j))
        return total

    roots = lax.fori_loop(0, planes // EMBED_UNROLL, embed_some, zero)
    energy_ref[...] = f32(-embed_scale) * roots + f32(pair_energy_scale) * (
        sum_f + f32(pair_shift - dens_shift) * sum_c
    )

    def see(q, side):
        for k, seen in enumerate(partners(embed[0, q], side, lanes)):
            embed[1 + k, q] = seen

    see(planes + HALO, side_of(0))

    def see_some(t, carry):
        for j in range(EMBED_UNROLL):
            see(HALO + t * EMBED_UNROLL + j, side_of(j))
        return carry

    lax.fori_loop(0, planes // EMBED_UNROLL, see_some, 0)

    def force(e, keep, carry):
        own = embed[0, e]
        nxt = embed[0, e + 1]
        at_v, at_u, at_uv = [embed[1 + k, e + 1] for k in range(3)]
        partner = (own + nxt, own + at_v, own + at_u, own + at_uv, nxt + at_v, nxt + at_u)
        weight = [slopes[e, k, 0] + partner[k] * slopes[e, k, 1] for k in range(6)]
        out = []
        for axis in range(3):
            g = [weight[k] * seps[e, k, axis] for k in range(6)]
            if keep:
                force_ref[axis, e - HALO] = carry[axis] + ((g[0] + g[1]) + (g[2] + g[3]))
            force_back[axis, 0, e + 1] = g[1] + g[4]
            force_back[axis, 1, e + 1] = g[2] + g[5]
            force_back[axis, 2, e + 1] = g[3]
            out.append((g[4] + g[5]) - g[0])
        return tuple(out)

    def force_pair(t, carry):
        carry = force(HALO + 2 * t, True, carry)
        return force(HALO + 2 * t + 1, True, carry)

    lax.fori_loop(0, planes // 2, force_pair, force(1, False, (zero, zero, zero)))

    def finish(t, carry):
        for j in range(FINISH_UNROLL):
            p = t * FINISH_UNROLL + j
            for axis in range(3):
                parts = [force_back[axis, k, p + HALO] for k in range(3)]
                force_ref[axis, p] = f32(force_scale) * (
                    force_ref[axis, p] - gather_back(*parts, side_of(j), lanes)
                )
        return carry

    lax.fori_loop(0, planes // FINISH_UNROLL, finish, 0)


def image_forces(side, planes, images):
    vmem = pl.BlockSpec(memory_space=pltpu.VMEM)
    rows = planes + 2 * HALO
    arrays = [source[0] for sources in images for source in sources]
    layouts = [[source[1:] for source in sources] for sources in images]
    results = pl.pallas_call(
        functools.partial(force_kernel, layouts),
        out_shape=(
            jax.ShapeDtypeStruct((3, planes, 8, 128), jnp.float32),
            jax.ShapeDtypeStruct((8, 128), jnp.float32),
        )
        * len(images),
        in_specs=[pl.BlockSpec(memory_space=pltpu.SMEM)] + [vmem] * len(arrays),
        out_specs=(vmem,) * (2 * len(images)),
        scratch_shapes=[
            pltpu.VMEM((3, rows, 8, 128), jnp.float32),
            pltpu.VMEM((3, 3, rows, 8, 128), jnp.float32),
            pltpu.VMEM((rows, 6, 3, 8, 128), jnp.float32),
            pltpu.VMEM((rows, 6, 2, 8, 128), jnp.float32),
            pltpu.VMEM((rows, 8, 128), jnp.float32),
            pltpu.VMEM((3, rows, 8, 128), jnp.float32),
            pltpu.VMEM((4, rows, 8, 128), jnp.float32),
            pltpu.VMEM((3, 3, rows, 8, 128), jnp.float32),
        ],
        compiler_params=pltpu.CompilerParams(vmem_limit_bytes=20 * 1024 * 1024),
        cost_estimate=pl.CostEstimate(
            flops=40_000_000, bytes_accessed=30_000_000, transcendentals=0
        ),
        name="slab_forces",
    )(side, *arrays)
    return results[::2], results[1::2]


def total_of(tile):
    return jnp.sum(jnp.sum(tile, axis=0, keepdims=True), axis=1, keepdims=True)


def regions_of(path):
    at = 0
    for k, rows in enumerate(PIECES):
        yield at, rows, [(pieces[k], 0) if len(pieces) > 1 else (pieces[0], at) for pieces in path]
        at += rows


def over_planes(body, rows, unroll, carry=0):
    def some(t, carry):
        for j in range(unroll):
            carry = body(t * unroll + j, carry)
        return carry

    return lax.fori_loop(0, rows // unroll, some, carry)


def groups(refs, counts):
    out, at = [], 0
    for count in counts:
        out.append(refs[at : at + count])
        at += count
    return out, refs[at:]


def moment_kernel(counts, side_ref, *refs):
    path, refs = groups(refs, counts)
    forces, energies, speed_sq, out_ref = refs[:2], refs[2:4], refs[4:6], refs[6]
    zero = jnp.zeros((8, 128), jnp.float32)
    sums = (zero,) * 12
    for first, rows, held in regions_of(path):

        def one(p, carry):
            carry = list(carry)
            for axis in range(3):
                at = [ref[axis, start + p] for ref, start in held]
                diff = [at[j + 1] - at[j] for j in range(3)]
                square = [d * d for d in diff]
                for j in range(2):
                    force = forces[j][axis, first + p]
                    terms = (
                        force * force,
                        force * diff[j + 1],
                        force * diff[j],
                        square[j + 1],
                        square[j],
                        diff[j] * diff[j + 1],
                    )
                    for k, term in enumerate(terms):
                        carry[6 * j + k] = carry[6 * j + k] + term
            return tuple(carry)

        sums = over_planes(one, rows, 2, sums)

    lane = lax.broadcasted_iota(jnp.int32, (1, 128), 1)
    odd = side_ref[0] == 1
    sign = jnp.where(odd, -1.0, 1.0).astype(jnp.float32)
    row = jnp.zeros((1, 128), jnp.float32)
    for j in range(2):
        ahead = [total_of(sums[6 * j + k]) for k in range(6)]
        values = (
            total_of(energies[j][...]),
            ahead[0],
            sign * jnp.where(odd, ahead[2], ahead[1]),
            sign * jnp.where(odd, ahead[1], ahead[2]),
            jnp.where(odd, ahead[4], ahead[3]),
            jnp.where(odd, ahead[3], ahead[4]),
            ahead[5],
            total_of(speed_sq[j][...]),
        )
        for k, value in enumerate(values):
            row = row + jnp.where(lane == 8 * j + k, value, 0.0)
    out_ref[...] = jnp.broadcast_to(row, out_ref.shape)


VMEM = pl.BlockSpec(memory_space=pltpu.VMEM)
SMEM = pl.BlockSpec(memory_space=pltpu.SMEM)
PARAMS = pltpu.CompilerParams(vmem_limit_bytes=16 * 1024 * 1024)
TILE = jax.ShapeDtypeStruct((8, 128), jnp.float32)


def moments(side, path, forces, energies, speed_sq, copies):
    counts = [len(pieces) for pieces in path]
    arrays = [piece for pieces in path for piece in pieces] + [*forces, *energies, *speed_sq]
    return pl.pallas_call(
        functools.partial(moment_kernel, counts),
        out_shape=jax.ShapeDtypeStruct((copies, 128), jnp.float32),
        in_specs=[SMEM] + [VMEM] * len(arrays),
        out_specs=VMEM,
        compiler_params=PARAMS,
        name="path_moments",
    )(side, *arrays)


def path_terms(summary, images):
    lane = lax.broadcasted_iota(jnp.int32, (8, 128), 1)
    image = lax.broadcasted_iota(jnp.int32, (8, 128), 0)

    def column(k):
        picked = jnp.sum(jnp.where(lane == k, summary, 0.0), axis=1, keepdims=True)
        return jnp.broadcast_to(picked, (8, 128))

    e_here, ff, f_fwd, f_bwd, fwd_sq, bwd_sq, fwd_bwd, speed_sq = [column(k) for k in range(8)]
    e_prev = pltpu.roll(e_here, 1, 0)
    e_next = pltpu.roll(e_here, 7, 0)
    inner = (image > 0) & (image < images - 1)
    rise = e_next - e_here
    fall = e_here - e_prev
    larger = jnp.maximum(jnp.abs(rise), jnp.abs(fall))
    smaller = jnp.minimum(jnp.abs(rise), jnp.abs(fall))
    upward = (e_next > e_here) & (e_here > e_prev)
    downward = (e_next < e_here) & (e_here < e_prev)
    toward = e_next > e_prev
    weight_fwd = jnp.where(
        upward, 1.0, jnp.where(downward, 0.0, jnp.where(toward, larger, smaller))
    )
    weight_bwd = jnp.where(
        upward, 0.0, jnp.where(downward, 1.0, jnp.where(toward, smaller, larger))
    )
    tangent_sq = (
        weight_fwd * weight_fwd * fwd_sq
        + 2.0 * weight_fwd * weight_bwd * fwd_bwd
        + weight_bwd * weight_bwd * bwd_sq
    )
    norm_sq = tangent_sq + stabilizer
    force_tan = weight_fwd * f_fwd + weight_bwd * f_bwd
    spring = spring_const * (jnp.sqrt(fwd_sq + stabilizer) - jnp.sqrt(bwd_sq + stabilizer))
    coefficient = -force_tan / norm_sq + spring / jnp.sqrt(norm_sq)
    neb_sq = ff + 2.0 * coefficient * force_tan + coefficient * coefficient * tangent_sq

    def over_inner(value):
        return jnp.sum(jnp.where(inner, value, 0.0), axis=0, keepdims=True)

    force_norm = jnp.sqrt(over_inner(neb_sq) + stabilizer)
    speed_norm = jnp.sqrt(over_inner(speed_sq) + stabilizer)
    gain = jnp.broadcast_to(fire_mixing * (speed_norm / force_norm) + time_step, (8, 128))
    keep = jnp.where(inner, 1.0 - fire_mixing, 0.0)
    push = jnp.where(inner, gain, 0.0)
    along_fwd = jnp.where(inner, gain * coefficient * weight_fwd, 0.0)
    along_bwd = jnp.where(inner, gain * coefficient * weight_bwd, 0.0)
    return keep, push, along_fwd, along_bwd


def step_terms(image_ref, gathered_ref, images, terms):
    image = lax.broadcasted_iota(jnp.int32, (8, 128), 0)
    summary = jnp.zeros((8, 128), jnp.float32)
    slabs = gathered_ref.shape[0] // images
    for g in range(images):
        rows = gathered_ref[g * slabs : (g + 1) * slabs, :]
        row = jnp.broadcast_to(jnp.sum(rows, axis=0, keepdims=True), (8, 128))
        summary = summary + jnp.where(image == g, row, 0.0)
        summary = summary + jnp.where(image == (g ^ 1), pltpu.roll(row, 120, 1), 0.0)
    keep, push, along_fwd, along_bwd = path_terms(summary, images)
    here = image_ref[0]
    odd = here % 2 == 1
    values = (keep, push, jnp.where(odd, -along_bwd, along_fwd), jnp.where(odd, -along_fwd, along_bwd))
    for j in range(2):
        at = image == (here + j * (1 - 2 * (here % 2)))
        for k, value in enumerate(values):
            own = jnp.sum(jnp.where(at, value, 0.0), axis=0, keepdims=True)
            terms[j, k] = jnp.broadcast_to(own, (8, 128))


def new_speed(terms, j, speed, force, ahead, behind):
    return terms[j, 0] * speed + terms[j, 1] * force + terms[j, 2] * ahead + terms[j, 3] * behind


def update_kernel(counts, images, image_ref, gathered_ref, slab_speed, *refs):
    path, refs = groups(refs, counts)
    forces, partner_speed, moved, new_speeds = refs[:2], refs[2], refs[3:5], refs[5:7]
    tops, bottoms, speed_sq, (terms, own_speed, sem) = refs[7], refs[8], refs[9:11], refs[11:]
    speeds = (own_speed, partner_speed)
    half = own_speed.shape[1]
    copy = pltpu.make_async_copy(
        slab_speed.at[:, pl.ds(image_ref[0] % 2 * half, half)], own_speed, sem
    )
    copy.start()
    step_terms(image_ref, gathered_ref, images, terms)
    copy.wait()
    sums = (jnp.zeros((8, 128), jnp.float32),) * 2
    for first, rows, held in regions_of(path):

        def one(p, carry):
            carry = list(carry)
            for axis in range(3):
                at = [ref[axis, start + p] for ref, start in held]
                diff = [at[j + 1] - at[j] for j in range(3)]
                for j in range(2):
                    q = first + p
                    speed = new_speed(terms, j, speeds[j][axis, q], forces[j][axis, q], diff[j + 1], diff[j])
                    new_speeds[j][axis, q] = speed
                    moved[j][axis, q] = at[j + 1] + time_step * speed
                    carry[j] = carry[j] + speed * speed
            return tuple(carry)

        sums = over_planes(one, rows, 2, sums)
    speed_sq[0][...], speed_sq[1][...] = sums
    planes = moved[0].shape[1]
    for j in range(2):
        tops[j] = moved[j][:, planes - HALO :]
        bottoms[j] = moved[j][:, :HALO]


def update(image, gathered, path, forces, slab_speed, partner_speed, images):
    counts = [len(pieces) for pieces in path]
    arrays = [piece for pieces in path for piece in pieces] + [*forces, partner_speed]
    out = jax.ShapeDtypeStruct(forces[0].shape, jnp.float32)
    edge = jax.ShapeDtypeStruct((2, 3, HALO, 8, 128), jnp.float32)
    results = pl.pallas_call(
        functools.partial(update_kernel, counts, images),
        out_shape=(out,) * 4 + (edge,) * 2 + (TILE,) * 2,
        in_specs=[SMEM, VMEM, pl.BlockSpec(memory_space=pltpu.HBM)] + [VMEM] * len(arrays),
        out_specs=(VMEM,) * 8,
        scratch_shapes=[
            pltpu.VMEM((2, 4, 8, 128), jnp.float32),
            pltpu.VMEM(forces[0].shape, jnp.float32),
            pltpu.SemaphoreType.DMA,
        ],
        compiler_params=PARAMS,
        name="fire_update",
    )(image, gathered, slab_speed, *arrays)
    return results[:2], results[2:4], results[4], results[5], results[6:]


def last_partner_kernel(images, image_ref, gathered_ref, before, here, after, force, speed, *outs):
    parts, terms_ref = outs[:-1], outs[-1]
    step_terms(image_ref, gathered_ref, images, terms_ref)
    for region, part in enumerate(parts):
        rows = part.shape[1]

        def one(p, carry):
            q = region * rows + p
            for axis in range(3):
                at = here[axis, q]
                part[axis, p] = new_speed(
                    terms_ref, 1, speed[axis, q], force[axis, q], after[axis, q] - at, at - before[axis, q]
                )
            return carry

        over_planes(one, rows, 2)


def last_partner(image, gathered, path, force, speed, images):
    part = jax.ShapeDtypeStruct((3, force.shape[1] // REGIONS, 8, 128), jnp.float32)
    return pl.pallas_call(
        functools.partial(last_partner_kernel, images),
        out_shape=(part,) * REGIONS + (jax.ShapeDtypeStruct((2, 4, 8, 128), jnp.float32),),
        in_specs=[SMEM] + [VMEM] * 6,
        out_specs=(VMEM,) * (REGIONS + 1),
        compiler_params=PARAMS,
        name="last_partner",
    )(image, gathered, *path, force, speed)


def last_own_kernel(side_ref, terms, before, here, after, force, speed, moved, new_ref):
    def one(p, carry):
        for axis in range(3):
            at = here[axis, p]
            new = new_speed(
                terms, 0, speed[axis, p], force[axis, p], after[axis, p] - at, at - before[axis, p]
            )
            new_ref[axis, p] = new
            moved[axis, p] = at + time_step * new
        return carry

    over_planes(one, here.shape[1], 2)


def last_own(side, terms, path, force, speed):
    planes = force.shape[1]
    chunk = planes // REGIONS
    block = pl.BlockSpec((3, chunk, 8, 128), lambda t, side_ref: (0, t, 0, 0))
    half = pl.BlockSpec((3, chunk, 8, 128), lambda t, side_ref: (0, side_ref[0] * REGIONS + t, 0, 0))
    out = jax.ShapeDtypeStruct((3, 2 * planes, 8, 128), jnp.float32)
    return pl.pallas_call(
        last_own_kernel,
        grid_spec=pltpu.PrefetchScalarGridSpec(
            num_scalar_prefetch=1,
            grid=(REGIONS,),
            in_specs=[pl.BlockSpec((2, 4, 8, 128), lambda t, side_ref: (0, 0, 0, 0))] + [block] * 5,
            out_specs=(half, half),
        ),
        out_shape=(out, out),
        compiler_params=PARAMS,
        name="last_own",
    )(side, terms, *path, force, speed)


def last_join_kernel(side_ref, here, speed, moved_in, speed_in, moved, new_ref):
    def one(p, carry):
        for axis in range(3):
            new = speed[axis, p]
            new_ref[axis, p] = new
            moved[axis, p] = here[axis, p] + time_step * new
        return carry

    over_planes(one, speed.shape[1], 4)


def last_join(side, region, here, speed, moved, speeds):
    rows = speed.shape[1]
    chunk = rows // JOIN_STEPS
    first = region * JOIN_STEPS
    block = pl.BlockSpec((3, chunk, 8, 128), lambda t, side_ref: (0, t, 0, 0))
    here_block = pl.BlockSpec((3, chunk, 8, 128), lambda t, side_ref: (0, first + t, 0, 0))
    half = pl.BlockSpec(
        (3, chunk, 8, 128),
        lambda t, side_ref: (0, (1 - side_ref[0]) * REGIONS * JOIN_STEPS + first + t, 0, 0),
    )
    out = jax.ShapeDtypeStruct(moved.shape, jnp.float32)
    whole = pl.BlockSpec(memory_space=pl.ANY)
    return pl.pallas_call(
        last_join_kernel,
        grid_spec=pltpu.PrefetchScalarGridSpec(
            num_scalar_prefetch=1,
            grid=(JOIN_STEPS,),
            in_specs=[here_block, block, whole, whole],
            out_specs=(half, half),
        ),
        out_shape=(out, out),
        input_output_aliases={3: 0, 4: 1},
        compiler_params=PARAMS,
        name="last_join",
    )(side, here, speed, moved, speeds)


def cut_kernel(blocks, squares, side_ref, *refs):
    count = len(blocks)
    source, outs, sems = refs[0], refs[1 : 1 + count], refs[-1]
    copies = []
    for k, out in enumerate(outs):
        at = 0
        for start, size in blocks[k]:
            rows = source.at[:, pl.ds(at_side(start, side_ref), size)]
            copies.append(
                pltpu.make_async_copy(rows, out.at[:, pl.ds(at, size)], sems.at[len(copies)])
            )
            at += size
    for copy in copies:
        copy.start()
    for copy in copies:
        copy.wait()
    if squares:

        def one(p, total):
            return total + sum(source[axis, p] * source[axis, p] for axis in range(3))

        refs[1 + count][...] = over_planes(one, source.shape[1], 4, jnp.zeros((8, 128), jnp.float32))


def at_side(pair, side_ref):
    even, odd = pair
    return even if even == odd else even + (odd - even) * side_ref[0]


def cut(side, array, blocks, squares=False):
    count = len(blocks)
    sizes = [sum(size for _, size in block) for block in blocks]
    return pl.pallas_call(
        functools.partial(cut_kernel, blocks, squares),
        out_shape=tuple(jax.ShapeDtypeStruct((3, size, 8, 128), jnp.float32) for size in sizes)
        + (TILE,) * squares,
        in_specs=[SMEM, VMEM if squares else pl.BlockSpec(memory_space=pltpu.HBM)],
        out_specs=(VMEM,) * (count + squares),
        scratch_shapes=[pltpu.SemaphoreType.DMA((sum(len(block) for block in blocks),))],
        compiler_params=PARAMS,
        name="cut",
    )(side, array)


def local(displacement, velocity):
    planes = displacement.shape[2] // (SIDE * SIDE)
    half = planes // 2
    images, slabs = lax.axis_size("image"), lax.axis_size("domain")
    both = ("image", "domain")
    own_image = lax.axis_index("image").astype(jnp.int32)
    side = own_image % 2
    image_arg, side_arg = own_image.reshape(1), side.reshape(1)
    slab = displacement.reshape(3, planes, 8, 128)
    slab_speed = velocity.reshape(3, planes, 8, 128)

    def at(image, domain):
        return image * slabs + domain % slabs

    everyone = [(i, d) for i in range(images) for d in range(slabs)]
    outer_own = [(at(i, d), at(i, d + 1 - 2 * (i % 2))) for i, d in everyone]
    outer_partner = [(at(i, d), at(i ^ 1, d - 1 + 2 * (i % 2))) for i, d in everyone]
    across = [(i, i ^ 1) for i in range(images)]
    own_out = [(i, i - 2 + 4 * (i % 2)) for i in range(images)]
    own_out = [(a, b) for a, b in own_out if 0 <= b < images]
    partner_out = [(b, a) for a, b in own_out]
    upward = [(at(i, d), at(i ^ 1, d + i % 2)) for i, d in everyone]
    downward = [(b, a) for a, b in upward]

    end, top = planes - HALO, half + HALO
    piece = PIECES[0]
    outer, inner = (0, top), (top, 0)
    edge_own, edge_partner, near_inner, own, lead, rest = cut(
        side_arg,
        slab,
        (
            (((end, 0), HALO),),
            (((0, end), HALO),),
            (((half, half - HALO), HALO),),
            (((0, half), half),),
            (((half, 0), piece), ((half - HALO, half), HALO)),
            (((half + piece, piece), PIECES[1]),),
        ),
    )
    halo_own = lax.ppermute(edge_own, both, outer_own)
    halo_partner = lax.ppermute(edge_partner, both, outer_partner)
    rest, halo_own, halo_partner = lax.optimization_barrier(
        (rest, halo_own, halo_partner)
    )
    partner = [lax.ppermute(part, "image", across) for part in (lead, rest)]
    beyond_own = lax.ppermute(own, "image", own_out)
    beyond_partner = [lax.ppermute(part, "image", partner_out) for part in partner]
    own_source = (
        (own, None, 0, half, (HALO, HALO)),
        (halo_own, None, 0, HALO, outer),
        (near_inner, None, 0, HALO, inner),
    )
    partner_source = (
        (partner[0], None, 0, piece, (HALO, HALO)),
        (partner[0], None, piece, HALO, inner),
        (partner[1], None, 0, PIECES[1], (HALO + piece,) * 2),
        (halo_partner, None, 0, HALO, outer),
    )
    forces, energies = image_forces(side_arg, half, (own_source, partner_source))
    far_speed, slab_sq = cut(side_arg, slab_speed, ((((half, 0), half),),), True)
    far_speed, *_ = lax.optimization_barrier((far_speed, partner[0]))
    partner_speed = lax.ppermute(far_speed, "image", across)

    path = (beyond_partner, [own], partner, [beyond_own])
    speeds = (slab_speed, partner_speed)
    speed_sq = (slab_sq, jnp.zeros_like(slab_sq))
    for step_index in range(FIRE_STEPS):
        if step_index > 0:
            forces, energies = image_forces(side_arg, half, sources)
        payload = moments(side_arg, path, forces, energies, speed_sq, images * slabs)
        gathered = lax.all_to_all(payload, both, 0, 0, tiled=True)
        if step_index == FIRE_STEPS - 1:
            break
        moved, speeds, tops, bottoms, speed_sq = update(
            image_arg, gathered, path, forces, *speeds, images
        )
        low = lax.ppermute(tops, both, upward)
        high = lax.ppermute(bottoms, both, downward)
        sources = [
            (
                (moved[j], None, 0, half, (HALO, HALO)),
                (low, 1 - j, 0, HALO, (0, 0)),
                (high, 1 - j, 0, HALO, (top, top)),
            )
            for j in range(2)
        ]
        path = (
            [lax.ppermute(moved[1], "image", partner_out)],
            [moved[0]],
            [moved[1]],
            [lax.ppermute(moved[0], "image", own_out)],
        )
        back_home, _, _ = lax.optimization_barrier((moved[1], low, high))
        returned = lax.ppermute(back_home, "image", across)
    whole = [pieces[0] for pieces in path]
    *last_speeds, terms = last_partner(
        image_arg, gathered, whole[1:], forces[1], speeds[1], images
    )
    last_speeds = [lax.ppermute(part, "image", across) for part in last_speeds]
    moved, new_speeds = last_own(side_arg, terms, whole[:3], forces[0], speeds[0])
    for region, part in enumerate(last_speeds):
        moved, new_speeds = last_join(side_arg, region, returned, part, moved, new_speeds)
    return (moved.reshape(displacement.shape), new_speeds.reshape(velocity.shape))


def solution(mesh):
    spec = P("image", None, "domain")
    return jax.shard_map(
        local,
        mesh=mesh,
        in_specs=(spec, spec),
        out_specs=(spec, spec),
        check_vma=False,
    )
```

```python
import functools
import math

import jax
import jax.numpy as jnp
from jax import lax
from jax.experimental import pallas as pl
from jax.experimental.pallas import tpu as pltpu
from jax.sharding import PartitionSpec as P

SIDE = 32
FIRE_STEPS = 2
QUANTITIES = 8
HALO = 2
REGIONS = 2
PIECES = (24, 24)
JOIN_STEPS = 2

lattice_const = 3.615
cutoff_sq = 9.61
nearest_sq = 6.533136
pair_scale = 30.0
pair_depth = 0.3
embed_scale = 1.2
bulk_root = 3.605551275463989
spring_const = 2.0
time_step = 0.1
fire_mixing = 0.1
stabilizer = 1e-06

reach_root = math.sqrt(cutoff_sq)
unit_half = 0.5 * lattice_const / reach_root
kappa = cutoff_sq / nearest_sq
dens_shift = (2.0 - kappa) / kappa
pair_shift = (2.5 - 2.0 * kappa) / (2.0 * kappa)
dens_scale = pair_scale * kappa
pair_energy_scale = pair_scale * pair_depth * 2.0 * kappa
dens_slope_shift = 0.75 * dens_shift
pair_slope_shift = 0.75 * pair_shift
dens_slope_scale = -4.0 * dens_scale / cutoff_sq
pair_slope_scale = -4.0 * pair_energy_scale / cutoff_sq
slope_ratio = dens_slope_scale / pair_slope_scale
force_scale = 2.0 * pair_slope_scale * reach_root


def shift(field, step_u, step_v, lanes):
    reach = step_u * SIDE + step_v
    turned = pltpu.roll(field, (-reach) % 128, 1)
    if step_u == 0:
        return turned
    carried = pltpu.roll(turned, (-step_u) % 8, 0)
    return jnp.where(lanes >= 128 - reach if reach > 0 else lanes < -reach, carried, turned)


def partners(field, step, lanes):
    return (
        shift(field, 0, step, lanes),
        shift(field, step, 0, lanes),
        shift(field, step, step, lanes),
    )


def gather_back(at_v, at_u, at_uv, step, lanes):
    return (
        shift(at_v, 0, -step, lanes)
        + shift(at_u, -step, 0, lanes)
        + shift(at_uv, -step, -step, lanes)
    )


def limits(step, u, v):
    far = jnp.float32(-1e30)
    in_u = (u + step >= 0) & (u + step < SIDE)
    in_v = (v + step >= 0) & (v + step < SIDE)
    one = jnp.ones_like(u, jnp.float32)
    return (
        jnp.where(in_v, one, far),
        jnp.where(in_u, one, far),
        jnp.where(in_u & in_v, one, far),
    )


def side_of(plane):
    return 1 if plane % 2 == 0 else -1


def force_kernel(layouts, side_ref, *refs):
    count = sum(len(layout) for layout in layouts)
    images = len(layouts)
    arrays, outs, scratch = refs[:count], refs[count : count + 2 * images], refs[count + 2 * images :]
    at = 0
    for j, layout in enumerate(layouts):
        sources = [
            (ref if slot is None else ref.at[slot], row, size, at_side(start, side_ref))
            for ref, (slot, row, size, start) in zip(arrays[at:], layout)
        ]
        at += len(layout)
        slab_forces(sources, outs[2 * j], outs[2 * j + 1], *scratch)


def slab_forces(sources, force_ref, energy_ref, pos, turned, seps, slopes, rho, back, embed, force_back):
    f32 = jnp.float32
    planes = force_ref.shape[1]
    lanes = lax.broadcasted_iota(jnp.int32, (8, 128), 1)
    subl = lax.broadcasted_iota(jnp.int32, (8, 128), 0)
    site_u = subl * 4 + lanes // SIDE
    site_v = lanes % SIDE
    inverse = f32(1.0 / reach_root)
    zero = jnp.zeros((8, 128), f32)

    def place(q, side, values):
        for axis in range(3):
            value = values[axis] * inverse
            pos[axis, q] = value
            for k, seen in enumerate(partners(value, side, lanes)):
                turned[axis, k, q] = seen

    for source, row, size, start in sources:
        unroll = max(n for n in range(2, 25, 2) if size % n == 0)

        def place_some(t, carry, source=source, row=row, start=start, unroll=unroll):
            for j in range(unroll):
                p = t * unroll + j
                place(start + p, side_of(j), [source[axis, row + p] for axis in range(3)])
            return carry

        lax.fori_loop(0, size // unroll, place_some, 0)

    def separations(e, step):
        h = f32(unit_half)
        sh = f32(step * unit_half)
        own = [pos[axis, e] for axis in range(3)]
        nxt = [pos[axis, e + 1] for axis in range(3)]
        seen = [[turned[axis, k, e + 1] for k in range(3)] for axis in range(3)]
        own_x = own[0] - h
        y_of = (own[1] + sh, own[1], own[1] - sh)
        z_of = (own[2] - sh, own[2], own[2] + sh)
        cross = [
            (nxt[0] - own_x, nxt[1] - y_of[0], nxt[2] - z_of[1]),
            (seen[0][0] - own_x, seen[1][0] - y_of[1], seen[2][0] - z_of[2]),
            (seen[0][1] - own_x, seen[1][1] - y_of[1], seen[2][1] - z_of[0]),
            (seen[0][2] - own_x, seen[1][2] - y_of[2], seen[2][2] - z_of[1]),
        ]
        near_y = nxt[1] - sh
        near_zv = nxt[2] + sh
        near_zu = nxt[2] - sh
        inside = [
            (seen[0][0] - nxt[0], seen[1][0] - near_y, seen[2][0] - near_zv),
            (seen[0][1] - nxt[0], seen[1][1] - near_y, seen[2][1] - near_zu),
        ]
        return cross + inside

    def density(e, step, bounds, carry):
        rho_part, sum_f, sum_c = carry
        one = jnp.ones((8, 128), f32)
        tops = (one, bounds[0], bounds[1], bounds[2], bounds[0], bounds[1])
        dens, cubes = [], []
        for k, sep in enumerate(separations(e, step)):
            y = sep[0] * sep[0] + sep[1] * sep[1] + sep[2] * sep[2]
            c = jnp.maximum(tops[k] - y, 0.0)
            square = c * c
            cube = square * c
            dens.append(cube * (c + f32(dens_shift)))
            cubes.append(cube)
            for axis in range(3):
                seps[e, k, axis] = sep[axis]
            slopes[e, k, 0] = square * (c + f32(pair_slope_shift))
            slopes[e, k, 1] = square * (c + f32(dens_slope_shift))
        cross = (dens[0] + dens[1]) + (dens[2] + dens[3])
        inside = dens[4] + dens[5]
        rho[e] = rho_part + cross
        back[0, e + 1] = dens[1] + dens[4]
        back[1, e + 1] = dens[2] + dens[5]
        back[2, e + 1] = dens[3]
        if 1 <= e <= planes:
            sum_f = sum_f + (cross + inside)
            sum_c = sum_c + (((cubes[0] + cubes[1]) + (cubes[2] + cubes[3])) + (cubes[4] + cubes[5]))
        return (dens[0] + inside, sum_f, sum_c)

    down = limits(-1, site_u, site_v)
    up = limits(1, site_u, site_v)

    carry = (zero, zero, zero)
    for e in range(planes + 2 * HALO - 1):
        carry = density(e, (-1, 1)[e % 2], (down, up)[e % 2], carry)
    _, sum_f, sum_c = carry

    def embedding(q, side):
        total = rho[q] + gather_back(back[0, q], back[1, q], back[2, q], side, lanes)
        w = 1.0 + f32(dens_scale) * total
        inv = lax.rsqrt(w)
        embed[0, q] = f32(-0.5 * embed_scale * slope_ratio) * inv
        return w * inv - f32(bulk_root)

    embedding(1, side_of(1))
    embedding(planes + HALO, side_of(0))

    roots = zero
    for q in range(HALO, HALO + planes):
        roots = roots + embedding(q, side_of(q))
    energy_ref[...] = f32(-embed_scale) * roots + f32(pair_energy_scale) * (
        sum_f + f32(pair_shift - dens_shift) * sum_c
    )

    def see(q, side):
        for k, seen in enumerate(partners(embed[0, q], side, lanes)):
            embed[1 + k, q] = seen

    for q in range(HALO, HALO + planes + 1):
        see(q, side_of(q))

    def force(e, keep, carry):
        own = embed[0, e]
        nxt = embed[0, e + 1]
        at_v, at_u, at_uv = [embed[1 + k, e + 1] for k in range(3)]
        partner = (own + nxt, own + at_v, own + at_u, own + at_uv, nxt + at_v, nxt + at_u)
        weight = [slopes[e, k, 0] + partner[k] * slopes[e, k, 1] for k in range(6)]
        out = []
        for axis in range(3):
            g = [weight[k] * seps[e, k, axis] for k in range(6)]
            if keep:
                force_ref[axis, e - HALO] = carry[axis] + ((g[0] + g[1]) + (g[2] + g[3]))
            force_back[axis, 0, e + 1] = g[1] + g[4]
            force_back[axis, 1, e + 1] = g[2] + g[5]
            force_back[axis, 2, e + 1] = g[3]
            out.append((g[4] + g[5]) - g[0])
        return tuple(out)

    carry = force(1, False, (zero, zero, zero))
    for e in range(HALO, HALO + planes):
        carry = force(e, True, carry)

    for p in range(planes):
        for axis in range(3):
            parts = [force_back[axis, k, p + HALO] for k in range(3)]
            force_ref[axis, p] = f32(force_scale) * (
                force_ref[axis, p] - gather_back(*parts, side_of(p), lanes)
            )


def image_forces(side, planes, images):
    vmem = pl.BlockSpec(memory_space=pltpu.VMEM)
    rows = planes + 2 * HALO
    arrays = [source[0] for sources in images for source in sources]
    layouts = [[source[1:] for source in sources] for sources in images]
    results = pl.pallas_call(
        functools.partial(force_kernel, layouts),
        out_shape=(
            jax.ShapeDtypeStruct((3, planes, 8, 128), jnp.float32),
            jax.ShapeDtypeStruct((8, 128), jnp.float32),
        )
        * len(images),
        in_specs=[pl.BlockSpec(memory_space=pltpu.SMEM)] + [vmem] * len(arrays),
        out_specs=(vmem,) * (2 * len(images)),
        scratch_shapes=[
            pltpu.VMEM((3, rows, 8, 128), jnp.float32),
            pltpu.VMEM((3, 3, rows, 8, 128), jnp.float32),
            pltpu.VMEM((rows, 6, 3, 8, 128), jnp.float32),
            pltpu.VMEM((rows, 6, 2, 8, 128), jnp.float32),
            pltpu.VMEM((rows, 8, 128), jnp.float32),
            pltpu.VMEM((3, rows, 8, 128), jnp.float32),
            pltpu.VMEM((4, rows, 8, 128), jnp.float32),
            pltpu.VMEM((3, 3, rows, 8, 128), jnp.float32),
        ],
        compiler_params=pltpu.CompilerParams(vmem_limit_bytes=20 * 1024 * 1024),
        cost_estimate=pl.CostEstimate(
            flops=40_000_000, bytes_accessed=30_000_000, transcendentals=0
        ),
        name="slab_forces",
    )(side, *arrays)
    return results[::2], results[1::2]


def total_of(tile):
    return jnp.sum(jnp.sum(tile, axis=0, keepdims=True), axis=1, keepdims=True)


def regions_of(path):
    at = 0
    for k, rows in enumerate(PIECES):
        yield at, rows, [(pieces[k], 0) if len(pieces) > 1 else (pieces[0], at) for pieces in path]
        at += rows


def over_planes(body, rows, unroll, carry=0):
    def some(t, carry):
        for j in range(unroll):
            carry = body(t * unroll + j, carry)
        return carry

    return lax.fori_loop(0, rows // unroll, some, carry)


def groups(refs, counts):
    out, at = [], 0
    for count in counts:
        out.append(refs[at : at + count])
        at += count
    return out, refs[at:]


def moment_kernel(counts, side_ref, *refs):
    path, refs = groups(refs, counts)
    forces, energies, speed_sq, out_ref = refs[:2], refs[2:4], refs[4:6], refs[6]
    zero = jnp.zeros((8, 128), jnp.float32)
    sums = (zero,) * 12
    for first, rows, held in regions_of(path):

        def one(p, carry):
            carry = list(carry)
            for axis in range(3):
                at = [ref[axis, start + p] for ref, start in held]
                diff = [at[j + 1] - at[j] for j in range(3)]
                square = [d * d for d in diff]
                for j in range(2):
                    force = forces[j][axis, first + p]
                    terms = (
                        force * force,
                        force * diff[j + 1],
                        force * diff[j],
                        square[j + 1],
                        square[j],
                        diff[j] * diff[j + 1],
                    )
                    for k, term in enumerate(terms):
                        carry[6 * j + k] = carry[6 * j + k] + term
            return tuple(carry)

        sums = over_planes(one, rows, 2, sums)

    lane = lax.broadcasted_iota(jnp.int32, (1, 128), 1)
    odd = side_ref[0] == 1
    sign = jnp.where(odd, -1.0, 1.0).astype(jnp.float32)
    row = jnp.zeros((1, 128), jnp.float32)
    for j in range(2):
        ahead = [total_of(sums[6 * j + k]) for k in range(6)]
        values = (
            total_of(energies[j][...]),
            ahead[0],
            sign * jnp.where(odd, ahead[2], ahead[1]),
            sign * jnp.where(odd, ahead[1], ahead[2]),
            jnp.where(odd, ahead[4], ahead[3]),
            jnp.where(odd, ahead[3], ahead[4]),
            ahead[5],
            total_of(speed_sq[j][...]),
        )
        for k, value in enumerate(values):
            row = row + jnp.where(lane == 8 * j + k, value, 0.0)
    out_ref[...] = jnp.broadcast_to(row, out_ref.shape)


VMEM = pl.BlockSpec(memory_space=pltpu.VMEM)
SMEM = pl.BlockSpec(memory_space=pltpu.SMEM)
PARAMS = pltpu.CompilerParams(vmem_limit_bytes=16 * 1024 * 1024)
TILE = jax.ShapeDtypeStruct((8, 128), jnp.float32)


def moments(side, path, forces, energies, speed_sq, copies):
    counts = [len(pieces) for pieces in path]
    arrays = [piece for pieces in path for piece in pieces] + [*forces, *energies, *speed_sq]
    return pl.pallas_call(
        functools.partial(moment_kernel, counts),
        out_shape=jax.ShapeDtypeStruct((copies, 128), jnp.float32),
        in_specs=[SMEM] + [VMEM] * len(arrays),
        out_specs=VMEM,
        compiler_params=PARAMS,
        name="path_moments",
    )(side, *arrays)


def path_terms(summary, images):
    lane = lax.broadcasted_iota(jnp.int32, (8, 128), 1)
    image = lax.broadcasted_iota(jnp.int32, (8, 128), 0)

    def column(k):
        picked = jnp.sum(jnp.where(lane == k, summary, 0.0), axis=1, keepdims=True)
        return jnp.broadcast_to(picked, (8, 128))

    e_here, ff, f_fwd, f_bwd, fwd_sq, bwd_sq, fwd_bwd, speed_sq = [column(k) for k in range(8)]
    e_prev = pltpu.roll(e_here, 1, 0)
    e_next = pltpu.roll(e_here, 7, 0)
    inner = (image > 0) & (image < images - 1)
    rise = e_next - e_here
    fall = e_here - e_prev
    larger = jnp.maximum(jnp.abs(rise), jnp.abs(fall))
    smaller = jnp.minimum(jnp.abs(rise), jnp.abs(fall))
    upward = (e_next > e_here) & (e_here > e_prev)
    downward = (e_next < e_here) & (e_here < e_prev)
    toward = e_next > e_prev
    weight_fwd = jnp.where(
        upward, 1.0, jnp.where(downward, 0.0, jnp.where(toward, larger, smaller))
    )
    weight_bwd = jnp.where(
        upward, 0.0, jnp.where(downward, 1.0, jnp.where(toward, smaller, larger))
    )
    tangent_sq = (
        weight_fwd * weight_fwd * fwd_sq
        + 2.0 * weight_fwd * weight_bwd * fwd_bwd
        + weight_bwd * weight_bwd * bwd_sq
    )
    norm_sq = tangent_sq + stabilizer
    force_tan = weight_fwd * f_fwd + weight_bwd * f_bwd
    spring = spring_const * (jnp.sqrt(fwd_sq + stabilizer) - jnp.sqrt(bwd_sq + stabilizer))
    coefficient = -force_tan / norm_sq + spring / jnp.sqrt(norm_sq)
    neb_sq = ff + 2.0 * coefficient * force_tan + coefficient * coefficient * tangent_sq

    def over_inner(value):
        return jnp.sum(jnp.where(inner, value, 0.0), axis=0, keepdims=True)

    force_norm = jnp.sqrt(over_inner(neb_sq) + stabilizer)
    speed_norm = jnp.sqrt(over_inner(speed_sq) + stabilizer)
    gain = jnp.broadcast_to(fire_mixing * (speed_norm / force_norm) + time_step, (8, 128))
    keep = jnp.where(inner, 1.0 - fire_mixing, 0.0)
    push = jnp.where(inner, gain, 0.0)
    along_fwd = jnp.where(inner, gain * coefficient * weight_fwd, 0.0)
    along_bwd = jnp.where(inner, gain * coefficient * weight_bwd, 0.0)
    return keep, push, along_fwd, along_bwd


def step_terms(image_ref, gathered_ref, images, terms):
    image = lax.broadcasted_iota(jnp.int32, (8, 128), 0)
    summary = jnp.zeros((8, 128), jnp.float32)
    slabs = gathered_ref.shape[0] // images
    for g in range(images):
        rows = gathered_ref[g * slabs : (g + 1) * slabs, :]
        row = jnp.broadcast_to(jnp.sum(rows, axis=0, keepdims=True), (8, 128))
        summary = summary + jnp.where(image == g, row, 0.0)
        summary = summary + jnp.where(image == (g ^ 1), pltpu.roll(row, 120, 1), 0.0)
    keep, push, along_fwd, along_bwd = path_terms(summary, images)
    here = image_ref[0]
    odd = here % 2 == 1
    values = (keep, push, jnp.where(odd, -along_bwd, along_fwd), jnp.where(odd, -along_fwd, along_bwd))
    for j in range(2):
        at = image == (here + j * (1 - 2 * (here % 2)))
        for k, value in enumerate(values):
            own = jnp.sum(jnp.where(at, value, 0.0), axis=0, keepdims=True)
            terms[j, k] = jnp.broadcast_to(own, (8, 128))


def new_speed(terms, j, speed, force, ahead, behind):
    return terms[j, 0] * speed + terms[j, 1] * force + terms[j, 2] * ahead + terms[j, 3] * behind


def update_kernel(counts, images, image_ref, gathered_ref, slab_speed, *refs):
    path, refs = groups(refs, counts)
    forces, partner_speed, moved, new_speeds = refs[:2], refs[2], refs[3:5], refs[5:7]
    tops, bottoms, speed_sq, (terms, own_speed, sem) = refs[7], refs[8], refs[9:11], refs[11:]
    speeds = (own_speed, partner_speed)
    half = own_speed.shape[1]
    copy = pltpu.make_async_copy(
        slab_speed.at[:, pl.ds(image_ref[0] % 2 * half, half)], own_speed, sem
    )
    copy.start()
    step_terms(image_ref, gathered_ref, images, terms)
    copy.wait()
    sums = (jnp.zeros((8, 128), jnp.float32),) * 2
    for first, rows, held in regions_of(path):

        def one(p, carry):
            carry = list(carry)
            for axis in range(3):
                at = [ref[axis, start + p] for ref, start in held]
                diff = [at[j + 1] - at[j] for j in range(3)]
                for j in range(2):
                    q = first + p
                    speed = new_speed(terms, j, speeds[j][axis, q], forces[j][axis, q], diff[j + 1], diff[j])
                    new_speeds[j][axis, q] = speed
                    moved[j][axis, q] = at[j + 1] + time_step * speed
                    carry[j] = carry[j] + speed * speed
            return tuple(carry)

        sums = over_planes(one, rows, 2, sums)
    speed_sq[0][...], speed_sq[1][...] = sums
    planes = moved[0].shape[1]
    for j in range(2):
        tops[j] = moved[j][:, planes - HALO :]
        bottoms[j] = moved[j][:, :HALO]


def update(image, gathered, path, forces, slab_speed, partner_speed, images):
    counts = [len(pieces) for pieces in path]
    arrays = [piece for pieces in path for piece in pieces] + [*forces, partner_speed]
    out = jax.ShapeDtypeStruct(forces[0].shape, jnp.float32)
    edge = jax.ShapeDtypeStruct((2, 3, HALO, 8, 128), jnp.float32)
    results = pl.pallas_call(
        functools.partial(update_kernel, counts, images),
        out_shape=(out,) * 4 + (edge,) * 2 + (TILE,) * 2,
        in_specs=[SMEM, VMEM, pl.BlockSpec(memory_space=pltpu.HBM)] + [VMEM] * len(arrays),
        out_specs=(VMEM,) * 8,
        scratch_shapes=[
            pltpu.VMEM((2, 4, 8, 128), jnp.float32),
            pltpu.VMEM(forces[0].shape, jnp.float32),
            pltpu.SemaphoreType.DMA,
        ],
        compiler_params=PARAMS,
        name="fire_update",
    )(image, gathered, slab_speed, *arrays)
    return results[:2], results[2:4], results[4], results[5], results[6:]


def last_partner_kernel(images, image_ref, gathered_ref, before, here, after, force, speed, *outs):
    parts, terms_ref = outs[:-1], outs[-1]
    step_terms(image_ref, gathered_ref, images, terms_ref)
    for region, part in enumerate(parts):
        rows = part.shape[1]

        def one(p, carry):
            q = region * rows + p
            for axis in range(3):
                at = here[axis, q]
                part[axis, p] = new_speed(
                    terms_ref, 1, speed[axis, q], force[axis, q], after[axis, q] - at, at - before[axis, q]
                )
            return carry

        over_planes(one, rows, 2)


def last_partner(image, gathered, path, force, speed, images):
    part = jax.ShapeDtypeStruct((3, force.shape[1] // REGIONS, 8, 128), jnp.float32)
    return pl.pallas_call(
        functools.partial(last_partner_kernel, images),
        out_shape=(part,) * REGIONS + (jax.ShapeDtypeStruct((2, 4, 8, 128), jnp.float32),),
        in_specs=[SMEM] + [VMEM] * 6,
        out_specs=(VMEM,) * (REGIONS + 1),
        compiler_params=PARAMS,
        name="last_partner",
    )(image, gathered, *path, force, speed)


def last_own_kernel(side_ref, terms, before, here, after, force, speed, moved, new_ref):
    def one(p, carry):
        for axis in range(3):
            at = here[axis, p]
            new = new_speed(
                terms, 0, speed[axis, p], force[axis, p], after[axis, p] - at, at - before[axis, p]
            )
            new_ref[axis, p] = new
            moved[axis, p] = at + time_step * new
        return carry

    over_planes(one, here.shape[1], 2)


def last_own(side, terms, path, force, speed):
    planes = force.shape[1]
    chunk = planes // REGIONS
    block = pl.BlockSpec((3, chunk, 8, 128), lambda t, side_ref: (0, t, 0, 0))
    half = pl.BlockSpec((3, chunk, 8, 128), lambda t, side_ref: (0, side_ref[0] * REGIONS + t, 0, 0))
    out = jax.ShapeDtypeStruct((3, 2 * planes, 8, 128), jnp.float32)
    return pl.pallas_call(
        last_own_kernel,
        grid_spec=pltpu.PrefetchScalarGridSpec(
            num_scalar_prefetch=1,
            grid=(REGIONS,),
            in_specs=[pl.BlockSpec((2, 4, 8, 128), lambda t, side_ref: (0, 0, 0, 0))] + [block] * 5,
            out_specs=(half, half),
        ),
        out_shape=(out, out),
        compiler_params=PARAMS,
        name="last_own",
    )(side, terms, *path, force, speed)


def last_join_kernel(side_ref, here, speed, moved_in, speed_in, moved, new_ref):
    def one(p, carry):
        for axis in range(3):
            new = speed[axis, p]
            new_ref[axis, p] = new
            moved[axis, p] = here[axis, p] + time_step * new
        return carry

    over_planes(one, speed.shape[1], 4)


def last_join(side, region, here, speed, moved, speeds):
    rows = speed.shape[1]
    chunk = rows // JOIN_STEPS
    first = region * JOIN_STEPS
    block = pl.BlockSpec((3, chunk, 8, 128), lambda t, side_ref: (0, t, 0, 0))
    here_block = pl.BlockSpec((3, chunk, 8, 128), lambda t, side_ref: (0, first + t, 0, 0))
    half = pl.BlockSpec(
        (3, chunk, 8, 128),
        lambda t, side_ref: (0, (1 - side_ref[0]) * REGIONS * JOIN_STEPS + first + t, 0, 0),
    )
    out = jax.ShapeDtypeStruct(moved.shape, jnp.float32)
    whole = pl.BlockSpec(memory_space=pl.ANY)
    return pl.pallas_call(
        last_join_kernel,
        grid_spec=pltpu.PrefetchScalarGridSpec(
            num_scalar_prefetch=1,
            grid=(JOIN_STEPS,),
            in_specs=[here_block, block, whole, whole],
            out_specs=(half, half),
        ),
        out_shape=(out, out),
        input_output_aliases={3: 0, 4: 1},
        compiler_params=PARAMS,
        name="last_join",
    )(side, here, speed, moved, speeds)


def cut_kernel(blocks, squares, side_ref, *refs):
    count = len(blocks)
    source, outs, sems = refs[0], refs[1 : 1 + count], refs[-1]
    copies = []
    for k, out in enumerate(outs):
        at = 0
        for start, size in blocks[k]:
            rows = source.at[:, pl.ds(at_side(start, side_ref), size)]
            copies.append(
                pltpu.make_async_copy(rows, out.at[:, pl.ds(at, size)], sems.at[len(copies)])
            )
            at += size
    for copy in copies:
        copy.start()
    for copy in copies:
        copy.wait()
    if squares:

        def one(p, total):
            return total + sum(source[axis, p] * source[axis, p] for axis in range(3))

        refs[1 + count][...] = over_planes(one, source.shape[1], 4, jnp.zeros((8, 128), jnp.float32))


def at_side(pair, side_ref):
    even, odd = pair
    return even if even == odd else even + (odd - even) * side_ref[0]


def cut(side, array, blocks, squares=False):
    count = len(blocks)
    sizes = [sum(size for _, size in block) for block in blocks]
    return pl.pallas_call(
        functools.partial(cut_kernel, blocks, squares),
        out_shape=tuple(jax.ShapeDtypeStruct((3, size, 8, 128), jnp.float32) for size in sizes)
        + (TILE,) * squares,
        in_specs=[SMEM, VMEM if squares else pl.BlockSpec(memory_space=pltpu.HBM)],
        out_specs=(VMEM,) * (count + squares),
        scratch_shapes=[pltpu.SemaphoreType.DMA((sum(len(block) for block in blocks),))],
        compiler_params=PARAMS,
        name="cut",
    )(side, array)


def local(displacement, velocity):
    planes = displacement.shape[2] // (SIDE * SIDE)
    half = planes // 2
    images, slabs = lax.axis_size("image"), lax.axis_size("domain")
    both = ("image", "domain")
    own_image = lax.axis_index("image").astype(jnp.int32)
    side = own_image % 2
    image_arg, side_arg = own_image.reshape(1), side.reshape(1)
    slab = displacement.reshape(3, planes, 8, 128)
    slab_speed = velocity.reshape(3, planes, 8, 128)

    def at(image, domain):
        return image * slabs + domain % slabs

    everyone = [(i, d) for i in range(images) for d in range(slabs)]
    outer_own = [(at(i, d), at(i, d + 1 - 2 * (i % 2))) for i, d in everyone]
    outer_partner = [(at(i, d), at(i ^ 1, d - 1 + 2 * (i % 2))) for i, d in everyone]
    across = [(i, i ^ 1) for i in range(images)]
    own_out = [(i, i - 2 + 4 * (i % 2)) for i in range(images)]
    own_out = [(a, b) for a, b in own_out if 0 <= b < images]
    partner_out = [(b, a) for a, b in own_out]
    upward = [(at(i, d), at(i ^ 1, d + i % 2)) for i, d in everyone]
    downward = [(b, a) for a, b in upward]

    end, top = planes - HALO, half + HALO
    piece = PIECES[0]
    outer, inner = (0, top), (top, 0)
    edge_own, edge_partner, near_inner, own, lead, rest = cut(
        side_arg,
        slab,
        (
            (((end, 0), HALO),),
            (((0, end), HALO),),
            (((half, half - HALO), HALO),),
            (((0, half), half),),
            (((half, 0), piece), ((half - HALO, half), HALO)),
            (((half + piece, piece), PIECES[1]),),
        ),
    )
    halo_own = lax.ppermute(edge_own, both, outer_own)
    halo_partner = lax.ppermute(edge_partner, both, outer_partner)
    own, halo_own, halo_partner = lax.optimization_barrier(
        (own, halo_own, halo_partner)
    )
    partner = [lax.ppermute(part, "image", across) for part in (lead, rest)]
    beyond_own = lax.ppermute(own, "image", own_out)
    beyond_partner = [lax.ppermute(part, "image", partner_out) for part in partner]
    own_source = (
        (own, None, 0, half, (HALO, HALO)),
        (halo_own, None, 0, HALO, outer),
        (near_inner, None, 0, HALO, inner),
    )
    partner_source = (
        (partner[0], None, 0, piece, (HALO, HALO)),
        (partner[0], None, piece, HALO, inner),
        (partner[1], None, 0, PIECES[1], (HALO + piece,) * 2),
        (halo_partner, None, 0, HALO, outer),
    )
    forces, energies = image_forces(side_arg, half, (own_source, partner_source))
    far_speed, slab_sq = cut(side_arg, slab_speed, ((((half, 0), half),),), True)
    far_speed, *_ = lax.optimization_barrier((far_speed, partner[0]))
    partner_speed = lax.ppermute(far_speed, "image", across)

    path = (beyond_partner, [own], partner, [beyond_own])
    speeds = (slab_speed, partner_speed)
    speed_sq = (slab_sq, jnp.zeros_like(slab_sq))
    for step_index in range(FIRE_STEPS):
        if step_index > 0:
            forces, energies = image_forces(side_arg, half, sources)
        payload = moments(side_arg, path, forces, energies, speed_sq, images * slabs)
        gathered = lax.all_to_all(payload, both, 0, 0, tiled=True)
        if step_index == FIRE_STEPS - 1:
            break
        moved, speeds, tops, bottoms, speed_sq = update(
            image_arg, gathered, path, forces, *speeds, images
        )
        low = lax.ppermute(tops, both, upward)
        high = lax.ppermute(bottoms, both, downward)
        sources = [
            (
                (moved[j], None, 0, half, (HALO, HALO)),
                (low, 1 - j, 0, HALO, (0, 0)),
                (high, 1 - j, 0, HALO, (top, top)),
            )
            for j in range(2)
        ]
        path = (
            [lax.ppermute(moved[1], "image", partner_out)],
            [moved[0]],
            [moved[1]],
            [lax.ppermute(moved[0], "image", own_out)],
        )
        back_home, _, _ = lax.optimization_barrier((moved[1], low, high))
        returned = lax.ppermute(back_home, "image", across)
    whole = [pieces[0] for pieces in path]
    *last_speeds, terms = last_partner(
        image_arg, gathered, whole[1:], forces[1], speeds[1], images
    )
    last_speeds = [lax.ppermute(part, "image", across) for part in last_speeds]
    moved, new_speeds = last_own(side_arg, terms, whole[:3], forces[0], speeds[0])
    for region, part in enumerate(last_speeds):
        moved, new_speeds = last_join(side_arg, region, returned, part, moved, new_speeds)
    return (moved.reshape(displacement.shape), new_speeds.reshape(velocity.shape))


def solution(mesh):
    spec = P("image", None, "domain")
    return jax.shard_map(
        local,
        mesh=mesh,
        in_specs=(spec, spec),
        out_specs=(spec, spec),
        check_vma=False,
    )
```

```python
import functools
import math

import jax
import jax.numpy as jnp
from jax import lax
from jax.experimental import pallas as pl
from jax.experimental.pallas import tpu as pltpu
from jax.sharding import PartitionSpec as P

SIDE = 32
FIRE_STEPS = 2
QUANTITIES = 8
HALO = 2
REGIONS = 2
PIECES = (24, 24)
JOIN_STEPS = 2

lattice_const = 3.615
cutoff_sq = 9.61
nearest_sq = 6.533136
pair_scale = 30.0
pair_depth = 0.3
embed_scale = 1.2
bulk_root = 3.605551275463989
spring_const = 2.0
time_step = 0.1
fire_mixing = 0.1
stabilizer = 1e-06

reach_root = math.sqrt(cutoff_sq)
unit_half = 0.5 * lattice_const / reach_root
kappa = cutoff_sq / nearest_sq
dens_shift = (2.0 - kappa) / kappa
pair_shift = (2.5 - 2.0 * kappa) / (2.0 * kappa)
dens_scale = pair_scale * kappa
pair_energy_scale = pair_scale * pair_depth * 2.0 * kappa
dens_slope_shift = 0.75 * dens_shift
pair_slope_shift = 0.75 * pair_shift
dens_slope_scale = -4.0 * dens_scale / cutoff_sq
pair_slope_scale = -4.0 * pair_energy_scale / cutoff_sq
slope_ratio = dens_slope_scale / pair_slope_scale
force_scale = 2.0 * pair_slope_scale * reach_root


def shift(field, step_u, step_v, lanes):
    reach = step_u * SIDE + step_v
    turned = pltpu.roll(field, (-reach) % 128, 1)
    if step_u == 0:
        return turned
    carried = pltpu.roll(turned, (-step_u) % 8, 0)
    return jnp.where(lanes >= 128 - reach if reach > 0 else lanes < -reach, carried, turned)


def partners(field, step, lanes):
    return (
        shift(field, 0, step, lanes),
        shift(field, step, 0, lanes),
        shift(field, step, step, lanes),
    )


def gather_back(at_v, at_u, at_uv, step, lanes):
    return (
        shift(at_v, 0, -step, lanes)
        + shift(at_u, -step, 0, lanes)
        + shift(at_uv, -step, -step, lanes)
    )


def limits(step, u, v):
    far = jnp.float32(-1e30)
    in_u = (u + step >= 0) & (u + step < SIDE)
    in_v = (v + step >= 0) & (v + step < SIDE)
    one = jnp.ones_like(u, jnp.float32)
    return (
        jnp.where(in_v, one, far),
        jnp.where(in_u, one, far),
        jnp.where(in_u & in_v, one, far),
    )


def side_of(plane):
    return 1 if plane % 2 == 0 else -1


def force_kernel(layouts, side_ref, *refs):
    count = sum(len(layout) for layout in layouts)
    images = len(layouts)
    arrays, outs, scratch = refs[:count], refs[count : count + 2 * images], refs[count + 2 * images :]
    at = 0
    for j, layout in enumerate(layouts):
        sources = [
            (ref if slot is None else ref.at[slot], row, size, at_side(start, side_ref))
            for ref, (slot, row, size, start) in zip(arrays[at:], layout)
        ]
        at += len(layout)
        slab_forces(sources, outs[2 * j], outs[2 * j + 1], *scratch)


def slab_forces(sources, force_ref, energy_ref, pos, turned, seps, slopes, rho, back, embed, force_back):
    f32 = jnp.float32
    planes = force_ref.shape[1]
    lanes = lax.broadcasted_iota(jnp.int32, (8, 128), 1)
    subl = lax.broadcasted_iota(jnp.int32, (8, 128), 0)
    site_u = subl * 4 + lanes // SIDE
    site_v = lanes % SIDE
    inverse = f32(1.0 / reach_root)
    zero = jnp.zeros((8, 128), f32)

    def place(q, side, values):
        for axis in range(3):
            value = values[axis] * inverse
            pos[axis, q] = value
            for k, seen in enumerate(partners(value, side, lanes)):
                turned[axis, k, q] = seen

    for source, row, size, start in sources:
        unroll = max(n for n in range(2, 25, 2) if size % n == 0)

        def place_some(t, carry, source=source, row=row, start=start, unroll=unroll):
            for j in range(unroll):
                p = t * unroll + j
                place(start + p, side_of(j), [source[axis, row + p] for axis in range(3)])
            return carry

        lax.fori_loop(0, size // unroll, place_some, 0)

    def separations(e, step):
        h = f32(unit_half)
        sh = f32(step * unit_half)
        own = [pos[axis, e] for axis in range(3)]
        nxt = [pos[axis, e + 1] for axis in range(3)]
        seen = [[turned[axis, k, e + 1] for k in range(3)] for axis in range(3)]
        own_x = own[0] - h
        y_of = (own[1] + sh, own[1], own[1] - sh)
        z_of = (own[2] - sh, own[2], own[2] + sh)
        cross = [
            (nxt[0] - own_x, nxt[1] - y_of[0], nxt[2] - z_of[1]),
            (seen[0][0] - own_x, seen[1][0] - y_of[1], seen[2][0] - z_of[2]),
            (seen[0][1] - own_x, seen[1][1] - y_of[1], seen[2][1] - z_of[0]),
            (seen[0][2] - own_x, seen[1][2] - y_of[2], seen[2][2] - z_of[1]),
        ]
        near_y = nxt[1] - sh
        near_zv = nxt[2] + sh
        near_zu = nxt[2] - sh
        inside = [
            (seen[0][0] - nxt[0], seen[1][0] - near_y, seen[2][0] - near_zv),
            (seen[0][1] - nxt[0], seen[1][1] - near_y, seen[2][1] - near_zu),
        ]
        return cross + inside

    def density(e, step, bounds, carry):
        rho_part, sum_f, sum_c = carry
        one = jnp.ones((8, 128), f32)
        tops = (one, bounds[0], bounds[1], bounds[2], bounds[0], bounds[1])
        dens, cubes = [], []
        for k, sep in enumerate(separations(e, step)):
            y = sep[0] * sep[0] + sep[1] * sep[1] + sep[2] * sep[2]
            c = jnp.maximum(tops[k] - y, 0.0)
            square = c * c
            cube = square * c
            dens.append(cube * (c + f32(dens_shift)))
            cubes.append(cube)
            for axis in range(3):
                seps[e, k, axis] = sep[axis]
            slopes[e, k, 0] = square * (c + f32(pair_slope_shift))
            slopes[e, k, 1] = square * (c + f32(dens_slope_shift))
        cross = (dens[0] + dens[1]) + (dens[2] + dens[3])
        inside = dens[4] + dens[5]
        rho[e] = rho_part + cross
        back[0, e + 1] = dens[1] + dens[4]
        back[1, e + 1] = dens[2] + dens[5]
        back[2, e + 1] = dens[3]
        if 1 <= e <= planes:
            sum_f = sum_f + (cross + inside)
            sum_c = sum_c + (((cubes[0] + cubes[1]) + (cubes[2] + cubes[3])) + (cubes[4] + cubes[5]))
        return (dens[0] + inside, sum_f, sum_c)

    down = limits(-1, site_u, site_v)
    up = limits(1, site_u, site_v)

    carry = (zero, zero, zero)
    for e in range(planes + 2 * HALO - 1):
        carry = density(e, (-1, 1)[e % 2], (down, up)[e % 2], carry)
    _, sum_f, sum_c = carry

    def embedding(q, side):
        total = rho[q] + gather_back(back[0, q], back[1, q], back[2, q], side, lanes)
        w = 1.0 + f32(dens_scale) * total
        inv = lax.rsqrt(w)
        embed[0, q] = f32(-0.5 * embed_scale * slope_ratio) * inv
        return w * inv - f32(bulk_root)

    embedding(1, side_of(1))
    embedding(planes + HALO, side_of(0))

    roots = zero
    for q in range(HALO, HALO + planes):
        roots = roots + embedding(q, side_of(q))
    energy_ref[...] = f32(-embed_scale) * roots + f32(pair_energy_scale) * (
        sum_f + f32(pair_shift - dens_shift) * sum_c
    )

    def see(q, side):
        for k, seen in enumerate(partners(embed[0, q], side, lanes)):
            embed[1 + k, q] = seen

    for q in range(HALO, HALO + planes + 1):
        see(q, side_of(q))

    def force(e, keep, carry):
        own = embed[0, e]
        nxt = embed[0, e + 1]
        at_v, at_u, at_uv = [embed[1 + k, e + 1] for k in range(3)]
        partner = (own + nxt, own + at_v, own + at_u, own + at_uv, nxt + at_v, nxt + at_u)
        weight = [slopes[e, k, 0] + partner[k] * slopes[e, k, 1] for k in range(6)]
        out = []
        for axis in range(3):
            g = [weight[k] * seps[e, k, axis] for k in range(6)]
            if keep:
                force_ref[axis, e - HALO] = carry[axis] + ((g[0] + g[1]) + (g[2] + g[3]))
            force_back[axis, 0, e + 1] = g[1] + g[4]
            force_back[axis, 1, e + 1] = g[2] + g[5]
            force_back[axis, 2, e + 1] = g[3]
            out.append((g[4] + g[5]) - g[0])
        return tuple(out)

    carry = force(1, False, (zero, zero, zero))
    for e in range(HALO, HALO + planes):
        carry = force(e, True, carry)

    for p in range(planes):
        for axis in range(3):
            parts = [force_back[axis, k, p + HALO] for k in range(3)]
            force_ref[axis, p] = f32(force_scale) * (
                force_ref[axis, p] - gather_back(*parts, side_of(p), lanes)
            )


def image_forces(side, planes, images):
    vmem = pl.BlockSpec(memory_space=pltpu.VMEM)
    rows = planes + 2 * HALO
    arrays = [source[0] for sources in images for source in sources]
    layouts = [[source[1:] for source in sources] for sources in images]
    results = pl.pallas_call(
        functools.partial(force_kernel, layouts),
        out_shape=(
            jax.ShapeDtypeStruct((3, planes, 8, 128), jnp.float32),
            jax.ShapeDtypeStruct((8, 128), jnp.float32),
        )
        * len(images),
        in_specs=[pl.BlockSpec(memory_space=pltpu.SMEM)] + [vmem] * len(arrays),
        out_specs=(vmem,) * (2 * len(images)),
        scratch_shapes=[
            pltpu.VMEM((3, rows, 8, 128), jnp.float32),
            pltpu.VMEM((3, 3, rows, 8, 128), jnp.float32),
            pltpu.VMEM((rows, 6, 3, 8, 128), jnp.float32),
            pltpu.VMEM((rows, 6, 2, 8, 128), jnp.float32),
            pltpu.VMEM((rows, 8, 128), jnp.float32),
            pltpu.VMEM((3, rows, 8, 128), jnp.float32),
            pltpu.VMEM((4, rows, 8, 128), jnp.float32),
            pltpu.VMEM((3, 3, rows, 8, 128), jnp.float32),
        ],
        compiler_params=pltpu.CompilerParams(vmem_limit_bytes=20 * 1024 * 1024),
        cost_estimate=pl.CostEstimate(
            flops=40_000_000, bytes_accessed=30_000_000, transcendentals=0
        ),
        name="slab_forces",
    )(side, *arrays)
    return results[::2], results[1::2]


def total_of(tile):
    return jnp.sum(jnp.sum(tile, axis=0, keepdims=True), axis=1, keepdims=True)


def regions_of(path):
    at = 0
    for k, rows in enumerate(PIECES):
        yield at, rows, [(pieces[k], 0) if len(pieces) > 1 else (pieces[0], at) for pieces in path]
        at += rows


def over_planes(body, rows, unroll, carry=0):
    def some(t, carry):
        for j in range(unroll):
            carry = body(t * unroll + j, carry)
        return carry

    return lax.fori_loop(0, rows // unroll, some, carry)


def groups(refs, counts):
    out, at = [], 0
    for count in counts:
        out.append(refs[at : at + count])
        at += count
    return out, refs[at:]


def moment_kernel(counts, side_ref, *refs):
    path, refs = groups(refs, counts)
    forces, energies, speed_sq, out_ref = refs[:2], refs[2:4], refs[4:6], refs[6]
    zero = jnp.zeros((8, 128), jnp.float32)
    sums = (zero,) * 12
    for first, rows, held in regions_of(path):

        def one(p, carry):
            carry = list(carry)
            for axis in range(3):
                at = [ref[axis, start + p] for ref, start in held]
                diff = [at[j + 1] - at[j] for j in range(3)]
                square = [d * d for d in diff]
                for j in range(2):
                    force = forces[j][axis, first + p]
                    terms = (
                        force * force,
                        force * diff[j + 1],
                        force * diff[j],
                        square[j + 1],
                        square[j],
                        diff[j] * diff[j + 1],
                    )
                    for k, term in enumerate(terms):
                        carry[6 * j + k] = carry[6 * j + k] + term
            return tuple(carry)

        sums = over_planes(one, rows, 2, sums)

    lane = lax.broadcasted_iota(jnp.int32, (1, 128), 1)
    odd = side_ref[0] == 1
    sign = jnp.where(odd, -1.0, 1.0).astype(jnp.float32)
    row = jnp.zeros((1, 128), jnp.float32)
    for j in range(2):
        ahead = [total_of(sums[6 * j + k]) for k in range(6)]
        values = (
            total_of(energies[j][...]),
            ahead[0],
            sign * jnp.where(odd, ahead[2], ahead[1]),
            sign * jnp.where(odd, ahead[1], ahead[2]),
            jnp.where(odd, ahead[4], ahead[3]),
            jnp.where(odd, ahead[3], ahead[4]),
            ahead[5],
            total_of(speed_sq[j][...]),
        )
        for k, value in enumerate(values):
            row = row + jnp.where(lane == 8 * j + k, value, 0.0)
    out_ref[...] = jnp.broadcast_to(row, out_ref.shape)


VMEM = pl.BlockSpec(memory_space=pltpu.VMEM)
SMEM = pl.BlockSpec(memory_space=pltpu.SMEM)
PARAMS = pltpu.CompilerParams(vmem_limit_bytes=16 * 1024 * 1024)
TILE = jax.ShapeDtypeStruct((8, 128), jnp.float32)


def moments(side, path, forces, energies, speed_sq, copies):
    counts = [len(pieces) for pieces in path]
    arrays = [piece for pieces in path for piece in pieces] + [*forces, *energies, *speed_sq]
    return pl.pallas_call(
        functools.partial(moment_kernel, counts),
        out_shape=jax.ShapeDtypeStruct((copies, 128), jnp.float32),
        in_specs=[SMEM] + [VMEM] * len(arrays),
        out_specs=VMEM,
        compiler_params=PARAMS,
        name="path_moments",
    )(side, *arrays)


def path_terms(summary, images):
    lane = lax.broadcasted_iota(jnp.int32, (8, 128), 1)
    image = lax.broadcasted_iota(jnp.int32, (8, 128), 0)

    def column(k):
        picked = jnp.sum(jnp.where(lane == k, summary, 0.0), axis=1, keepdims=True)
        return jnp.broadcast_to(picked, (8, 128))

    e_here, ff, f_fwd, f_bwd, fwd_sq, bwd_sq, fwd_bwd, speed_sq = [column(k) for k in range(8)]
    e_prev = pltpu.roll(e_here, 1, 0)
    e_next = pltpu.roll(e_here, 7, 0)
    inner = (image > 0) & (image < images - 1)
    rise = e_next - e_here
    fall = e_here - e_prev
    larger = jnp.maximum(jnp.abs(rise), jnp.abs(fall))
    smaller = jnp.minimum(jnp.abs(rise), jnp.abs(fall))
    upward = (e_next > e_here) & (e_here > e_prev)
    downward = (e_next < e_here) & (e_here < e_prev)
    toward = e_next > e_prev
    weight_fwd = jnp.where(
        upward, 1.0, jnp.where(downward, 0.0, jnp.where(toward, larger, smaller))
    )
    weight_bwd = jnp.where(
        upward, 0.0, jnp.where(downward, 1.0, jnp.where(toward, smaller, larger))
    )
    tangent_sq = (
        weight_fwd * weight_fwd * fwd_sq
        + 2.0 * weight_fwd * weight_bwd * fwd_bwd
        + weight_bwd * weight_bwd * bwd_sq
    )
    norm_sq = tangent_sq + stabilizer
    force_tan = weight_fwd * f_fwd + weight_bwd * f_bwd
    spring = spring_const * (jnp.sqrt(fwd_sq + stabilizer) - jnp.sqrt(bwd_sq + stabilizer))
    coefficient = -force_tan / norm_sq + spring / jnp.sqrt(norm_sq)
    neb_sq = ff + 2.0 * coefficient * force_tan + coefficient * coefficient * tangent_sq

    def over_inner(value):
        return jnp.sum(jnp.where(inner, value, 0.0), axis=0, keepdims=True)

    force_norm = jnp.sqrt(over_inner(neb_sq) + stabilizer)
    speed_norm = jnp.sqrt(over_inner(speed_sq) + stabilizer)
    gain = jnp.broadcast_to(fire_mixing * (speed_norm / force_norm) + time_step, (8, 128))
    keep = jnp.where(inner, 1.0 - fire_mixing, 0.0)
    push = jnp.where(inner, gain, 0.0)
    along_fwd = jnp.where(inner, gain * coefficient * weight_fwd, 0.0)
    along_bwd = jnp.where(inner, gain * coefficient * weight_bwd, 0.0)
    return keep, push, along_fwd, along_bwd


def step_terms(image_ref, gathered_ref, images, terms):
    image = lax.broadcasted_iota(jnp.int32, (8, 128), 0)
    summary = jnp.zeros((8, 128), jnp.float32)
    slabs = gathered_ref.shape[0] // images
    for g in range(images):
        rows = gathered_ref[g * slabs : (g + 1) * slabs, :]
        row = jnp.broadcast_to(jnp.sum(rows, axis=0, keepdims=True), (8, 128))
        summary = summary + jnp.where(image == g, row, 0.0)
        summary = summary + jnp.where(image == (g ^ 1), pltpu.roll(row, 120, 1), 0.0)
    keep, push, along_fwd, along_bwd = path_terms(summary, images)
    here = image_ref[0]
    odd = here % 2 == 1
    values = (keep, push, jnp.where(odd, -along_bwd, along_fwd), jnp.where(odd, -along_fwd, along_bwd))
    for j in range(2):
        at = image == (here + j * (1 - 2 * (here % 2)))
        for k, value in enumerate(values):
            own = jnp.sum(jnp.where(at, value, 0.0), axis=0, keepdims=True)
            terms[j, k] = jnp.broadcast_to(own, (8, 128))


def new_speed(terms, j, speed, force, ahead, behind):
    return terms[j, 0] * speed + terms[j, 1] * force + terms[j, 2] * ahead + terms[j, 3] * behind


def update_kernel(counts, images, image_ref, gathered_ref, slab_speed, *refs):
    path, refs = groups(refs, counts)
    forces, partner_speed, moved, new_speeds = refs[:2], refs[2], refs[3:5], refs[5:7]
    tops, bottoms, speed_sq, (terms, own_speed, sem) = refs[7], refs[8], refs[9:11], refs[11:]
    speeds = (own_speed, partner_speed)
    half = own_speed.shape[1]
    copy = pltpu.make_async_copy(
        slab_speed.at[:, pl.ds(image_ref[0] % 2 * half, half)], own_speed, sem
    )
    copy.start()
    step_terms(image_ref, gathered_ref, images, terms)
    copy.wait()
    sums = (jnp.zeros((8, 128), jnp.float32),) * 2
    for first, rows, held in regions_of(path):

        def one(p, carry):
            carry = list(carry)
            for axis in range(3):
                at = [ref[axis, start + p] for ref, start in held]
                diff = [at[j + 1] - at[j] for j in range(3)]
                for j in range(2):
                    q = first + p
                    speed = new_speed(terms, j, speeds[j][axis, q], forces[j][axis, q], diff[j + 1], diff[j])
                    new_speeds[j][axis, q] = speed
                    moved[j][axis, q] = at[j + 1] + time_step * speed
                    carry[j] = carry[j] + speed * speed
            return tuple(carry)

        sums = over_planes(one, rows, 2, sums)
    speed_sq[0][...], speed_sq[1][...] = sums
    planes = moved[0].shape[1]
    for j in range(2):
        tops[j] = moved[j][:, planes - HALO :]
        bottoms[j] = moved[j][:, :HALO]


def update(image, gathered, path, forces, slab_speed, partner_speed, images):
    counts = [len(pieces) for pieces in path]
    arrays = [piece for pieces in path for piece in pieces] + [*forces, partner_speed]
    out = jax.ShapeDtypeStruct(forces[0].shape, jnp.float32)
    edge = jax.ShapeDtypeStruct((2, 3, HALO, 8, 128), jnp.float32)
    results = pl.pallas_call(
        functools.partial(update_kernel, counts, images),
        out_shape=(out,) * 4 + (edge,) * 2 + (TILE,) * 2,
        in_specs=[SMEM, VMEM, pl.BlockSpec(memory_space=pltpu.HBM)] + [VMEM] * len(arrays),
        out_specs=(VMEM,) * 8,
        scratch_shapes=[
            pltpu.VMEM((2, 4, 8, 128), jnp.float32),
            pltpu.VMEM(forces[0].shape, jnp.float32),
            pltpu.SemaphoreType.DMA,
        ],
        compiler_params=PARAMS,
        name="fire_update",
    )(image, gathered, slab_speed, *arrays)
    return results[:2], results[2:4], results[4], results[5], results[6:]


def last_partner_kernel(images, image_ref, gathered_ref, before, here, after, force, speed, *outs):
    parts, terms_ref = outs[:-1], outs[-1]
    step_terms(image_ref, gathered_ref, images, terms_ref)
    for region, part in enumerate(parts):
        rows = part.shape[1]

        def one(p, carry):
            q = region * rows + p
            for axis in range(3):
                at = here[axis, q]
                part[axis, p] = new_speed(
                    terms_ref, 1, speed[axis, q], force[axis, q], after[axis, q] - at, at - before[axis, q]
                )
            return carry

        over_planes(one, rows, 2)


def last_partner(image, gathered, path, force, speed, images):
    part = jax.ShapeDtypeStruct((3, force.shape[1] // REGIONS, 8, 128), jnp.float32)
    return pl.pallas_call(
        functools.partial(last_partner_kernel, images),
        out_shape=(part,) * REGIONS + (jax.ShapeDtypeStruct((2, 4, 8, 128), jnp.float32),),
        in_specs=[SMEM] + [VMEM] * 6,
        out_specs=(VMEM,) * (REGIONS + 1),
        compiler_params=PARAMS,
        name="last_partner",
    )(image, gathered, *path, force, speed)


def last_own_kernel(side_ref, terms, before, here, after, force, speed, moved, new_ref):
    def one(p, carry):
        for axis in range(3):
            at = here[axis, p]
            new = new_speed(
                terms, 0, speed[axis, p], force[axis, p], after[axis, p] - at, at - before[axis, p]
            )
            new_ref[axis, p] = new
            moved[axis, p] = at + time_step * new
        return carry

    over_planes(one, here.shape[1], 2)


def last_own(side, terms, path, force, speed):
    planes = force.shape[1]
    chunk = planes // REGIONS
    block = pl.BlockSpec((3, chunk, 8, 128), lambda t, side_ref: (0, t, 0, 0))
    half = pl.BlockSpec((3, chunk, 8, 128), lambda t, side_ref: (0, side_ref[0] * REGIONS + t, 0, 0))
    out = jax.ShapeDtypeStruct((3, 2 * planes, 8, 128), jnp.float32)
    return pl.pallas_call(
        last_own_kernel,
        grid_spec=pltpu.PrefetchScalarGridSpec(
            num_scalar_prefetch=1,
            grid=(REGIONS,),
            in_specs=[pl.BlockSpec((2, 4, 8, 128), lambda t, side_ref: (0, 0, 0, 0))] + [block] * 5,
            out_specs=(half, half),
        ),
        out_shape=(out, out),
        compiler_params=PARAMS,
        name="last_own",
    )(side, terms, *path, force, speed)


def last_join_kernel(side_ref, here, speed, moved_in, speed_in, moved, new_ref):
    def one(p, carry):
        for axis in range(3):
            new = speed[axis, p]
            new_ref[axis, p] = new
            moved[axis, p] = here[axis, p] + time_step * new
        return carry

    over_planes(one, speed.shape[1], 4)


def last_join(side, region, here, speed, moved, speeds):
    rows = speed.shape[1]
    chunk = rows // JOIN_STEPS
    first = region * JOIN_STEPS
    block = pl.BlockSpec((3, chunk, 8, 128), lambda t, side_ref: (0, t, 0, 0))
    here_block = pl.BlockSpec((3, chunk, 8, 128), lambda t, side_ref: (0, first + t, 0, 0))
    half = pl.BlockSpec(
        (3, chunk, 8, 128),
        lambda t, side_ref: (0, (1 - side_ref[0]) * REGIONS * JOIN_STEPS + first + t, 0, 0),
    )
    out = jax.ShapeDtypeStruct(moved.shape, jnp.float32)
    whole = pl.BlockSpec(memory_space=pl.ANY)
    return pl.pallas_call(
        last_join_kernel,
        grid_spec=pltpu.PrefetchScalarGridSpec(
            num_scalar_prefetch=1,
            grid=(JOIN_STEPS,),
            in_specs=[here_block, block, whole, whole],
            out_specs=(half, half),
        ),
        out_shape=(out, out),
        input_output_aliases={3: 0, 4: 1},
        compiler_params=PARAMS,
        name="last_join",
    )(side, here, speed, moved, speeds)


def cut_kernel(blocks, squares, side_ref, *refs):
    count = len(blocks)
    source, outs, sems = refs[0], refs[1 : 1 + count], refs[-1]
    copies = []
    for k, out in enumerate(outs):
        at = 0
        for start, size in blocks[k]:
            rows = source.at[:, pl.ds(at_side(start, side_ref), size)]
            copies.append(
                pltpu.make_async_copy(rows, out.at[:, pl.ds(at, size)], sems.at[len(copies)])
            )
            at += size
    for copy in copies:
        copy.start()
    for copy in copies:
        copy.wait()
    if squares:

        def one(p, total):
            return total + sum(source[axis, p] * source[axis, p] for axis in range(3))

        refs[1 + count][...] = over_planes(one, source.shape[1], 4, jnp.zeros((8, 128), jnp.float32))


def at_side(pair, side_ref):
    even, odd = pair
    return even if even == odd else even + (odd - even) * side_ref[0]


def cut(side, array, blocks, squares=False):
    count = len(blocks)
    sizes = [sum(size for _, size in block) for block in blocks]
    return pl.pallas_call(
        functools.partial(cut_kernel, blocks, squares),
        out_shape=tuple(jax.ShapeDtypeStruct((3, size, 8, 128), jnp.float32) for size in sizes)
        + (TILE,) * squares,
        in_specs=[SMEM, VMEM if squares else pl.BlockSpec(memory_space=pltpu.HBM)],
        out_specs=(VMEM,) * (count + squares),
        scratch_shapes=[pltpu.SemaphoreType.DMA((sum(len(block) for block in blocks),))],
        compiler_params=PARAMS,
        name="cut",
    )(side, array)


def local(displacement, velocity):
    planes = displacement.shape[2] // (SIDE * SIDE)
    half = planes // 2
    images, slabs = lax.axis_size("image"), lax.axis_size("domain")
    both = ("image", "domain")
    own_image = lax.axis_index("image").astype(jnp.int32)
    side = own_image % 2
    image_arg, side_arg = own_image.reshape(1), side.reshape(1)
    slab = displacement.reshape(3, planes, 8, 128)
    slab_speed = velocity.reshape(3, planes, 8, 128)

    def at(image, domain):
        return image * slabs + domain % slabs

    everyone = [(i, d) for i in range(images) for d in range(slabs)]
    outer_own = [(at(i, d), at(i, d + 1 - 2 * (i % 2))) for i, d in everyone]
    outer_partner = [(at(i, d), at(i ^ 1, d - 1 + 2 * (i % 2))) for i, d in everyone]
    across = [(i, i ^ 1) for i in range(images)]
    own_out = [(i, i - 2 + 4 * (i % 2)) for i in range(images)]
    own_out = [(a, b) for a, b in own_out if 0 <= b < images]
    partner_out = [(b, a) for a, b in own_out]
    upward = [(at(i, d), at(i ^ 1, d + i % 2)) for i, d in everyone]
    downward = [(b, a) for a, b in upward]

    end, top = planes - HALO, half + HALO
    piece = PIECES[0]
    outer, inner = (0, top), (top, 0)
    edge_own, edge_partner, near_inner, own, lead, rest = cut(
        side_arg,
        slab,
        (
            (((end, 0), HALO),),
            (((0, end), HALO),),
            (((half, half - HALO), HALO),),
            (((0, half), half),),
            (((half, 0), piece), ((half - HALO, half), HALO)),
            (((half + piece, piece), PIECES[1]),),
        ),
    )
    halo_own = lax.ppermute(edge_own, both, outer_own)
    halo_partner = lax.ppermute(edge_partner, both, outer_partner)
    rest, halo_own, halo_partner = lax.optimization_barrier(
        (rest, halo_own, halo_partner)
    )
    partner = [lax.ppermute(part, "image", across) for part in (lead, rest)]
    beyond_own = lax.ppermute(own, "image", own_out)
    beyond_partner = [lax.ppermute(part, "image", partner_out) for part in partner]
    own_source = (
        (own, None, 0, half, (HALO, HALO)),
        (halo_own, None, 0, HALO, outer),
        (near_inner, None, 0, HALO, inner),
    )
    partner_source = (
        (partner[0], None, 0, piece, (HALO, HALO)),
        (partner[0], None, piece, HALO, inner),
        (partner[1], None, 0, PIECES[1], (HALO + piece,) * 2),
        (halo_partner, None, 0, HALO, outer),
    )
    forces, energies = image_forces(side_arg, half, (own_source, partner_source))
    far_speed, slab_sq = cut(side_arg, slab_speed, ((((half, 0), half),),), True)
    far_speed, *_ = lax.optimization_barrier((far_speed, beyond_partner[0], partner[1]))
    partner_speed = lax.ppermute(far_speed, "image", across)

    path = (beyond_partner, [own], partner, [beyond_own])
    speeds = (slab_speed, partner_speed)
    speed_sq = (slab_sq, jnp.zeros_like(slab_sq))
    for step_index in range(FIRE_STEPS):
        if step_index > 0:
            forces, energies = image_forces(side_arg, half, sources)
        payload = moments(side_arg, path, forces, energies, speed_sq, images * slabs)
        gathered = lax.all_to_all(payload, both, 0, 0, tiled=True)
        if step_index == FIRE_STEPS - 1:
            break
        moved, speeds, tops, bottoms, speed_sq = update(
            image_arg, gathered, path, forces, *speeds, images
        )
        low = lax.ppermute(tops, both, upward)
        high = lax.ppermute(bottoms, both, downward)
        sources = [
            (
                (moved[j], None, 0, half, (HALO, HALO)),
                (low, 1 - j, 0, HALO, (0, 0)),
                (high, 1 - j, 0, HALO, (top, top)),
            )
            for j in range(2)
        ]
        path = (
            [lax.ppermute(moved[1], "image", partner_out)],
            [moved[0]],
            [moved[1]],
            [lax.ppermute(moved[0], "image", own_out)],
        )
        back_home, _, _ = lax.optimization_barrier((moved[1], low, high))
        returned = lax.ppermute(back_home, "image", across)
    whole = [pieces[0] for pieces in path]
    *last_speeds, terms = last_partner(
        image_arg, gathered, whole[1:], forces[1], speeds[1], images
    )
    last_speeds = [lax.ppermute(part, "image", across) for part in last_speeds]
    moved, new_speeds = last_own(side_arg, terms, whole[:3], forces[0], speeds[0])
    for region, part in enumerate(last_speeds):
        moved, new_speeds = last_join(side_arg, region, returned, part, moved, new_speeds)
    return (moved.reshape(displacement.shape), new_speeds.reshape(velocity.shape))


def solution(mesh):
    spec = P("image", None, "domain")
    return jax.shard_map(
        local,
        mesh=mesh,
        in_specs=(spec, spec),
        out_specs=(spec, spec),
        check_vma=False,
    )
```

```python
import functools
import math

import jax
import jax.numpy as jnp
from jax import lax
from jax.experimental import pallas as pl
from jax.experimental.pallas import tpu as pltpu
from jax.sharding import PartitionSpec as P

SIDE = 32
FIRE_STEPS = 2
QUANTITIES = 8
HALO = 2
REGIONS = 2
PIECES = (24, 24)
JOIN_STEPS = 2

lattice_const = 3.615
cutoff_sq = 9.61
nearest_sq = 6.533136
pair_scale = 30.0
pair_depth = 0.3
embed_scale = 1.2
bulk_root = 3.605551275463989
spring_const = 2.0
time_step = 0.1
fire_mixing = 0.1
stabilizer = 1e-06

reach_root = math.sqrt(cutoff_sq)
unit_half = 0.5 * lattice_const / reach_root
kappa = cutoff_sq / nearest_sq
dens_shift = (2.0 - kappa) / kappa
pair_shift = (2.5 - 2.0 * kappa) / (2.0 * kappa)
dens_scale = pair_scale * kappa
pair_energy_scale = pair_scale * pair_depth * 2.0 * kappa
dens_slope_shift = 0.75 * dens_shift
pair_slope_shift = 0.75 * pair_shift
dens_slope_scale = -4.0 * dens_scale / cutoff_sq
pair_slope_scale = -4.0 * pair_energy_scale / cutoff_sq
slope_ratio = dens_slope_scale / pair_slope_scale
force_scale = 2.0 * pair_slope_scale * reach_root


def shift(field, step_u, step_v, lanes):
    reach = step_u * SIDE + step_v
    turned = pltpu.roll(field, (-reach) % 128, 1)
    if step_u == 0:
        return turned
    carried = pltpu.roll(turned, (-step_u) % 8, 0)
    return jnp.where(lanes >= 128 - reach if reach > 0 else lanes < -reach, carried, turned)


def partners(field, step, lanes):
    return (
        shift(field, 0, step, lanes),
        shift(field, step, 0, lanes),
        shift(field, step, step, lanes),
    )


def gather_back(at_v, at_u, at_uv, step, lanes):
    return (
        shift(at_v, 0, -step, lanes)
        + shift(at_u, -step, 0, lanes)
        + shift(at_uv, -step, -step, lanes)
    )


def limits(step, u, v):
    far = jnp.float32(-1e30)
    in_u = (u + step >= 0) & (u + step < SIDE)
    in_v = (v + step >= 0) & (v + step < SIDE)
    one = jnp.ones_like(u, jnp.float32)
    return (
        jnp.where(in_v, one, far),
        jnp.where(in_u, one, far),
        jnp.where(in_u & in_v, one, far),
    )


def side_of(plane):
    return 1 if plane % 2 == 0 else -1


def force_kernel(layouts, side_ref, *refs):
    count = sum(len(layout) for layout in layouts)
    images = len(layouts)
    arrays, outs, scratch = refs[:count], refs[count : count + 2 * images], refs[count + 2 * images :]
    at = 0
    for j, layout in enumerate(layouts):
        sources = [
            (ref if slot is None else ref.at[slot], row, size, at_side(start, side_ref))
            for ref, (slot, row, size, start) in zip(arrays[at:], layout)
        ]
        at += len(layout)
        slab_forces(sources, outs[2 * j], outs[2 * j + 1], *scratch)


def slab_forces(sources, force_ref, energy_ref, pos, turned, seps, slopes, rho, back, embed, force_back):
    f32 = jnp.float32
    planes = force_ref.shape[1]
    lanes = lax.broadcasted_iota(jnp.int32, (8, 128), 1)
    subl = lax.broadcasted_iota(jnp.int32, (8, 128), 0)
    site_u = subl * 4 + lanes // SIDE
    site_v = lanes % SIDE
    inverse = f32(1.0 / reach_root)
    zero = jnp.zeros((8, 128), f32)

    def place(q, side, values):
        for axis in range(3):
            value = values[axis] * inverse
            pos[axis, q] = value
            for k, seen in enumerate(partners(value, side, lanes)):
                turned[axis, k, q] = seen

    for source, row, size, start in sources:
        unroll = max(n for n in range(2, 25, 2) if size % n == 0)

        def place_some(t, carry, source=source, row=row, start=start, unroll=unroll):
            for j in range(unroll):
                p = t * unroll + j
                place(start + p, side_of(j), [source[axis, row + p] for axis in range(3)])
            return carry

        lax.fori_loop(0, size // unroll, place_some, 0)

    def separations(e, step):
        h = f32(unit_half)
        sh = f32(step * unit_half)
        own = [pos[axis, e] for axis in range(3)]
        nxt = [pos[axis, e + 1] for axis in range(3)]
        seen = [[turned[axis, k, e + 1] for k in range(3)] for axis in range(3)]
        own_x = own[0] - h
        y_of = (own[1] + sh, own[1], own[1] - sh)
        z_of = (own[2] - sh, own[2], own[2] + sh)
        cross = [
            (nxt[0] - own_x, nxt[1] - y_of[0], nxt[2] - z_of[1]),
            (seen[0][0] - own_x, seen[1][0] - y_of[1], seen[2][0] - z_of[2]),
            (seen[0][1] - own_x, seen[1][1] - y_of[1], seen[2][1] - z_of[0]),
            (seen[0][2] - own_x, seen[1][2] - y_of[2], seen[2][2] - z_of[1]),
        ]
        near_y = nxt[1] - sh
        near_zv = nxt[2] + sh
        near_zu = nxt[2] - sh
        inside = [
            (seen[0][0] - nxt[0], seen[1][0] - near_y, seen[2][0] - near_zv),
            (seen[0][1] - nxt[0], seen[1][1] - near_y, seen[2][1] - near_zu),
        ]
        return cross + inside

    def density(e, step, bounds, carry):
        rho_part, sum_f, sum_c = carry
        one = jnp.ones((8, 128), f32)
        tops = (one, bounds[0], bounds[1], bounds[2], bounds[0], bounds[1])
        dens, cubes = [], []
        for k, sep in enumerate(separations(e, step)):
            y = sep[0] * sep[0] + sep[1] * sep[1] + sep[2] * sep[2]
            c = jnp.maximum(tops[k] - y, 0.0)
            square = c * c
            cube = square * c
            dens.append(cube * (c + f32(dens_shift)))
            cubes.append(cube)
            for axis in range(3):
                seps[e, k, axis] = sep[axis]
            slopes[e, k, 0] = square * (c + f32(pair_slope_shift))
            slopes[e, k, 1] = square * (c + f32(dens_slope_shift))
        cross = (dens[0] + dens[1]) + (dens[2] + dens[3])
        inside = dens[4] + dens[5]
        rho[e] = rho_part + cross
        back[0, e + 1] = dens[1] + dens[4]
        back[1, e + 1] = dens[2] + dens[5]
        back[2, e + 1] = dens[3]
        if 1 <= e <= planes:
            sum_f = sum_f + (cross + inside)
            sum_c = sum_c + (((cubes[0] + cubes[1]) + (cubes[2] + cubes[3])) + (cubes[4] + cubes[5]))
        return (dens[0] + inside, sum_f, sum_c)

    down = limits(-1, site_u, site_v)
    up = limits(1, site_u, site_v)

    carry = (zero, zero, zero)
    for e in range(planes + 2 * HALO - 1):
        carry = density(e, (-1, 1)[e % 2], (down, up)[e % 2], carry)
    _, sum_f, sum_c = carry

    def embedding(q, side):
        total = rho[q] + gather_back(back[0, q], back[1, q], back[2, q], side, lanes)
        w = 1.0 + f32(dens_scale) * total
        inv = lax.rsqrt(w)
        embed[0, q] = f32(-0.5 * embed_scale * slope_ratio) * inv
        return w * inv - f32(bulk_root)

    embedding(1, side_of(1))
    embedding(planes + HALO, side_of(0))

    roots = zero
    for q in range(HALO, HALO + planes):
        roots = roots + embedding(q, side_of(q))
    energy_ref[...] = f32(-embed_scale) * roots + f32(pair_energy_scale) * (
        sum_f + f32(pair_shift - dens_shift) * sum_c
    )

    def see(q, side):
        for k, seen in enumerate(partners(embed[0, q], side, lanes)):
            embed[1 + k, q] = seen

    for q in range(HALO, HALO + planes + 1):
        see(q, side_of(q))

    def force(e, keep, carry):
        own = embed[0, e]
        nxt = embed[0, e + 1]
        at_v, at_u, at_uv = [embed[1 + k, e + 1] for k in range(3)]
        partner = (own + nxt, own + at_v, own + at_u, own + at_uv, nxt + at_v, nxt + at_u)
        weight = [slopes[e, k, 0] + partner[k] * slopes[e, k, 1] for k in range(6)]
        out = []
        for axis in range(3):
            g = [weight[k] * seps[e, k, axis] for k in range(6)]
            if keep:
                force_ref[axis, e - HALO] = carry[axis] + ((g[0] + g[1]) + (g[2] + g[3]))
            force_back[axis, 0, e + 1] = g[1] + g[4]
            force_back[axis, 1, e + 1] = g[2] + g[5]
            force_back[axis, 2, e + 1] = g[3]
            out.append((g[4] + g[5]) - g[0])
        return tuple(out)

    carry = force(1, False, (zero, zero, zero))
    for e in range(HALO, HALO + planes):
        carry = force(e, True, carry)

    for p in range(planes):
        for axis in range(3):
            parts = [force_back[axis, k, p + HALO] for k in range(3)]
            force_ref[axis, p] = f32(force_scale) * (
                force_ref[axis, p] - gather_back(*parts, side_of(p), lanes)
            )


def image_forces(side, planes, images):
    vmem = pl.BlockSpec(memory_space=pltpu.VMEM)
    rows = planes + 2 * HALO
    arrays = [source[0] for sources in images for source in sources]
    layouts = [[source[1:] for source in sources] for sources in images]
    results = pl.pallas_call(
        functools.partial(force_kernel, layouts),
        out_shape=(
            jax.ShapeDtypeStruct((3, planes, 8, 128), jnp.float32),
            jax.ShapeDtypeStruct((8, 128), jnp.float32),
        )
        * len(images),
        in_specs=[pl.BlockSpec(memory_space=pltpu.SMEM)] + [vmem] * len(arrays),
        out_specs=(vmem,) * (2 * len(images)),
        scratch_shapes=[
            pltpu.VMEM((3, rows, 8, 128), jnp.float32),
            pltpu.VMEM((3, 3, rows, 8, 128), jnp.float32),
            pltpu.VMEM((rows, 6, 3, 8, 128), jnp.float32),
            pltpu.VMEM((rows, 6, 2, 8, 128), jnp.float32),
            pltpu.VMEM((rows, 8, 128), jnp.float32),
            pltpu.VMEM((3, rows, 8, 128), jnp.float32),
            pltpu.VMEM((4, rows, 8, 128), jnp.float32),
            pltpu.VMEM((3, 3, rows, 8, 128), jnp.float32),
        ],
        compiler_params=pltpu.CompilerParams(vmem_limit_bytes=20 * 1024 * 1024),
        cost_estimate=pl.CostEstimate(
            flops=40_000_000, bytes_accessed=30_000_000, transcendentals=0
        ),
        name="slab_forces",
    )(side, *arrays)
    return results[::2], results[1::2]


def total_of(tile):
    return jnp.sum(jnp.sum(tile, axis=0, keepdims=True), axis=1, keepdims=True)


def regions_of(path):
    at = 0
    for k, rows in enumerate(PIECES):
        yield at, rows, [(pieces[k], 0) if len(pieces) > 1 else (pieces[0], at) for pieces in path]
        at += rows


def over_planes(body, rows, unroll, carry=0):
    def some(t, carry):
        for j in range(unroll):
            carry = body(t * unroll + j, carry)
        return carry

    return lax.fori_loop(0, rows // unroll, some, carry)


def groups(refs, counts):
    out, at = [], 0
    for count in counts:
        out.append(refs[at : at + count])
        at += count
    return out, refs[at:]


def moment_kernel(counts, side_ref, *refs):
    path, refs = groups(refs, counts)
    forces, energies, speed_sq, out_ref = refs[:2], refs[2:4], refs[4:6], refs[6]
    zero = jnp.zeros((8, 128), jnp.float32)
    sums = (zero,) * 12
    for first, rows, held in regions_of(path):

        def one(p, carry):
            carry = list(carry)
            for axis in range(3):
                at = [ref[axis, start + p] for ref, start in held]
                diff = [at[j + 1] - at[j] for j in range(3)]
                square = [d * d for d in diff]
                for j in range(2):
                    force = forces[j][axis, first + p]
                    terms = (
                        force * force,
                        force * diff[j + 1],
                        force * diff[j],
                        square[j + 1],
                        square[j],
                        diff[j] * diff[j + 1],
                    )
                    for k, term in enumerate(terms):
                        carry[6 * j + k] = carry[6 * j + k] + term
            return tuple(carry)

        sums = over_planes(one, rows, 2, sums)

    lane = lax.broadcasted_iota(jnp.int32, (1, 128), 1)
    odd = side_ref[0] == 1
    sign = jnp.where(odd, -1.0, 1.0).astype(jnp.float32)
    row = jnp.zeros((1, 128), jnp.float32)
    for j in range(2):
        ahead = [total_of(sums[6 * j + k]) for k in range(6)]
        values = (
            total_of(energies[j][...]),
            ahead[0],
            sign * jnp.where(odd, ahead[2], ahead[1]),
            sign * jnp.where(odd, ahead[1], ahead[2]),
            jnp.where(odd, ahead[4], ahead[3]),
            jnp.where(odd, ahead[3], ahead[4]),
            ahead[5],
            total_of(speed_sq[j][...]),
        )
        for k, value in enumerate(values):
            row = row + jnp.where(lane == 8 * j + k, value, 0.0)
    out_ref[...] = jnp.broadcast_to(row, out_ref.shape)


VMEM = pl.BlockSpec(memory_space=pltpu.VMEM)
SMEM = pl.BlockSpec(memory_space=pltpu.SMEM)
PARAMS = pltpu.CompilerParams(vmem_limit_bytes=16 * 1024 * 1024)
TILE = jax.ShapeDtypeStruct((8, 128), jnp.float32)


def moments(side, path, forces, energies, speed_sq, copies):
    counts = [len(pieces) for pieces in path]
    arrays = [piece for pieces in path for piece in pieces] + [*forces, *energies, *speed_sq]
    return pl.pallas_call(
        functools.partial(moment_kernel, counts),
        out_shape=jax.ShapeDtypeStruct((copies, 128), jnp.float32),
        in_specs=[SMEM] + [VMEM] * len(arrays),
        out_specs=VMEM,
        compiler_params=PARAMS,
        name="path_moments",
    )(side, *arrays)


def path_terms(summary, images):
    lane = lax.broadcasted_iota(jnp.int32, (8, 128), 1)
    image = lax.broadcasted_iota(jnp.int32, (8, 128), 0)

    def column(k):
        picked = jnp.sum(jnp.where(lane == k, summary, 0.0), axis=1, keepdims=True)
        return jnp.broadcast_to(picked, (8, 128))

    e_here, ff, f_fwd, f_bwd, fwd_sq, bwd_sq, fwd_bwd, speed_sq = [column(k) for k in range(8)]
    e_prev = pltpu.roll(e_here, 1, 0)
    e_next = pltpu.roll(e_here, 7, 0)
    inner = (image > 0) & (image < images - 1)
    rise = e_next - e_here
    fall = e_here - e_prev
    larger = jnp.maximum(jnp.abs(rise), jnp.abs(fall))
    smaller = jnp.minimum(jnp.abs(rise), jnp.abs(fall))
    upward = (e_next > e_here) & (e_here > e_prev)
    downward = (e_next < e_here) & (e_here < e_prev)
    toward = e_next > e_prev
    weight_fwd = jnp.where(
        upward, 1.0, jnp.where(downward, 0.0, jnp.where(toward, larger, smaller))
    )
    weight_bwd = jnp.where(
        upward, 0.0, jnp.where(downward, 1.0, jnp.where(toward, smaller, larger))
    )
    tangent_sq = (
        weight_fwd * weight_fwd * fwd_sq
        + 2.0 * weight_fwd * weight_bwd * fwd_bwd
        + weight_bwd * weight_bwd * bwd_sq
    )
    norm_sq = tangent_sq + stabilizer
    force_tan = weight_fwd * f_fwd + weight_bwd * f_bwd
    spring = spring_const * (jnp.sqrt(fwd_sq + stabilizer) - jnp.sqrt(bwd_sq + stabilizer))
    coefficient = -force_tan / norm_sq + spring / jnp.sqrt(norm_sq)
    neb_sq = ff + 2.0 * coefficient * force_tan + coefficient * coefficient * tangent_sq

    def over_inner(value):
        return jnp.sum(jnp.where(inner, value, 0.0), axis=0, keepdims=True)

    force_norm = jnp.sqrt(over_inner(neb_sq) + stabilizer)
    speed_norm = jnp.sqrt(over_inner(speed_sq) + stabilizer)
    gain = jnp.broadcast_to(fire_mixing * (speed_norm / force_norm) + time_step, (8, 128))
    keep = jnp.where(inner, 1.0 - fire_mixing, 0.0)
    push = jnp.where(inner, gain, 0.0)
    along_fwd = jnp.where(inner, gain * coefficient * weight_fwd, 0.0)
    along_bwd = jnp.where(inner, gain * coefficient * weight_bwd, 0.0)
    return keep, push, along_fwd, along_bwd


def step_terms(image_ref, gathered_ref, images, terms):
    image = lax.broadcasted_iota(jnp.int32, (8, 128), 0)
    summary = jnp.zeros((8, 128), jnp.float32)
    slabs = gathered_ref.shape[0] // images
    for g in range(images):
        rows = gathered_ref[g * slabs : (g + 1) * slabs, :]
        row = jnp.broadcast_to(jnp.sum(rows, axis=0, keepdims=True), (8, 128))
        summary = summary + jnp.where(image == g, row, 0.0)
        summary = summary + jnp.where(image == (g ^ 1), pltpu.roll(row, 120, 1), 0.0)
    keep, push, along_fwd, along_bwd = path_terms(summary, images)
    here = image_ref[0]
    odd = here % 2 == 1
    values = (keep, push, jnp.where(odd, -along_bwd, along_fwd), jnp.where(odd, -along_fwd, along_bwd))
    for j in range(2):
        at = image == (here + j * (1 - 2 * (here % 2)))
        for k, value in enumerate(values):
            own = jnp.sum(jnp.where(at, value, 0.0), axis=0, keepdims=True)
            terms[j, k] = jnp.broadcast_to(own, (8, 128))


def new_speed(terms, j, speed, force, ahead, behind):
    return terms[j, 0] * speed + terms[j, 1] * force + terms[j, 2] * ahead + terms[j, 3] * behind


def update_kernel(counts, images, image_ref, gathered_ref, slab_speed, *refs):
    path, refs = groups(refs, counts)
    forces, partner_speed, moved, new_speeds = refs[:2], refs[2], refs[3:5], refs[5:7]
    tops, bottoms, speed_sq, (terms, own_speed, sem) = refs[7], refs[8], refs[9:11], refs[11:]
    speeds = (own_speed, partner_speed)
    half = own_speed.shape[1]
    copy = pltpu.make_async_copy(
        slab_speed.at[:, pl.ds(image_ref[0] % 2 * half, half)], own_speed, sem
    )
    copy.start()
    step_terms(image_ref, gathered_ref, images, terms)
    copy.wait()
    sums = (jnp.zeros((8, 128), jnp.float32),) * 2
    for first, rows, held in regions_of(path):

        def one(p, carry):
            carry = list(carry)
            for axis in range(3):
                at = [ref[axis, start + p] for ref, start in held]
                diff = [at[j + 1] - at[j] for j in range(3)]
                for j in range(2):
                    q = first + p
                    speed = new_speed(terms, j, speeds[j][axis, q], forces[j][axis, q], diff[j + 1], diff[j])
                    new_speeds[j][axis, q] = speed
                    moved[j][axis, q] = at[j + 1] + time_step * speed
                    carry[j] = carry[j] + speed * speed
            return tuple(carry)

        sums = over_planes(one, rows, 2, sums)
    speed_sq[0][...], speed_sq[1][...] = sums
    planes = moved[0].shape[1]
    for j in range(2):
        tops[j] = moved[j][:, planes - HALO :]
        bottoms[j] = moved[j][:, :HALO]


def update(image, gathered, path, forces, slab_speed, partner_speed, images):
    counts = [len(pieces) for pieces in path]
    arrays = [piece for pieces in path for piece in pieces] + [*forces, partner_speed]
    out = jax.ShapeDtypeStruct(forces[0].shape, jnp.float32)
    edge = jax.ShapeDtypeStruct((2, 3, HALO, 8, 128), jnp.float32)
    results = pl.pallas_call(
        functools.partial(update_kernel, counts, images),
        out_shape=(out,) * 4 + (edge,) * 2 + (TILE,) * 2,
        in_specs=[SMEM, VMEM, pl.BlockSpec(memory_space=pltpu.HBM)] + [VMEM] * len(arrays),
        out_specs=(VMEM,) * 8,
        scratch_shapes=[
            pltpu.VMEM((2, 4, 8, 128), jnp.float32),
            pltpu.VMEM(forces[0].shape, jnp.float32),
            pltpu.SemaphoreType.DMA,
        ],
        compiler_params=PARAMS,
        name="fire_update",
    )(image, gathered, slab_speed, *arrays)
    return results[:2], results[2:4], results[4], results[5], results[6:]


def last_partner_kernel(images, image_ref, gathered_ref, before, here, after, force, speed, *outs):
    parts, terms_ref = outs[:-1], outs[-1]
    step_terms(image_ref, gathered_ref, images, terms_ref)
    for region, part in enumerate(parts):
        rows = part.shape[1]

        def one(p, carry):
            q = region * rows + p
            for axis in range(3):
                at = here[axis, q]
                part[axis, p] = new_speed(
                    terms_ref, 1, speed[axis, q], force[axis, q], after[axis, q] - at, at - before[axis, q]
                )
            return carry

        over_planes(one, rows, 2)


def last_partner(image, gathered, path, force, speed, images):
    part = jax.ShapeDtypeStruct((3, force.shape[1] // REGIONS, 8, 128), jnp.float32)
    return pl.pallas_call(
        functools.partial(last_partner_kernel, images),
        out_shape=(part,) * REGIONS + (jax.ShapeDtypeStruct((2, 4, 8, 128), jnp.float32),),
        in_specs=[SMEM] + [VMEM] * 6,
        out_specs=(VMEM,) * (REGIONS + 1),
        compiler_params=PARAMS,
        name="last_partner",
    )(image, gathered, *path, force, speed)


def last_own_kernel(side_ref, terms, before, here, after, force, speed, moved, new_ref):
    def one(p, carry):
        for axis in range(3):
            at = here[axis, p]
            new = new_speed(
                terms, 0, speed[axis, p], force[axis, p], after[axis, p] - at, at - before[axis, p]
            )
            new_ref[axis, p] = new
            moved[axis, p] = at + time_step * new
        return carry

    over_planes(one, here.shape[1], 2)


def last_own(side, terms, path, force, speed):
    planes = force.shape[1]
    chunk = planes // REGIONS
    block = pl.BlockSpec((3, chunk, 8, 128), lambda t, side_ref: (0, t, 0, 0))
    half = pl.BlockSpec((3, chunk, 8, 128), lambda t, side_ref: (0, side_ref[0] * REGIONS + t, 0, 0))
    out = jax.ShapeDtypeStruct((3, 2 * planes, 8, 128), jnp.float32)
    return pl.pallas_call(
        last_own_kernel,
        grid_spec=pltpu.PrefetchScalarGridSpec(
            num_scalar_prefetch=1,
            grid=(REGIONS,),
            in_specs=[pl.BlockSpec((2, 4, 8, 128), lambda t, side_ref: (0, 0, 0, 0))] + [block] * 5,
            out_specs=(half, half),
        ),
        out_shape=(out, out),
        compiler_params=PARAMS,
        name="last_own",
    )(side, terms, *path, force, speed)


def last_join_kernel(side_ref, here, speed, moved_in, speed_in, moved, new_ref):
    def one(p, carry):
        for axis in range(3):
            new = speed[axis, p]
            new_ref[axis, p] = new
            moved[axis, p] = here[axis, p] + time_step * new
        return carry

    over_planes(one, speed.shape[1], 4)


def last_join(side, region, here, speed, moved, speeds):
    rows = speed.shape[1]
    chunk = rows // JOIN_STEPS
    first = region * JOIN_STEPS
    block = pl.BlockSpec((3, chunk, 8, 128), lambda t, side_ref: (0, t, 0, 0))
    here_block = pl.BlockSpec((3, chunk, 8, 128), lambda t, side_ref: (0, first + t, 0, 0))
    half = pl.BlockSpec(
        (3, chunk, 8, 128),
        lambda t, side_ref: (0, (1 - side_ref[0]) * REGIONS * JOIN_STEPS + first + t, 0, 0),
    )
    out = jax.ShapeDtypeStruct(moved.shape, jnp.float32)
    whole = pl.BlockSpec(memory_space=pl.ANY)
    return pl.pallas_call(
        last_join_kernel,
        grid_spec=pltpu.PrefetchScalarGridSpec(
            num_scalar_prefetch=1,
            grid=(JOIN_STEPS,),
            in_specs=[here_block, block, whole, whole],
            out_specs=(half, half),
        ),
        out_shape=(out, out),
        input_output_aliases={3: 0, 4: 1},
        compiler_params=PARAMS,
        name="last_join",
    )(side, here, speed, moved, speeds)


def cut_kernel(blocks, squares, side_ref, *refs):
    count = len(blocks)
    source, outs, sems = refs[0], refs[1 : 1 + count], refs[-1]
    copies = []
    for k, out in enumerate(outs):
        at = 0
        for start, size in blocks[k]:
            rows = source.at[:, pl.ds(at_side(start, side_ref), size)]
            copies.append(
                pltpu.make_async_copy(rows, out.at[:, pl.ds(at, size)], sems.at[len(copies)])
            )
            at += size
    for copy in copies:
        copy.start()
    for copy in copies:
        copy.wait()
    if squares:

        def one(p, total):
            return total + sum(source[axis, p] * source[axis, p] for axis in range(3))

        refs[1 + count][...] = over_planes(one, source.shape[1], 4, jnp.zeros((8, 128), jnp.float32))


def at_side(pair, side_ref):
    even, odd = pair
    return even if even == odd else even + (odd - even) * side_ref[0]


def cut(side, array, blocks, squares=False):
    count = len(blocks)
    sizes = [sum(size for _, size in block) for block in blocks]
    return pl.pallas_call(
        functools.partial(cut_kernel, blocks, squares),
        out_shape=tuple(jax.ShapeDtypeStruct((3, size, 8, 128), jnp.float32) for size in sizes)
        + (TILE,) * squares,
        in_specs=[SMEM, VMEM if squares else pl.BlockSpec(memory_space=pltpu.HBM)],
        out_specs=(VMEM,) * (count + squares),
        scratch_shapes=[pltpu.SemaphoreType.DMA((sum(len(block) for block in blocks),))],
        compiler_params=PARAMS,
        name="cut",
    )(side, array)


def local(displacement, velocity):
    planes = displacement.shape[2] // (SIDE * SIDE)
    half = planes // 2
    images, slabs = lax.axis_size("image"), lax.axis_size("domain")
    both = ("image", "domain")
    own_image = lax.axis_index("image").astype(jnp.int32)
    side = own_image % 2
    image_arg, side_arg = own_image.reshape(1), side.reshape(1)
    slab = displacement.reshape(3, planes, 8, 128)
    slab_speed = velocity.reshape(3, planes, 8, 128)

    def at(image, domain):
        return image * slabs + domain % slabs

    everyone = [(i, d) for i in range(images) for d in range(slabs)]
    outer_own = [(at(i, d), at(i, d + 1 - 2 * (i % 2))) for i, d in everyone]
    outer_partner = [(at(i, d), at(i ^ 1, d - 1 + 2 * (i % 2))) for i, d in everyone]
    across = [(i, i ^ 1) for i in range(images)]
    own_out = [(i, i - 2 + 4 * (i % 2)) for i in range(images)]
    own_out = [(a, b) for a, b in own_out if 0 <= b < images]
    partner_out = [(b, a) for a, b in own_out]
    upward = [(at(i, d), at(i ^ 1, d + i % 2)) for i, d in everyone]
    downward = [(b, a) for a, b in upward]

    end, top = planes - HALO, half + HALO
    piece = PIECES[0]
    outer, inner = (0, top), (top, 0)
    edge_own, edge_partner, near_inner, own, lead, rest = cut(
        side_arg,
        slab,
        (
            (((end, 0), HALO),),
            (((0, end), HALO),),
            (((half, half - HALO), HALO),),
            (((0, half), half),),
            (((half, 0), piece), ((half - HALO, half), HALO)),
            (((half + piece, piece), PIECES[1]),),
        ),
    )
    halo_own = lax.ppermute(edge_own, both, outer_own)
    halo_partner = lax.ppermute(edge_partner, both, outer_partner)
    rest, halo_own, halo_partner = lax.optimization_barrier(
        (rest, halo_own, halo_partner)
    )
    partner = [lax.ppermute(part, "image", across) for part in (lead, rest)]
    beyond_own = lax.ppermute(own, "image", own_out)
    beyond_partner = [lax.ppermute(part, "image", partner_out) for part in partner]
    own_source = (
        (own, None, 0, half, (HALO, HALO)),
        (halo_own, None, 0, HALO, outer),
        (near_inner, None, 0, HALO, inner),
    )
    partner_source = (
        (partner[0], None, 0, piece, (HALO, HALO)),
        (partner[0], None, piece, HALO, inner),
        (partner[1], None, 0, PIECES[1], (HALO + piece,) * 2),
        (halo_partner, None, 0, HALO, outer),
    )
    forces, energies = image_forces(side_arg, half, (own_source, partner_source))
    far_speed, slab_sq = cut(side_arg, slab_speed, ((((half, 0), half),),), True)
    far_speed, *_ = lax.optimization_barrier((far_speed, partner[0], halo_own, halo_partner))
    partner_speed = lax.ppermute(far_speed, "image", across)

    path = (beyond_partner, [own], partner, [beyond_own])
    speeds = (slab_speed, partner_speed)
    speed_sq = (slab_sq, jnp.zeros_like(slab_sq))
    for step_index in range(FIRE_STEPS):
        if step_index > 0:
            forces, energies = image_forces(side_arg, half, sources)
        payload = moments(side_arg, path, forces, energies, speed_sq, images * slabs)
        gathered = lax.all_to_all(payload, both, 0, 0, tiled=True)
        if step_index == FIRE_STEPS - 1:
            break
        moved, speeds, tops, bottoms, speed_sq = update(
            image_arg, gathered, path, forces, *speeds, images
        )
        low = lax.ppermute(tops, both, upward)
        high = lax.ppermute(bottoms, both, downward)
        sources = [
            (
                (moved[j], None, 0, half, (HALO, HALO)),
                (low, 1 - j, 0, HALO, (0, 0)),
                (high, 1 - j, 0, HALO, (top, top)),
            )
            for j in range(2)
        ]
        path = (
            [lax.ppermute(moved[1], "image", partner_out)],
            [moved[0]],
            [moved[1]],
            [lax.ppermute(moved[0], "image", own_out)],
        )
        back_home, _, _ = lax.optimization_barrier((moved[1], low, high))
        returned = lax.ppermute(back_home, "image", across)
    whole = [pieces[0] for pieces in path]
    *last_speeds, terms = last_partner(
        image_arg, gathered, whole[1:], forces[1], speeds[1], images
    )
    last_speeds = [lax.ppermute(part, "image", across) for part in last_speeds]
    moved, new_speeds = last_own(side_arg, terms, whole[:3], forces[0], speeds[0])
    for region, part in enumerate(last_speeds):
        moved, new_speeds = last_join(side_arg, region, returned, part, moved, new_speeds)
    return (moved.reshape(displacement.shape), new_speeds.reshape(velocity.shape))


def solution(mesh):
    spec = P("image", None, "domain")
    return jax.shard_map(
        local,
        mesh=mesh,
        in_specs=(spec, spec),
        out_specs=(spec, spec),
        check_vma=False,
    )
```
